32 devices in a mesh: dp: 16 (over z, y, core), tensor: 2 (over x).
Axes of the slice: x: 2, y: 2, z: 4, core: 2. Of those that a mesh axis runs over, the one named last changes fastest.
Arguments:
- tokens: bfloat16 [18432, 1536], P(('dp', 'tensor')), may hold values from -6 to 6
- timestep: bfloat16 [48, 1024], P('dp'), may hold values from -6 to 6
- caption: bfloat16 [48, 256, 2048], P('dp'), may hold values from -6 to 6
- caption_mask: int32 [48, 256], P('dp'), may hold values from 0 to 1, as said below
- image_lengths: int32 [48], P('dp'), may hold values from 72 to 768, as said below
- patch_pos: int32 [2, 18432], P(None, 'dp'), may hold values from 0 to 31, as said below
- ada_weight: bfloat16 [1024, 6144], P(None, 'tensor'), may hold values from -0.1875 to 0.1875
- ada_bias: float32 [6144], P('tensor'), may hold values from -3 to 3
- attention_norm: float32 [1536], replicated, may hold values from 0.25 to 1.75
- attention_post: float32 [1536], replicated, may hold values from 0.25 to 1.75
- feedforward_norm: float32 [1536], replicated, may hold values from 0.25 to 1.75
- feedforward_post: float32 [1536], replicated, may hold values from 0.25 to 1.75
- query_weight: bfloat16 [1536, 1536], P(None, 'tensor'), may hold values from -0.15625 to 0.15625
- key_weight: bfloat16 [1536, 1536], P(None, 'tensor'), may hold values from -0.15625 to 0.15625
- value_weight: bfloat16 [1536, 1536], P(None, 'tensor'), may hold values from -0.15625 to 0.15625
- query_gain: float32 [24, 64], P('tensor'), may hold values from 0.8 to 2
- key_gain: float32 [24, 64], P('tensor'), may hold values from 0.8 to 2
- cross_keys: bfloat16 [2048, 1536], P(None, 'tensor'), may hold values from -0.125 to 0.125
- cross_values: bfloat16 [2048, 1536], P(None, 'tensor'), may hold values from -0.125 to 0.125
- cross_gain: float32 [24, 64], P('tensor'), may hold values from 0.8 to 2
- cross_gate: float32 [24], P('tensor'), may hold values from -1.5 to 1.5
- output_weight: bfloat16 [1536, 1536], P('tensor'), may hold values from -0.15625 to 0.15625
- gate_weight: bfloat16 [1536, 4096], P(None, 'tensor'), may hold values from -0.15625 to 0.15625
- up_weight: bfloat16 [1536, 4096], P(None, 'tensor'), may hold values from -0.15625 to 0.15625
- down_weight: bfloat16 [4096, 1536], P('tensor'), may hold values from -0.09375 to 0.09375
- cotangent: bfloat16 [18432, 1536], P(('dp', 'tensor')), may hold values from -6 to 6
Outputs:
- out: bfloat16 [18432, 1536], P(('dp', 'tensor'))
- tokens_grad: float32 [18432, 1536], P(('dp', 'tensor'))
- ada_weight_grad: float32 [1024, 6144], P('dp', 'tensor')
- ada_bias_grad: float32 [6144], P('tensor')
- attention_norm_grad: float32 [1536], replicated
- attention_post_grad: float32 [1536], replicated
- feedforward_norm_grad: float32 [1536], replicated
- feedforward_post_grad: float32 [1536], replicated
- query_weight_grad: float32 [1536, 1536], P('dp', 'tensor')
- key_weight_grad: float32 [1536, 1536], P('dp', 'tensor')
- value_weight_grad: float32 [1536, 1536], P('dp', 'tensor')
- query_gain_grad: float32 [24, 64], P('tensor')
- key_gain_grad: float32 [24, 64], P('tensor')
- cross_keys_grad: float32 [2048, 1536], P('dp', 'tensor')
- cross_values_grad: float32 [2048, 1536], P('dp', 'tensor')
- cross_gain_grad: float32 [24, 64], P('tensor')
- cross_gate_grad: float32 [24], P('tensor')
- output_weight_grad: float32 [1536, 1536], P('tensor', 'dp')
- gate_weight_grad: float32 [1536, 4096], P('dp', 'tensor')
- up_weight_grad: float32 [1536, 4096], P('dp', 'tensor')
- down_weight_grad: float32 [4096, 1536], P('tensor', 'dp')
The draws below stay inside these ranges and needn't reach their ends.
Inputs may be any that keep to these rules, and one draw needn't show every extreme that they name: `image_lengths`: the 3 lengths of each index of dp sum to 1152. `caption_mask`: each row is 1 on a leading run of 8 to 256 positions and 0 after it; in each index of dp one image uses all 256. `patch_pos`: patch rows and columns of the tokens of an image, its rows of 16 to 32 patches read one after another; the longest image of each index of dp has rows of 32.
All inputs are finite; a program needn't handle non-finite values.
Results may differ from the reference program's by a relative error of at most 0.022.
Values may be sent and summed in bfloat16 or wider, within the bound.
No kernel may reach another device: no remote copies, remote signals or barrier semaphores. Data moves between devices by JAX's collectives and lax.ppermute only.
A program may use at most 576 MiB of HBM per device.

```python
import math
import jax
import jax.numpy as jnp
from jax import lax

D = 1536
HEADS = 24
HD = 64
FF = 4096
CAPD = 2048
ADA = 1024
CAP = 256
IMGS = 3
TOK_DEV = 1152
IMG_MAX = 768
TOKENS = 18432
IMAGES = 48
N_DP = 16


def group_layout(key):
    base = jax.random.fold_in(key, 11)
    first_key, second_key = jax.random.split(base)
    width_key = jax.random.fold_in(key, 23)
    group_count = IMAGES // IMGS
    least = TOK_DEV // 16
    longest = IMG_MAX
    remain = TOK_DEV - longest
    other = jax.random.randint(first_key, (group_count,), least, remain - least + 1).astype(jnp.int32)
    table = jnp.stack([jnp.full((group_count,), longest, jnp.int32), other, (remain - other).astype(jnp.int32)], axis=1)
    other_widths = jax.random.randint(width_key, (group_count, 2), 16, 33).astype(jnp.int32)
    width_table = jnp.concatenate([jnp.full((group_count, 1), 32, jnp.int32), other_widths], axis=1)
    ranks = jax.random.randint(second_key, (group_count, 3), 0, 1 << 20) * 4 + jnp.arange(3, dtype=jnp.int32)[None, :]
    order_idx = jnp.argsort(ranks, axis=1)
    lengths = jnp.take_along_axis(table, order_idx, axis=1).astype(jnp.int32)
    widths = jnp.take_along_axis(width_table, order_idx, axis=1).astype(jnp.int32)
    return (lengths, widths)


def draw_image_lengths(key, part):
    lengths, widths = group_layout(key)
    return lengths.reshape(-1)


def draw_patch_pos(key, part):
    lengths, row_widths = group_layout(key)
    image_ends = jnp.cumsum(lengths, axis=1)
    image_starts = image_ends - lengths
    places = jnp.arange(TOK_DEV, dtype=jnp.int32)
    member = (places[None, :, None] >= image_starts[:, None, :]) & (places[None, :, None] < image_ends[:, None, :])
    local_place = jnp.sum(jnp.where(member, places[None, :, None] - image_starts[:, None, :], 0), axis=2)
    token_width = jnp.sum(jnp.where(member, row_widths[:, None, :], 0), axis=2)
    patch_rows = local_place // token_width
    patch_cols = local_place % token_width
    return jnp.stack([patch_rows.reshape(-1), patch_cols.reshape(-1)]).astype(jnp.int32)


def draw_caption_mask(key, part):
    base = jax.random.fold_in(key, 31)
    first_key, second_key = jax.random.split(base)
    group_count = IMAGES // IMGS
    lengths = jax.random.randint(first_key, (IMAGES,), min(8, CAP), CAP + 1).astype(jnp.int32)
    full_one = jax.random.randint(second_key, (group_count,), 0, IMGS).astype(jnp.int32)
    picked = jnp.arange(IMAGES, dtype=jnp.int32) % IMGS == jnp.repeat(full_one, IMGS)
    lengths = jnp.where(picked, CAP, lengths)
    return (jnp.arange(CAP, dtype=jnp.int32)[None, :] < lengths[:, None]).astype(jnp.int32)


def with_spikes(values, own_key, source, target, parts, factor):
    def block_of(dim):
        return (jnp.arange(values.shape[dim]) // (values.shape[dim] // parts)).reshape((-1,) + (1,) * (values.ndim - 1 - dim))

    near = jax.random.permutation(own_key, parts)[block_of(target)]
    second = (block_of(target) + parts // 2) % parts
    return jnp.where((block_of(source) == near) | (block_of(source) == second), factor * values, values)


def levels(rng, extent, pieces, smallest, largest):
    loudness, own = 1.0, jax.random.fold_in(rng, 6)
    for position, shards_of in pieces:
        draws = jnp.exp(jax.random.uniform(jax.random.fold_in(own, position), (shards_of,), jnp.float32, smallest / len(pieces), largest / len(pieces)))
        loudness = loudness * jnp.repeat(draws, extent[position] // shards_of).reshape([-1 if axis == position else 1 for axis in range(len(extent))])
    return loudness


def gaussian(own_key, dims, width, bound, pieces=(), held_as=jnp.bfloat16):
    values = jax.random.normal(own_key, dims, jnp.float32) * width
    if len(pieces) > 0:
        values = levels(own_key, dims, pieces, -0.22, 0.18) * values
    return jnp.clip(values, min=-bound, max=bound).astype(held_as)


def heavy_noise(rng, dims, width, reach, shards, heavy, held_as=jnp.bfloat16):
    drawn = width * jax.random.normal(rng, dims, jnp.float32)
    if shards:
        drawn = drawn * levels(rng, dims, shards, -0.22, 0.18)
    return jnp.clip(with_spikes(drawn, jax.random.fold_in(rng, 3), *heavy), -reach, reach).astype(held_as)


def setup_inputs(seed: int = 0) -> dict:
    key_of = jax.random.split(jax.random.key(seed), 27)
    return {
        "tokens": gaussian(key_of[0], (TOKENS, D), 1.0, 6.0, ((0, 32),)),
        "timestep": gaussian(key_of[1], (IMAGES, ADA), 1.0, 6.0, ((0, 16),)),
        "caption": gaussian(key_of[2], (IMAGES, CAP, CAPD), 1.0, 6.0, ((0, 16),)),
        "caption_mask": draw_caption_mask(jax.random.fold_in(key_of[26], 71), 0),
        "image_lengths": draw_image_lengths(jax.random.fold_in(key_of[26], 71), 0),
        "patch_pos": draw_patch_pos(jax.random.fold_in(key_of[26], 71), 0),
        "ada_weight": gaussian(key_of[6], (ADA, 4 * D), ADA ** -0.5, 0.1875, ((1, 2),)),
        "ada_bias": gaussian(key_of[7], (4 * D,), 0.5, 3.0, ((0, 2),), jnp.float32),
        "attention_norm": jnp.clip(1.0 + 0.15 * jax.random.normal(key_of[8], (D,), jnp.float32), 0.25, 1.75),
        "attention_post": jnp.clip(1.0 + 0.15 * jax.random.normal(key_of[9], (D,), jnp.float32), 0.25, 1.75),
        "feedforward_norm": jnp.clip(1.0 + 0.15 * jax.random.normal(key_of[10], (D,), jnp.float32), 0.25, 1.75),
        "feedforward_post": jnp.clip(1.0 + 0.15 * jax.random.normal(key_of[11], (D,), jnp.float32), 0.25, 1.75),
        "query_weight": gaussian(key_of[12], (D, HEADS * HD), D ** -0.5, 0.15625, ((1, 2),)),
        "key_weight": gaussian(key_of[13], (D, HEADS * HD), D ** -0.5, 0.15625, ((1, 2),)),
        "value_weight": gaussian(key_of[14], (D, HEADS * HD), D ** -0.5, 0.15625, ((1, 2),)),
        "query_gain": jnp.clip(0.8 + 1.2 * jax.random.uniform(key_of[15], (HEADS, HD), jnp.float32) ** levels(key_of[15], (HEADS, HD), ((0, 2),), -0.2, 0.2), 0.8, 2.0),
        "key_gain": jnp.clip(0.8 + 1.2 * jax.random.uniform(key_of[16], (HEADS, HD), jnp.float32) ** levels(key_of[16], (HEADS, HD), ((0, 2),), -0.2, 0.2), 0.8, 2.0),
        "cross_keys": gaussian(key_of[17], (CAPD, HEADS * HD), CAPD ** -0.5, 0.125, ((1, 2),)),
        "cross_values": gaussian(key_of[18], (CAPD, HEADS * HD), CAPD ** -0.5, 0.125, ((1, 2),)),
        "cross_gain": jnp.clip(0.8 + 1.2 * jax.random.uniform(key_of[19], (HEADS, HD), jnp.float32) ** levels(key_of[19], (HEADS, HD), ((0, 2),), -0.2, 0.2), 0.8, 2.0),
        "cross_gate": jnp.clip(jax.random.uniform(key_of[20], (HEADS,), jnp.float32, -1.5, 1.5) * levels(key_of[20], (HEADS,), ((0, 2),), -0.4, 0.0), -1.5, 1.5),
        "output_weight": gaussian(key_of[21], (HEADS * HD, D), (HEADS * HD) ** -0.5, 0.15625, ((0, 2),)),
        "gate_weight": gaussian(key_of[22], (D, FF), D ** -0.5, 0.15625, ((1, 2),)),
        "up_weight": gaussian(key_of[23], (D, FF), D ** -0.5, 0.15625, ((1, 2),)),
        "down_weight": gaussian(key_of[24], (FF, D), FF ** -0.5, 0.09375, ((0, 2),)),
        "cotangent": heavy_noise(key_of[25], (TOKENS, D), 1.0, 6.0, ((0, 32),), (0, 1, 32, 2.75)),
    }


@jax.custom_vjp
def low(v):
    return lax.optimization_barrier(v.astype(jnp.bfloat16)).astype(jnp.float32)

@jax.custom_vjp
def low_back(v):
    return v

def low_keep(v):
    return (low(v), None)

def low_pass(kept, grad):
    return (grad,)

def back_keep(v):
    return (v, None)

def back_low(kept, grad):
    return (low(grad),)
low.defvjp(low_keep, low_pass)
low_back.defvjp(back_keep, back_low)
epsilon = 1e-05
negative = -1e+30
theta = 10000.0
highest = lax.Precision.HIGHEST

def silu_of(values):
    return values / (1.0 + jnp.exp(-values))

def unit(values):
    return values * lax.rsqrt(lax.optimization_barrier(jnp.mean(values * values, axis=-1, keepdims=True)) + epsilon)

def softmax_rows(scores):
    top = lax.optimization_barrier(jnp.max(scores, axis=-1, keepdims=True))
    expo = jnp.exp(scores - top)
    return expo / lax.optimization_barrier(jnp.sum(expo, axis=-1, keepdims=True))

def rope_tables(positions):
    quarter = HD // 4
    freqs = jnp.power(theta, -(jnp.arange(quarter, dtype=jnp.float32) / quarter))
    angles = jnp.concatenate([positions[0].astype(jnp.float32)[:, None] * freqs[None, :], positions[1].astype(jnp.float32)[:, None] * freqs[None, :]], axis=1)
    return (jnp.cos(angles), jnp.sin(angles))

def rotate(values, cosine, sine):
    half = values.shape[-1] // 2
    first = values[..., :half]
    second = values[..., half:]
    cosine = cosine[:, None, :]
    sine = sine[:, None, :]
    return jnp.concatenate([first * cosine - second * sine, first * sine + second * cosine], axis=-1)

def group_layer(x_group, time_group, cap_group, mask_group, len_group, pos_group, params):
    ada_weight, ada_bias, attention_norm, attention_post, feedforward_norm, feedforward_post, query_weight, key_weight, value_weight, query_gain, key_gain, cross_keys, cross_values, cross_gain, cross_gate, output_weight, gate_weight, up_weight, down_weight = params
    image_ends = jnp.cumsum(len_group)
    places = jnp.arange(TOK_DEV, dtype=jnp.int32)
    image_of = lax.optimization_barrier(jnp.sum((places[:, None] >= image_ends[None, :]).astype(jnp.int32), axis=1))
    silu_time = low(silu_of(time_group))
    modulation = jnp.dot(silu_time, ada_weight, precision=highest) + ada_bias
    token_mod = jnp.take(modulation, image_of, axis=0)
    scale_attn = token_mod[:, :D]
    gate_attn = jnp.tanh(token_mod[:, D:2 * D])
    scale_ffn = token_mod[:, 2 * D:3 * D]
    gate_ffn = jnp.tanh(token_mod[:, 3 * D:])
    normed_in = low(unit(x_group) * attention_norm * (1.0 + scale_attn))
    q_raw = low_back(jnp.dot(normed_in, query_weight, precision=highest)).reshape(TOK_DEV, HEADS, HD)
    k_raw = low_back(jnp.dot(normed_in, key_weight, precision=highest)).reshape(TOK_DEV, HEADS, HD)
    values = low(low_back(jnp.dot(normed_in, value_weight, precision=highest))).reshape(TOK_DEV, HEADS, HD)
    cosine, sine = rope_tables(pos_group)
    queries = low(rotate(unit(q_raw) * query_gain, cosine, sine))
    keys = low(rotate(unit(k_raw) * key_gain, cosine, sine))
    cap_flat = cap_group.reshape(IMGS * CAP, CAPD)
    ck_raw = low_back(jnp.dot(cap_flat, cross_keys, precision=highest)).reshape(IMGS * CAP, HEADS, HD)
    cap_keys = low(unit(ck_raw) * cross_gain)
    cap_values = low(low_back(jnp.dot(cap_flat, cross_values, precision=highest))).reshape(IMGS * CAP, HEADS, HD)
    score_scale = 1.0 / math.sqrt(HD)
    same_image = image_of[:, None] == image_of[None, :]
    self_scores = low_back(jnp.einsum('qhd,khd->hqk', queries, keys, precision=highest) * score_scale)
    self_probs = softmax_rows(jnp.where(same_image[None], self_scores, negative))
    self_out = jnp.einsum('hqk,khd->qhd', low(self_probs), values, precision=highest)
    key_image = jnp.arange(IMGS * CAP, dtype=jnp.int32) // CAP
    key_valid = mask_group.reshape(-1) > 0
    allowed = (image_of[:, None] == key_image[None, :]) & key_valid[None, :]
    cross_scores = low_back(jnp.einsum('qhd,khd->hqk', queries, cap_keys, precision=highest) * score_scale)
    cross_probs = softmax_rows(jnp.where(allowed[None], cross_scores, negative))
    cross_out = jnp.einsum('hqk,khd->qhd', low(cross_probs), cap_values, precision=highest)
    mixed = low_back(low(self_out + jnp.tanh(cross_gate)[None, :, None] * cross_out)).reshape(TOK_DEV, HEADS * HD)
    attn = low_back(jnp.dot(mixed, output_weight, precision=highest))
    hidden = x_group + gate_attn * unit(attn) * attention_post
    normed_ffn = low(unit(hidden) * feedforward_norm * (1.0 + scale_ffn))
    gate_pre = low_back(jnp.dot(normed_ffn, gate_weight, precision=highest))
    up_pre = low_back(jnp.dot(normed_ffn, up_weight, precision=highest))
    inner = low(silu_of(gate_pre) * up_pre)
    ffn = low_back(jnp.dot(inner, down_weight, precision=highest))
    return hidden + gate_ffn * unit(ffn) * feedforward_post

def reference(tokens, timestep, caption, caption_mask, image_lengths, patch_pos, ada_weight, ada_bias, attention_norm, attention_post, feedforward_norm, feedforward_post, query_weight, key_weight, value_weight, query_gain, key_gain, cross_keys, cross_values, cross_gain, cross_gate, output_weight, gate_weight, up_weight, down_weight, cotangent):
    weights = tuple((item.astype(jnp.float32) for item in (ada_weight, ada_bias, attention_norm, attention_post, feedforward_norm, feedforward_post, query_weight, key_weight, value_weight, query_gain, key_gain, cross_keys, cross_values, cross_gain, cross_gate, output_weight, gate_weight, up_weight, down_weight)))
    x_groups = tokens.astype(jnp.float32).reshape(N_DP, TOK_DEV, D)
    time_groups = timestep.astype(jnp.float32).reshape(N_DP, IMGS, ADA)
    cap_groups = caption.astype(jnp.float32).reshape(N_DP, IMGS, CAP, CAPD)
    mask_groups = caption_mask.reshape(N_DP, IMGS, CAP)
    len_groups = image_lengths.reshape(N_DP, IMGS)
    pos_groups = patch_pos.reshape(2, N_DP, TOK_DEV).transpose(1, 0, 2)

    def forward(inputs, params):

        def one_group(items):
            x_group, time_group, cap_group, mask_group, len_group, pos_group = items
            return group_layer(x_group, time_group, cap_group, mask_group, len_group, pos_group, params)
        return lax.map(jax.checkpoint(one_group), (inputs, time_groups, cap_groups, mask_groups, len_groups, pos_groups))
    result, pullback = jax.vjp(forward, x_groups, weights)
    grad_inputs, grad_w = pullback(cotangent.astype(jnp.float32).reshape(N_DP, TOK_DEV, D))
    return (result.reshape(TOKENS, D).astype(jnp.bfloat16), grad_inputs.reshape(TOKENS, D), grad_w[0], grad_w[1], grad_w[2], grad_w[3], grad_w[4], grad_w[5], grad_w[6], grad_w[7], grad_w[8], grad_w[9], grad_w[10], grad_w[11], grad_w[12], grad_w[13], grad_w[14], grad_w[15], grad_w[16], grad_w[17], grad_w[18])
```

```python
import math

import jax
import jax.numpy as jnp
from jax import lax
from jax.experimental import pallas as pl
from jax.experimental.pallas import tpu as pltpu
from jax.sharding import PartitionSpec as P

epsilon = 1e-05
penalty = 1024.0
theta = 10000.0
lanes = 128
half_lanes = 64
query_block = 256
bf16 = jnp.bfloat16
f32 = jnp.float32
vmem_bytes = 60 * 1024 * 1024


def sigmoid_of(values):
    return 1.0 / (1.0 + jnp.exp(-values))


def unit_rows(values):
    factor = lax.rsqrt(jnp.mean(values * values, axis=-1, keepdims=True) + epsilon)
    return (values * factor, factor)


def unit_back(gradient, normed, factor):
    return factor * (gradient - normed * jnp.mean(gradient * normed, axis=-1, keepdims=True))


def dot_nn(left, right):
    return lax.dot_general(left, right, (((1,), (0,)), ((), ())), preferred_element_type=f32)


def dot_nt(left, right):
    return lax.dot_general(left, right, (((1,), (1,)), ((), ())), preferred_element_type=f32)


def dot_tn(left, right):
    return lax.dot_general(left, right, (((0,), (0,)), ((), ())), preferred_element_type=f32)


def lane_index(rows):
    return lax.broadcasted_iota(jnp.int32, (rows, lanes), 1)


def halves_matrix(crossed):
    row = lax.broadcasted_iota(jnp.int32, (lanes, lanes), 0) // half_lanes
    col = lax.broadcasted_iota(jnp.int32, (lanes, lanes), 1) // half_lanes
    same = (row != col) if crossed else (row == col)
    return jnp.where(same, 1.0, 0.0).astype(bf16)


def half_sums(values, matrix):
    high = values.astype(bf16)
    rest = (values - high.astype(f32)).astype(bf16)
    return dot_nn(high, matrix) + dot_nn(rest, matrix)


def head_unit(values, matrix):
    factor = lax.rsqrt(half_sums(values * values, matrix) * (1.0 / half_lanes) + epsilon)
    return values * factor, factor


def head_unit_back(gradient, normed, factor, matrix):
    mean = half_sums(gradient * normed, matrix) * (1.0 / half_lanes)
    return factor * (gradient - normed * mean)


def swap_quarters(values):
    lane = lane_index(values.shape[0])
    ahead = pltpu.roll(values, lanes - 32, 1)
    behind = pltpu.roll(values, 32, 1)
    return jnp.where(lane % half_lanes < 32, ahead, behind)


def three_parts(values):
    first = values.astype(bf16)
    rest = values - first.astype(f32)
    second = rest.astype(bf16)
    third = (rest - second.astype(f32)).astype(bf16)
    return first, second, third


def put_lanes(target, place, head, values):
    lane = lane_index(target.shape[0])
    base = half_lanes * (1 - head) + place
    for offset, part in enumerate(three_parts(values)):
        target = jnp.where(lane == base + offset, part, target)
    return target


def both(head_zero, head_one):
    return jnp.where(lane_index(head_zero.shape[0]) < half_lanes, head_zero, head_one)


def pair_operands(values, features):
    return both(values, features), both(features, values)


def blocks_of(rows):
    starts = list(range(0, rows, query_block))
    return [(start, min(query_block, rows - start)) for start in starts]


def forward_kernel(block_count, image_count, present, *refs):
    q_refs = refs[:block_count]
    k_refs = refs[block_count : 2 * block_count]
    v_refs = refs[2 * block_count : 3 * block_count]
    (
        ck_ref,
        cv_ref,
        gain_ref,
        cos_ref,
        sin_ref,
        fq_ref,
        fk_ref,
        fc_ref,
        mixed_ref,
        so_ref,
        co_ref,
        qa_ref,
        ka_ref,
        ca_ref,
        va_ref,
        cva_ref,
        acc_ref,
    ) = refs[3 * block_count :]
    rows = cos_ref.shape[0]
    cap_rows = ck_ref.shape[0] // image_count
    same = halves_matrix(False)
    q_raw = jnp.concatenate([ref[...] for ref in q_refs], axis=0).astype(f32)
    k_raw = jnp.concatenate([ref[...] for ref in k_refs], axis=0).astype(f32)
    cosine = cos_ref[...]
    sine = sin_ref[...]
    q_gained = head_unit(q_raw, same)[0] * gain_ref[0, 0:1, :]
    q_turned = q_gained * cosine + swap_quarters(q_gained) * sine
    queries = (q_turned.astype(bf16).astype(f32) * (1.0 / math.sqrt(half_lanes))).astype(bf16)
    k_gained = head_unit(k_raw, same)[0] * gain_ref[0, 1:2, :]
    keys = (k_gained * cosine + swap_quarters(k_gained) * sine).astype(bf16)
    cap_keys = (head_unit(ck_ref[...].astype(f32), same)[0] * gain_ref[0, 2:3, :]).astype(bf16)
    values = jnp.concatenate([ref[...] for ref in v_refs], axis=0)
    cap_values = cv_ref[...]
    ones = jnp.ones_like(values)
    cap_ones = jnp.ones_like(cap_values)
    for head, (qa, ka, ca, va, cva) in enumerate(
        zip(
            pair_operands(queries, fq_ref[...]),
            pair_operands(keys, fk_ref[...]),
            pair_operands(cap_keys, fc_ref[...]),
            pair_operands(values, ones),
            pair_operands(cap_values, cap_ones),
        )
    ):
        span = slice(head * lanes, (head + 1) * lanes)
        qa_ref[:, span] = qa
        ka_ref[:, span] = ka
        ca_ref[:, span] = ca
        va_ref[:, span] = va
        cva_ref[:, span] = cva
    gate = gain_ref[0, 3:4, :]
    for index, (start, size) in enumerate(blocks_of(rows)):
        own = slice(start, start + size)
        self_parts = []
        for head in range(2):
            span = slice(head * lanes, (head + 1) * lanes)
            scores = dot_nt(qa_ref[own, span], ka_ref[:, span])
            self_parts.append(dot_nn(jnp.exp(scores).astype(bf16), va_ref[:, span]))
        acc_ref[0:size, :] = jnp.zeros((size, 2 * lanes), f32)
        for image in range(image_count):

            @pl.when(present[index * image_count + image] > 0)
            def _():
                caps = slice(image * cap_rows, (image + 1) * cap_rows)
                for head in range(2):
                    span = slice(head * lanes, (head + 1) * lanes)
                    scores = dot_nt(qa_ref[own, span], ca_ref[caps, span])
                    acc_ref[0:size, span] += dot_nn(
                        jnp.exp(scores).astype(bf16), cva_ref[caps, span]
                    )

        cross_parts = [acc_ref[0:size, 0:lanes], acc_ref[0:size, lanes:]]
        outs = []
        for parts in (self_parts, cross_parts):
            total = pltpu.roll(both(parts[1], parts[0]), half_lanes, 1)
            outs.append(both(parts[0], parts[1]) / total)
        so_ref[own, :] = outs[0].astype(bf16)
        co_ref[own, :] = outs[1].astype(bf16)
        mixed_ref[own, :] = (outs[0] + gate * outs[1]).astype(bf16)
        for head in range(2):
            span = slice(head * lanes, (head + 1) * lanes)
            qa = qa_ref[own, span]
            qa = put_lanes(qa, 3, head, -jnp.log(self_parts[head]))
            qa = put_lanes(qa, 6, head, -jnp.log(cross_parts[head]))
            qa_ref[own, span] = qa


def backward_kernel(block_count, image_count, present, *refs):
    q_refs = refs[:block_count]
    k_refs = refs[block_count : 2 * block_count]
    v_refs = refs[2 * block_count : 3 * block_count]
    (
        ck_ref,
        cv_ref,
        gain_ref,
        cos_ref,
        sin_ref,
        so_ref,
        co_ref,
        qa_ref,
        ka_ref,
        ca_ref,
        gm_ref,
        gq_ref,
        gk_ref,
        gv_ref,
        gck_ref,
        gcv_ref,
        stat_ref,
        ga_ref,
        va_ref,
        cva_ref,
        kt_ref,
        ct_ref,
        dq_ref,
        dk_ref,
        dv_ref,
        dck_ref,
        dcv_ref,
    ) = refs[3 * block_count :]
    rows = cos_ref.shape[0]
    cap_rows = ck_ref.shape[0] // image_count
    same = halves_matrix(False)
    crossed = halves_matrix(True)
    grads = gm_ref[...]
    grads_float = grads.astype(f32)
    cross_product = grads_float * co_ref[...].astype(f32)
    self_delta = half_sums(grads_float * so_ref[...].astype(f32), crossed)
    cross_delta = half_sums(cross_product, crossed)
    values = jnp.concatenate([ref[...] for ref in v_refs], axis=0)
    blank = jnp.zeros_like(grads)
    lane = lane_index(rows) % half_lanes
    self_ones = jnp.where(lane < 3, 1.0, 0.0).astype(bf16)
    lane_cap = lane_index(ck_ref.shape[0]) % half_lanes
    cross_ones = jnp.where((lane_cap >= 3) & (lane_cap < 6), 1.0, 0.0).astype(bf16)
    for head, (ga, va, cva) in enumerate(
        zip(
            pair_operands(grads, blank),
            pair_operands(values, self_ones),
            pair_operands(cv_ref[...], cross_ones),
        )
    ):
        span = slice(head * lanes, (head + 1) * lanes)
        ga = put_lanes(ga, 0, head, -self_delta)
        ga = put_lanes(ga, 3, head, -cross_delta)
        ga_ref[:, span] = ga
        va_ref[:, span] = va
        cva_ref[:, span] = cva
        kt_ref[span, :] = ka_ref[:, span].astype(f32).T.astype(bf16)
        ct_ref[span, :] = ca_ref[:, span].astype(f32).T.astype(bf16)
    dk_ref[...] = jnp.zeros_like(dk_ref)
    dv_ref[...] = jnp.zeros_like(dv_ref)
    dck_ref[...] = jnp.zeros_like(dck_ref)
    dcv_ref[...] = jnp.zeros_like(dcv_ref)
    for index, (start, size) in enumerate(blocks_of(rows)):
        own = slice(start, start + size)
        for head in range(2):
            span = slice(head * lanes, (head + 1) * lanes)
            top = head * half_lanes
            place = slice(head * lanes + top, head * lanes + top + half_lanes)
            qa = qa_ref[own, span]
            ga = ga_ref[own, span]
            probs = jnp.exp(dot_nt(ka_ref[:, span], qa))
            grad_scores = (probs * dot_nt(va_ref[:, span], ga)).astype(bf16)
            dv_ref[:, span] += dot_nn(probs.astype(bf16), ga)
            dk_ref[:, span] += dot_nn(grad_scores, qa)
            dq_ref[top : top + half_lanes, own] = dot_nn(kt_ref[place, :], grad_scores)
        for image in range(image_count):

            @pl.when(present[index * image_count + image] > 0)
            def _():
                caps = slice(image * cap_rows, (image + 1) * cap_rows)
                for head in range(2):
                    span = slice(head * lanes, (head + 1) * lanes)
                    top = head * half_lanes
                    place = slice(head * lanes + top, head * lanes + top + half_lanes)
                    gate = gain_ref[0, 3:4, top : top + 1]
                    qa = qa_ref[own, span]
                    ga = ga_ref[own, span]
                    probs = jnp.exp(dot_nt(ca_ref[caps, span], qa))
                    grad_scores = (probs * dot_nt(cva_ref[caps, span], ga)).astype(bf16)
                    dcv_ref[caps, span] += dot_nn(probs.astype(bf16), ga)
                    dck_ref[caps, span] += dot_nn(grad_scores, qa)
                    dq_ref[top : top + half_lanes, own] += gate * dot_nn(
                        ct_ref[place, caps], grad_scores
                    )

    cosine = cos_ref[...]
    sine = sin_ref[...]
    gate_row = gain_ref[0, 3:4, :]
    scale = 1.0 / math.sqrt(half_lanes)
    sums = []
    for refs_of, place, out_ref, grad in (
        (q_refs, 0, gq_ref, dq_ref[...].T * scale),
        (k_refs, 1, gk_ref, both(dk_ref[:, 0:lanes], dk_ref[:, lanes:])),
    ):
        raw = jnp.concatenate([ref[...] for ref in refs_of], axis=0).astype(f32)
        normed, factor = head_unit(raw, same)
        turned = grad * cosine - swap_quarters(grad) * sine
        sums.append(jnp.sum(turned * normed, axis=0, keepdims=True))
        gain = gain_ref[0, place : place + 1, :]
        out_ref[...] = head_unit_back(turned * gain, normed, factor, same).astype(bf16)
    gv_ref[...] = both(dv_ref[:, 0:lanes], dv_ref[:, lanes:]).astype(bf16)
    grad = both(dck_ref[:, 0:lanes], dck_ref[:, lanes:]) * gate_row
    normed, factor = head_unit(ck_ref[...].astype(f32), same)
    sums.append(jnp.sum(grad * normed, axis=0, keepdims=True))
    gck_ref[...] = head_unit_back(grad * gain_ref[0, 2:3, :], normed, factor, same).astype(bf16)
    gcv_ref[...] = (both(dcv_ref[:, 0:lanes], dcv_ref[:, lanes:]) * gate_row).astype(bf16)
    sums.append(jnp.sum(cross_product, axis=0, keepdims=True))
    stat_ref[0] = jnp.concatenate(sums + [jnp.zeros((4, lanes), f32)], axis=0)


def columns_spec(rows, width):
    return pl.BlockSpec((rows, width), lambda pair, *_: (0, pair))


def whole_spec(rows):
    return pl.BlockSpec((rows, lanes), lambda pair, *_: (0, 0))


def gain_spec():
    return pl.BlockSpec((1, 8, lanes), lambda pair, *_: (pair, 0, 0))


def attention_forward(present, q_raw, k_raw, values, ck_raw, cap_values, gains, tables, images):
    cosine, sine, fq, fk, fc = tables
    count = len(q_raw)
    local = q_raw[0].shape[0]
    rows = local * count
    caps = ck_raw.shape[0]
    pairs = q_raw[0].shape[1] // lanes
    width = pairs * lanes
    grid = pltpu.PrefetchScalarGridSpec(
        num_scalar_prefetch=1,
        grid=(pairs,),
        in_specs=[columns_spec(local, lanes)] * (3 * count)
        + [columns_spec(caps, lanes)] * 2
        + [gain_spec()]
        + [whole_spec(rows)] * 4
        + [whole_spec(caps)],
        out_specs=[columns_spec(rows, lanes)] * 3
        + [columns_spec(rows, 2 * lanes)] * 2
        + [columns_spec(caps, 2 * lanes)],
        scratch_shapes=[
            pltpu.VMEM((rows, 2 * lanes), bf16),
            pltpu.VMEM((caps, 2 * lanes), bf16),
            pltpu.VMEM((query_block, 2 * lanes), f32),
        ],
    )
    return pl.pallas_call(
        lambda *refs: forward_kernel(count, images, *refs),
        grid_spec=grid,
        out_shape=[jax.ShapeDtypeStruct((rows, width), bf16)] * 3
        + [jax.ShapeDtypeStruct((rows, 2 * width), bf16)] * 2
        + [jax.ShapeDtypeStruct((caps, 2 * width), bf16)],
        compiler_params=pltpu.CompilerParams(vmem_limit_bytes=vmem_bytes),
        name="attention_forward",
    )(present, *q_raw, *k_raw, *values, ck_raw, cap_values, gains, cosine, sine, fq, fk, fc)


def attention_backward(
    present, q_raw, k_raw, values, ck_raw, cap_values, gains, tables, kept, grad_mixed, images
):
    cosine, sine = tables[:2]
    self_out, cross_out, qa, ka, ca = kept
    count = len(q_raw)
    local = q_raw[0].shape[0]
    rows = local * count
    caps = ck_raw.shape[0]
    pairs = q_raw[0].shape[1] // lanes
    width = pairs * lanes
    grid = pltpu.PrefetchScalarGridSpec(
        num_scalar_prefetch=1,
        grid=(pairs,),
        in_specs=[columns_spec(local, lanes)] * (3 * count)
        + [columns_spec(caps, lanes)] * 2
        + [gain_spec()]
        + [whole_spec(rows)] * 2
        + [columns_spec(rows, lanes)] * 2
        + [columns_spec(rows, 2 * lanes)] * 2
        + [columns_spec(caps, 2 * lanes)]
        + [columns_spec(rows, lanes)],
        out_specs=[columns_spec(rows, lanes)] * 3
        + [columns_spec(caps, lanes)] * 2
        + [gain_spec()],
        scratch_shapes=[
            pltpu.VMEM((rows, 2 * lanes), bf16),
            pltpu.VMEM((rows, 2 * lanes), bf16),
            pltpu.VMEM((caps, 2 * lanes), bf16),
            pltpu.VMEM((2 * lanes, rows), bf16),
            pltpu.VMEM((2 * lanes, caps), bf16),
            pltpu.VMEM((lanes, rows), f32),
            pltpu.VMEM((rows, 2 * lanes), f32),
            pltpu.VMEM((rows, 2 * lanes), f32),
            pltpu.VMEM((caps, 2 * lanes), f32),
            pltpu.VMEM((caps, 2 * lanes), f32),
        ],
    )
    return pl.pallas_call(
        lambda *refs: backward_kernel(count, images, *refs),
        grid_spec=grid,
        out_shape=[jax.ShapeDtypeStruct((rows, width), bf16)] * 3
        + [jax.ShapeDtypeStruct((caps, width), bf16)] * 2
        + [jax.ShapeDtypeStruct((pairs, 8, lanes), f32)],
        compiler_params=pltpu.CompilerParams(vmem_limit_bytes=vmem_bytes),
        name="attention_backward",
    )(
        present,
        *q_raw,
        *k_raw,
        *values,
        ck_raw,
        cap_values,
        gains,
        cosine,
        sine,
        self_out,
        cross_out,
        qa,
        ka,
        ca,
        grad_mixed,
    )


def gather_blocks(block):
    count = lax.axis_size("tensor")
    return [block] + [
        lax.ppermute(block, "tensor", [((i + step) % count, i) for i in range(count)])
        for step in range(1, count)
    ]


def scatter_blocks(own, others):
    count = lax.axis_size("tensor")
    for step in range(1, count):
        moved = lax.ppermute(
            others[step - 1].astype(bf16),
            "tensor",
            [(i, (i + step) % count) for i in range(count)],
        )
        own = own + moved.astype(f32)
    return own


def per_token(table, images):
    rows = table[0:1]
    for image in range(1, table.shape[0]):
        rows = jnp.where(images[:, None] == image, table[image : image + 1], rows)
    return rows


def image_sums(values, images, count):
    chosen = (jnp.arange(count, dtype=jnp.int32)[:, None] == images[None, :]).astype(bf16)
    return dot_nn(chosen, values.astype(bf16))


def rope_tables(positions):
    lane = jnp.arange(lanes, dtype=jnp.int32)
    place = lane % 32
    freqs = jnp.power(theta, -((place % 16).astype(f32) / 16))
    spot = jnp.where(place[None, :] < 16, positions[0][:, None], positions[1][:, None])
    angles = spot.astype(f32) * freqs[None, :]
    sign = jnp.where(lane % half_lanes < 32, -1.0, 1.0)
    return (jnp.cos(angles), jnp.sin(angles) * sign[None, :])


def feature_lanes(images, valid, count, ones_at):
    lane = (jnp.arange(lanes, dtype=jnp.int32) % half_lanes)[None, :]
    outside = (lane < count) & ((lane != images[:, None]) | ~valid[:, None])
    ones = (lane >= ones_at) & (lane < ones_at + 3)
    return jnp.where(outside, -penalty, jnp.where(ones, 1.0, 0.0)).astype(bf16)


def pad_columns(values, width):
    return jnp.pad(values, ((0, 0), (0, width - values.shape[1])))


def on_device(
    tokens,
    timestep,
    caption,
    caption_mask,
    image_lengths,
    patch_pos,
    ada_weight,
    ada_bias,
    attention_norm,
    attention_post,
    feedforward_norm,
    feedforward_post,
    query_weight,
    key_weight,
    value_weight,
    query_gain,
    key_gain,
    cross_keys,
    cross_values,
    cross_gain,
    cross_gate,
    output_weight,
    gate_weight,
    up_weight,
    down_weight,
    cotangent,
):
    local_rows, model_width = tokens.shape
    tensor_count = lax.axis_size("tensor")
    tensor_place = lax.axis_index("tensor")
    group_tokens = local_rows * tensor_count
    image_count, cap_len, cap_width = caption.shape
    local_heads, head_size = query_gain.shape
    head_columns = local_heads * head_size
    pairs = (local_heads + 1) // 2
    pair_columns = pairs * lanes
    cap_total = image_count * cap_len

    token_blocks = gather_blocks(tokens)

    places = (
        jnp.arange(group_tokens, dtype=jnp.int32) + tensor_place * local_rows
    ) % group_tokens
    image_all = jnp.zeros((group_tokens,), jnp.int32)
    end = jnp.zeros((), jnp.int32)
    for image in range(image_count - 1):
        end = end + image_lengths[image]
        image_all = image_all + (places >= end).astype(jnp.int32)
    image_own = image_all[:local_rows]
    positions = jnp.roll(patch_pos, -tensor_place * local_rows, axis=1)
    cosine, sine = rope_tables(positions)
    lane = (jnp.arange(lanes, dtype=jnp.int32) % half_lanes)[None, :]
    query_features = (lane == image_all[:, None]).astype(bf16)
    everywhere = jnp.ones((group_tokens,), jnp.bool_)
    key_features = feature_lanes(image_all, everywhere, image_count, 3)
    cap_features = feature_lanes(
        jnp.arange(cap_total, dtype=jnp.int32) // cap_len,
        caption_mask.reshape(-1) > 0,
        image_count,
        6,
    )
    block_total = -(-group_tokens // query_block)
    block_place = jnp.arange(group_tokens, dtype=jnp.int32) // query_block
    hit = (block_place[None, None, :] == jnp.arange(block_total)[:, None, None]) & (
        image_all[None, None, :] == jnp.arange(image_count)[None, :, None]
    )
    present = jnp.max(hit.astype(jnp.int32), axis=2).reshape(-1)
    head_gate = jnp.tanh(cross_gate)
    gain_rows = jnp.stack(
        [
            query_gain.reshape(-1),
            key_gain.reshape(-1),
            cross_gain.reshape(-1),
            jnp.repeat(head_gate, head_size),
        ]
    )
    gains = (
        jnp.pad(gain_rows, ((0, 4), (0, pair_columns - head_columns)))
        .reshape(8, pairs, lanes)
        .transpose(1, 0, 2)
    )
    tables = (cosine, sine, query_features, key_features, cap_features)

    time_float = timestep.astype(f32)
    silu_time = (time_float * sigmoid_of(time_float)).astype(bf16)
    mod_part = dot_nn(silu_time, ada_weight) + ada_bias
    modulation = lax.all_gather(mod_part, "tensor", axis=1, tiled=True)
    scale_attn = 1.0 + modulation[:, :model_width]
    gate_attn = jnp.tanh(modulation[:, model_width : 2 * model_width])
    scale_ffn = 1.0 + modulation[:, 2 * model_width : 3 * model_width]
    gate_ffn = jnp.tanh(modulation[:, 3 * model_width :])
    norm_attn = scale_attn * attention_norm
    post_attn = gate_attn * attention_post
    norm_ffn = scale_ffn * feedforward_norm
    post_ffn = gate_ffn * feedforward_post

    cap_flat = caption.reshape(cap_total, cap_width)
    ck_raw = pad_columns(dot_nn(cap_flat, cross_keys), pair_columns)
    cap_values = pad_columns(dot_nn(cap_flat, cross_values).astype(bf16), pair_columns)

    normed, q_raw, k_raw, values = [], [], [], []
    for index, block in enumerate(token_blocks):
        images = image_all[index * local_rows : (index + 1) * local_rows]
        unit = unit_rows(block.astype(f32))[0]
        rows = (unit * per_token(norm_attn, images)).astype(bf16)
        normed.append(rows)
        q_raw.append(pad_columns(dot_nn(rows, query_weight), pair_columns))
        k_raw.append(pad_columns(dot_nn(rows, key_weight), pair_columns))
        values.append(pad_columns(dot_nn(rows, value_weight).astype(bf16), pair_columns))

    mixed, *kept = attention_forward(
        present, q_raw, k_raw, values, ck_raw, cap_values, gains, tables, image_count
    )
    mixed = mixed[:, :head_columns]

    def block_rows(array, index):
        return array[index * local_rows : (index + 1) * local_rows]

    attn_others = [
        dot_nn(block_rows(mixed, index), output_weight) for index in range(1, tensor_count)
    ]
    attn_rows = scatter_blocks(dot_nn(block_rows(mixed, 0), output_weight), attn_others)
    attn_unit, attn_factor = unit_rows(attn_rows)
    x_float = tokens.astype(f32)
    hidden = x_float + attn_unit * per_token(post_attn, image_own)
    hidden_unit, hidden_factor = unit_rows(hidden)
    ffn_in = gather_blocks((hidden_unit * per_token(norm_ffn, image_own)).astype(bf16))

    gate_pre, up_pre, inner, ffn_parts = [], [], [], []
    for rows in ffn_in:
        gate_block = dot_nn(rows, gate_weight)
        up_block = dot_nn(rows, up_weight)
        inner_block = (gate_block * sigmoid_of(gate_block) * up_block).astype(bf16)
        gate_pre.append(gate_block)
        up_pre.append(up_block)
        inner.append(inner_block)
        ffn_parts.append(dot_nn(inner_block, down_weight))
    ffn_rows = scatter_blocks(ffn_parts[0], ffn_parts[1:])
    ffn_unit, ffn_factor = unit_rows(ffn_rows)
    layer_out = (hidden + ffn_unit * per_token(post_ffn, image_own)).astype(bf16)

    grad_out = cotangent.astype(f32)
    sums_ffn_post = image_sums(grad_out * ffn_unit, image_own, image_count)
    grad_ffn = gather_blocks(
        unit_back(grad_out * per_token(post_ffn, image_own), ffn_unit, ffn_factor).astype(bf16)
    )
    grad_gate, grad_up, grad_in_parts = [], [], []
    for index, rows in enumerate(grad_ffn):
        grad_inner = dot_nt(rows, down_weight)
        sig = sigmoid_of(gate_pre[index])
        act = gate_pre[index] * sig
        grad_up_block = (grad_inner * act).astype(bf16)
        grad_gate_block = (
            grad_inner * up_pre[index] * sig * (1.0 + gate_pre[index] * (1.0 - sig))
        ).astype(bf16)
        grad_up.append(grad_up_block)
        grad_gate.append(grad_gate_block)
        grad_in_parts.append(
            dot_nt(grad_gate_block, gate_weight) + dot_nt(grad_up_block, up_weight)
        )
    grad_ffn_in = scatter_blocks(grad_in_parts[0], grad_in_parts[1:])

    def joined(blocks):
        return jnp.concatenate(blocks, axis=0)

    ffn_in_all = joined(ffn_in)
    gate_up_grad = dot_tn(
        ffn_in_all, jnp.concatenate([joined(grad_gate), joined(grad_up)], axis=1)
    ).astype(bf16)
    down_grad = dot_tn(joined(grad_ffn), joined(inner)).astype(bf16)

    sums_ffn_norm = image_sums(grad_ffn_in * hidden_unit, image_own, image_count)
    grad_hidden = grad_out + unit_back(
        grad_ffn_in * per_token(norm_ffn, image_own), hidden_unit, hidden_factor
    )
    sums_attn_post = image_sums(grad_hidden * attn_unit, image_own, image_count)
    grad_attn = joined(
        gather_blocks(
            unit_back(
                grad_hidden * per_token(post_attn, image_own), attn_unit, attn_factor
            ).astype(bf16)
        )
    )
    output_grad = dot_tn(grad_attn, mixed).astype(bf16)
    grad_mixed = pad_columns(dot_nt(grad_attn, output_weight).astype(bf16), pair_columns)
    grad_q, grad_k, grad_v, grad_ck, grad_cv, stats = attention_backward(
        present,
        q_raw,
        k_raw,
        values,
        ck_raw,
        cap_values,
        gains,
        tables,
        kept,
        grad_mixed,
        image_count,
    )
    stats = stats.transpose(1, 0, 2).reshape(8, pair_columns)[:, :head_columns]
    stats = stats.reshape(8, local_heads, head_size)
    grad_head_gate = jnp.sum(stats[3], axis=1) * (1.0 - head_gate * head_gate)
    grad_qkv = jnp.concatenate(
        [part[:, :head_columns] for part in (grad_q, grad_k, grad_v)], axis=1
    )
    grad_cap = jnp.concatenate([part[:, :head_columns] for part in (grad_ck, grad_cv)], axis=1)

    def input_part(index):
        return sum(
            dot_nt(block_rows(part[:, :head_columns], index), weight)
            for part, weight in (
                (grad_q, query_weight),
                (grad_k, key_weight),
                (grad_v, value_weight),
            )
        )

    grad_normed_others = [input_part(index) for index in range(1, tensor_count)]
    grad_normed = scatter_blocks(input_part(0), grad_normed_others)
    cap_grad = dot_tn(cap_flat, grad_cap).astype(bf16)
    qkv_grad = dot_tn(joined(normed), grad_qkv).astype(bf16)

    x_unit, x_factor = unit_rows(x_float)
    sums_attn_norm = image_sums(grad_normed * x_unit, image_own, image_count)
    tokens_grad = grad_hidden + unit_back(
        grad_normed * per_token(norm_attn, image_own), x_unit, x_factor
    )

    norm_parts = jnp.stack(
        [
            jnp.sum(sums_attn_norm * scale_attn, axis=0),
            jnp.sum(sums_attn_post * gate_attn, axis=0),
            jnp.sum(sums_ffn_norm * scale_ffn, axis=0),
            jnp.sum(sums_ffn_post * gate_ffn, axis=0),
        ]
    )
    grad_mod_part = jnp.concatenate(
        [
            sums_attn_norm * attention_norm,
            sums_attn_post * attention_post * (1.0 - gate_attn * gate_attn),
            sums_ffn_norm * feedforward_norm,
            sums_ffn_post * feedforward_post * (1.0 - gate_ffn * gate_ffn),
        ],
        axis=1,
    )
    norm_sums = lax.psum(norm_parts, ("dp", "tensor"))
    grad_mod = lax.psum_scatter(grad_mod_part, "tensor", scatter_dimension=1, tiled=True)
    mod_all = lax.all_gather(grad_mod, "dp", axis=0, tiled=True)
    time_all = lax.all_gather(silu_time, "dp", axis=0, tiled=True)
    bias_own = jnp.sum(mod_all, axis=0)
    dp_count = lax.axis_size("dp")
    ada_rows = silu_time.shape[1] // dp_count
    time_own = lax.dynamic_slice_in_dim(time_all, lax.axis_index("dp") * ada_rows, ada_rows, axis=1)
    ada_grad = dot_tn(time_own, mod_all.astype(bf16))
    head_parts = jnp.concatenate([stats[:3].reshape(-1), grad_head_gate])
    head_sums = lax.psum(head_parts, "dp")
    gain_sums = head_sums[: 3 * head_columns].reshape(3, local_heads, head_size)
    gate_own = head_sums[3 * head_columns :]

    def over_dp(gradient):
        return lax.psum_scatter(gradient, "dp", scatter_dimension=0, tiled=True).astype(f32)

    gate_up_sum = over_dp(gate_up_grad)
    down_sum = over_dp(down_grad).T
    output_sum = over_dp(output_grad).T
    cap_sum = over_dp(cap_grad)
    qkv_sum = over_dp(qkv_grad)
    hidden_columns = gate_weight.shape[1]
    return (
        layer_out,
        tokens_grad,
        ada_grad,
        bias_own,
        norm_sums[0],
        norm_sums[1],
        norm_sums[2],
        norm_sums[3],
        qkv_sum[:, :head_columns],
        qkv_sum[:, head_columns : 2 * head_columns],
        qkv_sum[:, 2 * head_columns :],
        gain_sums[0],
        gain_sums[1],
        cap_sum[:, :head_columns],
        cap_sum[:, head_columns:],
        gain_sums[2],
        gate_own,
        output_sum,
        gate_up_sum[:, :hidden_columns],
        gate_up_sum[:, hidden_columns:],
        down_sum,
    )


def solution(mesh):
    placed = (
        P(("dp", "tensor"), None),
        P("dp", None),
        P("dp", None, None),
        P("dp", None),
        P("dp"),
        P(None, "dp"),
        P(None, "tensor"),
        P("tensor"),
        P(),
        P(),
        P(),
        P(),
        P(None, "tensor"),
        P(None, "tensor"),
        P(None, "tensor"),
        P("tensor", None),
        P("tensor", None),
        P(None, "tensor"),
        P(None, "tensor"),
        P("tensor", None),
        P("tensor"),
        P("tensor", None),
        P(None, "tensor"),
        P(None, "tensor"),
        P("tensor", None),
        P(("dp", "tensor"), None),
    )
    return jax.shard_map(
        on_device,
        mesh=mesh,
        in_specs=placed,
        out_specs=(
            P(("dp", "tensor"), None),
            P(("dp", "tensor"), None),
            P("dp", "tensor"),
            P("tensor"),
            P(),
            P(),
            P(),
            P(),
            P("dp", "tensor"),
            P("dp", "tensor"),
            P("dp", "tensor"),
            P("tensor", None),
            P("tensor", None),
            P("dp", "tensor"),
            P("dp", "tensor"),
            P("tensor", None),
            P("tensor"),
            P("tensor", "dp"),
            P("dp", "tensor"),
            P("dp", "tensor"),
            P("tensor", "dp"),
        ),
        check_vma=False,
    )
```

```python
import math

import jax
import jax.numpy as jnp
from jax import lax
from jax.experimental import pallas as pl
from jax.experimental.pallas import tpu as pltpu
from jax.sharding import PartitionSpec as P

epsilon = 1e-05
penalty = 1024.0
theta = 10000.0
lanes = 128
half_lanes = 64
query_block = 256
bf16 = jnp.bfloat16
f32 = jnp.float32
vmem_bytes = 60 * 1024 * 1024


def sigmoid_of(values):
    return 1.0 / (1.0 + jnp.exp(-values))


def unit_rows(values):
    factor = lax.rsqrt(jnp.mean(values * values, axis=-1, keepdims=True) + epsilon)
    return (values * factor, factor)


def unit_back(gradient, normed, factor):
    return factor * (gradient - normed * jnp.mean(gradient * normed, axis=-1, keepdims=True))


def dot_nn(left, right):
    return lax.dot_general(left, right, (((1,), (0,)), ((), ())), preferred_element_type=f32)


def dot_nt(left, right):
    return lax.dot_general(left, right, (((1,), (1,)), ((), ())), preferred_element_type=f32)


def dot_tn(left, right):
    return lax.dot_general(left, right, (((0,), (0,)), ((), ())), preferred_element_type=f32)


def lane_index(rows):
    return lax.broadcasted_iota(jnp.int32, (rows, lanes), 1)


def halves_matrix(crossed):
    row = lax.broadcasted_iota(jnp.int32, (lanes, lanes), 0) // half_lanes
    col = lax.broadcasted_iota(jnp.int32, (lanes, lanes), 1) // half_lanes
    same = (row != col) if crossed else (row == col)
    return jnp.where(same, 1.0, 0.0).astype(bf16)


def half_sums(values, matrix):
    high = values.astype(bf16)
    rest = (values - high.astype(f32)).astype(bf16)
    return dot_nn(high, matrix) + dot_nn(rest, matrix)


def head_unit(values, matrix):
    factor = lax.rsqrt(half_sums(values * values, matrix) * (1.0 / half_lanes) + epsilon)
    return values * factor, factor


def head_unit_back(gradient, normed, factor, matrix):
    mean = half_sums(gradient * normed, matrix) * (1.0 / half_lanes)
    return factor * (gradient - normed * mean)


def swap_quarters(values):
    lane = lane_index(values.shape[0])
    ahead = pltpu.roll(values, lanes - 32, 1)
    behind = pltpu.roll(values, 32, 1)
    return jnp.where(lane % half_lanes < 32, ahead, behind)


def three_parts(values):
    first = values.astype(bf16)
    rest = values - first.astype(f32)
    second = rest.astype(bf16)
    third = (rest - second.astype(f32)).astype(bf16)
    return first, second, third


def put_lanes(target, place, head, values):
    lane = lane_index(target.shape[0])
    base = half_lanes * (1 - head) + place
    for offset, part in enumerate(three_parts(values)):
        target = jnp.where(lane == base + offset, part, target)
    return target


def both(head_zero, head_one):
    return jnp.where(lane_index(head_zero.shape[0]) < half_lanes, head_zero, head_one)


def pair_operands(values, features):
    return both(values, features), both(features, values)


def blocks_of(rows):
    starts = list(range(0, rows, query_block))
    return [(start, min(query_block, rows - start)) for start in starts]


def forward_kernel(block_count, image_count, present, *refs):
    q_refs = refs[:block_count]
    k_refs = refs[block_count : 2 * block_count]
    v_refs = refs[2 * block_count : 3 * block_count]
    (
        ck_ref,
        cv_ref,
        gain_ref,
        cos_ref,
        sin_ref,
        fq_ref,
        fk_ref,
        fc_ref,
        mixed_ref,
        so_ref,
        co_ref,
        qa_ref,
        ka_ref,
        ca_ref,
        va_ref,
        cva_ref,
        acc_ref,
    ) = refs[3 * block_count :]
    rows = cos_ref.shape[0]
    cap_rows = ck_ref.shape[0] // image_count
    same = halves_matrix(False)
    q_raw = jnp.concatenate([ref[...] for ref in q_refs], axis=0).astype(f32)
    k_raw = jnp.concatenate([ref[...] for ref in k_refs], axis=0).astype(f32)
    cosine = cos_ref[...]
    sine = sin_ref[...]
    q_gained = head_unit(q_raw, same)[0] * gain_ref[0, 0:1, :]
    q_turned = q_gained * cosine + swap_quarters(q_gained) * sine
    queries = (q_turned.astype(bf16).astype(f32) * (1.0 / math.sqrt(half_lanes))).astype(bf16)
    k_gained = head_unit(k_raw, same)[0] * gain_ref[0, 1:2, :]
    keys = (k_gained * cosine + swap_quarters(k_gained) * sine).astype(bf16)
    cap_keys = (head_unit(ck_ref[...].astype(f32), same)[0] * gain_ref[0, 2:3, :]).astype(bf16)
    values = jnp.concatenate([ref[...] for ref in v_refs], axis=0)
    cap_values = cv_ref[...]
    ones = jnp.ones_like(values)
    cap_ones = jnp.ones_like(cap_values)
    for head, (qa, ka, ca, va, cva) in enumerate(
        zip(
            pair_operands(queries, fq_ref[...]),
            pair_operands(keys, fk_ref[...]),
            pair_operands(cap_keys, fc_ref[...]),
            pair_operands(values, ones),
            pair_operands(cap_values, cap_ones),
        )
    ):
        span = slice(head * lanes, (head + 1) * lanes)
        qa_ref[:, span] = qa
        ka_ref[:, span] = ka
        ca_ref[:, span] = ca
        va_ref[:, span] = va
        cva_ref[:, span] = cva
    gate = gain_ref[0, 3:4, :]
    for index, (start, size) in enumerate(blocks_of(rows)):
        own = slice(start, start + size)
        self_parts = []
        for head in range(2):
            span = slice(head * lanes, (head + 1) * lanes)
            scores = dot_nt(qa_ref[own, span], ka_ref[:, span])
            self_parts.append(dot_nn(jnp.exp(scores).astype(bf16), va_ref[:, span]))
        acc_ref[0:size, :] = jnp.zeros((size, 2 * lanes), f32)
        for image in range(image_count):

            @pl.when(present[index * image_count + image] > 0)
            def _():
                caps = slice(image * cap_rows, (image + 1) * cap_rows)
                for head in range(2):
                    span = slice(head * lanes, (head + 1) * lanes)
                    scores = dot_nt(qa_ref[own, span], ca_ref[caps, span])
                    acc_ref[0:size, span] += dot_nn(
                        jnp.exp(scores).astype(bf16), cva_ref[caps, span]
                    )

        cross_parts = [acc_ref[0:size, 0:lanes], acc_ref[0:size, lanes:]]
        outs = []
        for parts in (self_parts, cross_parts):
            total = pltpu.roll(both(parts[1], parts[0]), half_lanes, 1)
            outs.append(both(parts[0], parts[1]) / total)
        so_ref[own, :] = outs[0].astype(bf16)
        co_ref[own, :] = outs[1].astype(bf16)
        mixed_ref[own, :] = (outs[0] + gate * outs[1]).astype(bf16)
        for head in range(2):
            span = slice(head * lanes, (head + 1) * lanes)
            qa = qa_ref[own, span]
            qa = put_lanes(qa, 3, head, -jnp.log(self_parts[head]))
            qa = put_lanes(qa, 6, head, -jnp.log(cross_parts[head]))
            qa_ref[own, span] = qa


def backward_kernel(block_count, image_count, present, *refs):
    q_refs = refs[:block_count]
    k_refs = refs[block_count : 2 * block_count]
    v_refs = refs[2 * block_count : 3 * block_count]
    (
        ck_ref,
        cv_ref,
        gain_ref,
        cos_ref,
        sin_ref,
        so_ref,
        co_ref,
        qa_ref,
        ka_ref,
        ca_ref,
        gm_ref,
        gq_ref,
        gk_ref,
        gv_ref,
        gck_ref,
        gcv_ref,
        stat_ref,
        ga_ref,
        va_ref,
        cva_ref,
        kt_ref,
        ct_ref,
        dq_ref,
        dk_ref,
        dv_ref,
        dck_ref,
        dcv_ref,
    ) = refs[3 * block_count :]
    rows = cos_ref.shape[0]
    cap_rows = ck_ref.shape[0] // image_count
    same = halves_matrix(False)
    crossed = halves_matrix(True)
    grads = gm_ref[...]
    grads_float = grads.astype(f32)
    cross_product = grads_float * co_ref[...].astype(f32)
    self_delta = half_sums(grads_float * so_ref[...].astype(f32), crossed)
    cross_delta = half_sums(cross_product, crossed)
    values = jnp.concatenate([ref[...] for ref in v_refs], axis=0)
    blank = jnp.zeros_like(grads)
    lane = lane_index(rows) % half_lanes
    self_ones = jnp.where(lane < 3, 1.0, 0.0).astype(bf16)
    lane_cap = lane_index(ck_ref.shape[0]) % half_lanes
    cross_ones = jnp.where((lane_cap >= 3) & (lane_cap < 6), 1.0, 0.0).astype(bf16)
    for head, (ga, va, cva) in enumerate(
        zip(
            pair_operands(grads, blank),
            pair_operands(values, self_ones),
            pair_operands(cv_ref[...], cross_ones),
        )
    ):
        span = slice(head * lanes, (head + 1) * lanes)
        ga = put_lanes(ga, 0, head, -self_delta)
        ga = put_lanes(ga, 3, head, -cross_delta)
        ga_ref[:, span] = ga
        va_ref[:, span] = va
        cva_ref[:, span] = cva
        kt_ref[span, :] = ka_ref[:, span].astype(f32).T.astype(bf16)
        ct_ref[span, :] = ca_ref[:, span].astype(f32).T.astype(bf16)
    dk_ref[...] = jnp.zeros_like(dk_ref)
    dv_ref[...] = jnp.zeros_like(dv_ref)
    dck_ref[...] = jnp.zeros_like(dck_ref)
    dcv_ref[...] = jnp.zeros_like(dcv_ref)
    for index, (start, size) in enumerate(blocks_of(rows)):
        own = slice(start, start + size)
        for head in range(2):
            span = slice(head * lanes, (head + 1) * lanes)
            top = head * half_lanes
            place = slice(head * lanes + top, head * lanes + top + half_lanes)
            qa = qa_ref[own, span]
            ga = ga_ref[own, span]
            probs = jnp.exp(dot_nt(ka_ref[:, span], qa))
            grad_scores = (probs * dot_nt(va_ref[:, span], ga)).astype(bf16)
            dv_ref[:, span] += dot_nn(probs.astype(bf16), ga)
            dk_ref[:, span] += dot_nn(grad_scores, qa)
            dq_ref[top : top + half_lanes, own] = dot_nn(kt_ref[place, :], grad_scores)
        for image in range(image_count):

            @pl.when(present[index * image_count + image] > 0)
            def _():
                caps = slice(image * cap_rows, (image + 1) * cap_rows)
                for head in range(2):
                    span = slice(head * lanes, (head + 1) * lanes)
                    top = head * half_lanes
                    place = slice(head * lanes + top, head * lanes + top + half_lanes)
                    gate = gain_ref[0, 3:4, top : top + 1]
                    qa = qa_ref[own, span]
                    ga = ga_ref[own, span]
                    probs = jnp.exp(dot_nt(ca_ref[caps, span], qa))
                    grad_scores = (probs * dot_nt(cva_ref[caps, span], ga)).astype(bf16)
                    dcv_ref[caps, span] += dot_nn(probs.astype(bf16), ga)
                    dck_ref[caps, span] += dot_nn(grad_scores, qa)
                    dq_ref[top : top + half_lanes, own] += gate * dot_nn(
                        ct_ref[place, caps], grad_scores
                    )

    cosine = cos_ref[...]
    sine = sin_ref[...]
    gate_row = gain_ref[0, 3:4, :]
    scale = 1.0 / math.sqrt(half_lanes)
    sums = []
    for refs_of, place, out_ref, grad in (
        (q_refs, 0, gq_ref, dq_ref[...].T * scale),
        (k_refs, 1, gk_ref, both(dk_ref[:, 0:lanes], dk_ref[:, lanes:])),
    ):
        raw = jnp.concatenate([ref[...] for ref in refs_of], axis=0).astype(f32)
        normed, factor = head_unit(raw, same)
        turned = grad * cosine - swap_quarters(grad) * sine
        sums.append(jnp.sum(turned * normed, axis=0, keepdims=True))
        gain = gain_ref[0, place : place + 1, :]
        out_ref[...] = head_unit_back(turned * gain, normed, factor, same).astype(bf16)
    gv_ref[...] = both(dv_ref[:, 0:lanes], dv_ref[:, lanes:]).astype(bf16)
    grad = both(dck_ref[:, 0:lanes], dck_ref[:, lanes:]) * gate_row
    normed, factor = head_unit(ck_ref[...].astype(f32), same)
    sums.append(jnp.sum(grad * normed, axis=0, keepdims=True))
    gck_ref[...] = head_unit_back(grad * gain_ref[0, 2:3, :], normed, factor, same).astype(bf16)
    gcv_ref[...] = (both(dcv_ref[:, 0:lanes], dcv_ref[:, lanes:]) * gate_row).astype(bf16)
    sums.append(jnp.sum(cross_product, axis=0, keepdims=True))
    stat_ref[0] = jnp.concatenate(sums + [jnp.zeros((4, lanes), f32)], axis=0)


def cost_of(seconds):
    return pl.CostEstimate(
        flops=int(seconds * 1.1e15), bytes_accessed=int(seconds * 3e12), transcendentals=0
    )


def columns_spec(rows, width):
    return pl.BlockSpec((rows, width), lambda pair, *_: (0, pair))


def whole_spec(rows):
    return pl.BlockSpec((rows, lanes), lambda pair, *_: (0, 0))


def gain_spec():
    return pl.BlockSpec((1, 8, lanes), lambda pair, *_: (pair, 0, 0))


def attention_forward(present, q_raw, k_raw, values, ck_raw, cap_values, gains, tables, images):
    cosine, sine, fq, fk, fc = tables
    count = len(q_raw)
    local = q_raw[0].shape[0]
    rows = local * count
    caps = ck_raw.shape[0]
    pairs = q_raw[0].shape[1] // lanes
    width = pairs * lanes
    grid = pltpu.PrefetchScalarGridSpec(
        num_scalar_prefetch=1,
        grid=(pairs,),
        in_specs=[columns_spec(local, lanes)] * (3 * count)
        + [columns_spec(caps, lanes)] * 2
        + [gain_spec()]
        + [whole_spec(rows)] * 4
        + [whole_spec(caps)],
        out_specs=[columns_spec(rows, lanes)] * 3
        + [columns_spec(rows, 2 * lanes)] * 2
        + [columns_spec(caps, 2 * lanes)],
        scratch_shapes=[
            pltpu.VMEM((rows, 2 * lanes), bf16),
            pltpu.VMEM((caps, 2 * lanes), bf16),
            pltpu.VMEM((query_block, 2 * lanes), f32),
        ],
    )
    return pl.pallas_call(
        lambda *refs: forward_kernel(count, images, *refs),
        grid_spec=grid,
        out_shape=[jax.ShapeDtypeStruct((rows, width), bf16)] * 3
        + [jax.ShapeDtypeStruct((rows, 2 * width), bf16)] * 2
        + [jax.ShapeDtypeStruct((caps, 2 * width), bf16)],
        compiler_params=pltpu.CompilerParams(vmem_limit_bytes=vmem_bytes),
        cost_estimate=cost_of(60e-6),
        name="attention_forward",
    )(present, *q_raw, *k_raw, *values, ck_raw, cap_values, gains, cosine, sine, fq, fk, fc)


def attention_backward(
    present,
    first,
    calls_pairs,
    earlier,
    q_raw,
    k_raw,
    values,
    ck_raw,
    cap_values,
    gains,
    tables,
    kept,
    grad_mixed,
    images,
):
    cosine, sine = tables[:2]
    self_out, cross_out, qa, ka, ca = kept
    count = len(q_raw)
    local = q_raw[0].shape[0]
    rows = local * count
    caps = ck_raw.shape[0]
    pairs = q_raw[0].shape[1] // lanes
    width = pairs * lanes

    def columns(rows, width):
        return pl.BlockSpec((rows, width), lambda pair, *_: (0, first + pair))

    own_gains = pl.BlockSpec((1, 8, lanes), lambda pair, *_: (first + pair, 0, 0))
    inputs = [
        *q_raw,
        *k_raw,
        *values,
        ck_raw,
        cap_values,
        gains,
        cosine,
        sine,
        self_out,
        cross_out,
        qa,
        ka,
        ca,
        grad_mixed,
    ]
    earlier = list(earlier or [])
    grid = pltpu.PrefetchScalarGridSpec(
        num_scalar_prefetch=1,
        grid=(calls_pairs,),
        in_specs=[columns(local, lanes)] * (3 * count)
        + [columns(caps, lanes)] * 2
        + [own_gains]
        + [whole_spec(rows)] * 2
        + [columns(rows, lanes)] * 2
        + [columns(rows, 2 * lanes)] * 2
        + [columns(caps, 2 * lanes)]
        + [columns(rows, lanes)]
        + [pl.BlockSpec(memory_space=pl.ANY)] * len(earlier),
        out_specs=[columns(rows, lanes)] * 3 + [columns(caps, lanes)] * 2 + [own_gains],
        scratch_shapes=[
            pltpu.VMEM((rows, 2 * lanes), bf16),
            pltpu.VMEM((rows, 2 * lanes), bf16),
            pltpu.VMEM((caps, 2 * lanes), bf16),
            pltpu.VMEM((2 * lanes, rows), bf16),
            pltpu.VMEM((2 * lanes, caps), bf16),
            pltpu.VMEM((lanes, rows), f32),
            pltpu.VMEM((rows, 2 * lanes), f32),
            pltpu.VMEM((rows, 2 * lanes), f32),
            pltpu.VMEM((caps, 2 * lanes), f32),
            pltpu.VMEM((caps, 2 * lanes), f32),
        ],
    )

    def kernel(present_ref, *refs):
        inside = len(inputs)
        backward_kernel(count, images, present_ref, *refs[:inside], *refs[inside + len(earlier) :])

    return pl.pallas_call(
        kernel,
        grid_spec=grid,
        out_shape=[jax.ShapeDtypeStruct((rows, width), bf16)] * 3
        + [jax.ShapeDtypeStruct((caps, width), bf16)] * 2
        + [jax.ShapeDtypeStruct((pairs, 8, lanes), f32)],
        input_output_aliases={1 + len(inputs) + k: k for k in range(len(earlier))},
        compiler_params=pltpu.CompilerParams(vmem_limit_bytes=vmem_bytes),
        cost_estimate=cost_of(15e-6 * calls_pairs),
        name="attention_backward",
    )(present, *inputs, *earlier)


def pick(table_ref, images):
    rows = table_ref[0:1, :]
    for image in range(1, table_ref.shape[0]):
        rows = jnp.where(images == image, table_ref[image : image + 1, :], rows)
    return rows


def unit_of(values):
    factor = lax.rsqrt(jnp.mean(values * values, axis=-1, keepdims=True) + epsilon)
    return values * factor, factor


def total_of(refs):
    total = refs[0][...].astype(f32)
    for ref in refs[1:]:
        total = total + ref[...].astype(f32)
    return total


def row_stage(body, rows_in, tables, images, rows_out, sum_count, name):
    count, width = rows_in[0][0].shape
    image_count = tables[0].shape[0]
    tile = next(size for size in (96, 48, 16) if count % size == 0)
    flat = [array for group in rows_in for array in group]
    lengths = [len(group) for group in rows_in]

    def kernel(*refs):
        refs = list(refs)
        groups = []
        for length in lengths:
            groups.append(refs[:length])
            refs = refs[length:]
        table_refs, refs = refs[: len(tables)], refs[len(tables) :]
        images_ref, refs = refs[0], refs[1:]
        outs, sums = refs[: len(rows_out)], refs[len(rows_out) :]
        images_here = images_ref[...]
        if sum_count:

            @pl.when(pl.program_id(0) == 0)
            def _():
                for ref in sums:
                    ref[...] = jnp.zeros_like(ref)

        def add(index, values):
            for image in range(image_count):
                part = jnp.where(images_here == image, values, 0.0)
                sums[index][image : image + 1, :] += jnp.sum(part, axis=0, keepdims=True)

        body(groups, table_refs, images_here, outs, add)

    row_spec = pl.BlockSpec((tile, width), lambda i: (i, 0))
    return pl.pallas_call(
        kernel,
        grid=(count // tile,),
        in_specs=[row_spec] * len(flat)
        + [pl.BlockSpec(table.shape, lambda i: (0, 0)) for table in tables]
        + [pl.BlockSpec((tile, 1), lambda i: (i, 0))],
        out_specs=[row_spec] * len(rows_out)
        + [pl.BlockSpec((image_count, width), lambda i: (0, 0))] * sum_count,
        out_shape=[jax.ShapeDtypeStruct((count, width), kind) for kind in rows_out]
        + [jax.ShapeDtypeStruct((image_count, width), f32)] * sum_count,
        compiler_params=pltpu.CompilerParams(vmem_limit_bytes=vmem_bytes),
        cost_estimate=cost_of(3e-6),
        name=name,
    )(*flat, *tables, images[:, None])


def normed_body(groups, tables, images, outs, add):
    (tokens,) = groups
    unit, _ = unit_of(total_of(tokens))
    outs[0][...] = (unit * pick(tables[0], images)).astype(bf16)


def hidden_body(groups, tables, images, outs, add):
    attn_parts, tokens = groups
    attn = total_of(attn_parts)
    unit, _ = unit_of(attn)
    hidden = total_of(tokens) + unit * pick(tables[0], images)
    outs[0][...] = attn
    outs[1][...] = hidden
    unit, _ = unit_of(hidden)
    outs[2][...] = (unit * pick(tables[1], images)).astype(bf16)


def output_body(groups, tables, images, outs, add):
    ffn_parts, hidden, cotangent = groups
    unit, factor = unit_of(total_of(ffn_parts))
    post = pick(tables[0], images)
    grad_out = total_of(cotangent)
    outs[0][...] = (total_of(hidden) + unit * post).astype(bf16)
    add(0, grad_out * unit)
    outs[1][...] = unit_back(grad_out * post, unit, factor).astype(bf16)


def middle_body(groups, tables, images, outs, add):
    grad_parts, hidden, attn, cotangent = groups
    grad_in = total_of(grad_parts)
    unit, factor = unit_of(total_of(hidden))
    add(0, grad_in * unit)
    grad_hidden = total_of(cotangent) + unit_back(
        grad_in * pick(tables[0], images), unit, factor
    )
    outs[0][...] = grad_hidden
    unit, factor = unit_of(total_of(attn))
    add(1, grad_hidden * unit)
    outs[1][...] = unit_back(grad_hidden * pick(tables[1], images), unit, factor).astype(bf16)


def input_body(groups, tables, images, outs, add):
    grad_parts, tokens, grad_hidden = groups
    grad_in = total_of(grad_parts)
    unit, factor = unit_of(total_of(tokens))
    add(0, grad_in * unit)
    outs[0][...] = total_of(grad_hidden) + unit_back(
        grad_in * pick(tables[0], images), unit, factor
    )


def weight_grad(bits, shards, lefts, rights, name, tiles=(256, lanes)):
    depth = lefts[0].shape[1]
    rows = sum(left.shape[0] for left in lefts)
    shard_rows = depth // shards
    spans = [right[1:] for right in rights]
    rights = [right[0] for right in rights]
    widths = [width for _, width in spans]
    tile = next(t for t in tiles if all(c % t == 0 for span in spans for c in span))
    starts = [sum(widths[:k]) // tile for k in range(len(widths) + 1)]
    ends = [len(lefts) + sum(len(pieces) for pieces in rights[:k]) for k in range(len(rights) + 1)]

    def kernel(bits_ref, *refs):
        left_refs = refs[: len(lefts)]
        kept_ref, sent_ref, turned_ref, total_ref = refs[ends[-1] :]
        step = pl.program_id(0)
        bit = bits_ref[0]

        @pl.when(step == 0)
        def _():
            left = jnp.concatenate([ref[...] for ref in left_refs], axis=0)
            turned_ref[...] = left.astype(f32).T.astype(bf16)

        for index in range(len(rights)):

            @pl.when((step >= starts[index]) & (step < starts[index + 1]))
            def _():
                own = refs[ends[index] : ends[index + 1]]
                right = jnp.concatenate([ref[...] for ref in own], axis=0)
                total_ref[...] = dot_nn(turned_ref[...], right)

        for place in range(shards // 2):
            kept = pl.multiple_of((2 * place + bit) * shard_rows, 8)
            sent = pl.multiple_of((2 * place + 1 - bit) * shard_rows, 8)
            kept_ref[place] = total_ref[pl.ds(kept, shard_rows), :].astype(bf16)
            sent_ref[place] = total_ref[pl.ds(sent, shard_rows), :].astype(bf16)

    def right_spec(index, count):
        first, last = starts[index], starts[index + 1] - starts[index] - 1
        base = spans[index][0] // tile
        return pl.BlockSpec((count, tile), lambda j, s: (0, base + jnp.clip(j - first, 0, last)))

    out = jax.ShapeDtypeStruct((shards // 2, shard_rows, sum(widths)), bf16)
    out_spec = pl.BlockSpec((shards // 2, shard_rows, tile), lambda j, s: (0, 0, j))
    return pl.pallas_call(
        kernel,
        grid_spec=pltpu.PrefetchScalarGridSpec(
            num_scalar_prefetch=1,
            grid=(starts[-1],),
            in_specs=[pl.BlockSpec(left.shape, lambda j, s: (0, 0)) for left in lefts]
            + [
                right_spec(index, piece.shape[0])
                for index, pieces in enumerate(rights)
                for piece in pieces
            ],
            out_specs=[out_spec, out_spec],
            scratch_shapes=[pltpu.VMEM((depth, rows), bf16), pltpu.VMEM((depth, tile), f32)],
        ),
        out_shape=[out, out],
        compiler_params=pltpu.CompilerParams(vmem_limit_bytes=vmem_bytes),
        cost_estimate=pl.CostEstimate(
            flops=2 * rows * depth * sum(widths), bytes_accessed=2 * depth * sum(widths), transcendentals=0
        ),
        name=name,
    )(bits, *lefts, *[piece for pieces in rights for piece in pieces])


def add_and_split(bits, level, kept, moved):
    shards, rows, width = kept.shape

    def kernel(bits_ref, kept_stay, moved_stay, kept_go, moved_go, stay_ref, go_ref):
        stay_ref[...] = (kept_stay[...].astype(f32) + moved_stay[...].astype(f32)).astype(bf16)
        go_ref[...] = (kept_go[...].astype(f32) + moved_go[...].astype(f32)).astype(bf16)

    stay = pl.BlockSpec((1, rows, width), lambda j, s: (2 * j + s[level], 0, 0))
    go = pl.BlockSpec((1, rows, width), lambda j, s: (2 * j + 1 - s[level], 0, 0))
    put = pl.BlockSpec((1, rows, width), lambda j, s: (j, 0, 0))
    out = jax.ShapeDtypeStruct((shards // 2, rows, width), bf16)
    return pl.pallas_call(
        kernel,
        grid_spec=pltpu.PrefetchScalarGridSpec(
            num_scalar_prefetch=1,
            grid=(shards // 2,),
            in_specs=[stay, stay, go, go],
            out_specs=[put, put],
        ),
        out_shape=[out, out],
        compiler_params=pltpu.CompilerParams(vmem_limit_bytes=vmem_bytes),
        cost_estimate=cost_of(3e-6),
        name="add_and_split",
    )(bits, kept, moved, kept, moved)


class DpSum:
    def __init__(self, bits, halves):
        self.bits = bits
        self.kept, self.sent = halves
        self.level = 0
        self.levels = len(bits_of("dp"))

    def send(self):
        self.moved = partner(self.sent, "dp", self.level)

    def add(self, *earlier):
        moved = after(self.moved, *earlier) if earlier else self.moved
        self.level += 1
        if self.level < self.levels:
            self.kept, self.sent = add_and_split(self.bits, self.level, self.kept, moved)
            self.send()
        else:
            self.total = self.kept[0].astype(f32) + moved[0].astype(f32)
            self.sent = self.total


def tensor_moved(array, step):
    count = lax.axis_size("tensor")
    return lax.ppermute(array, "tensor", [((i + step) % count, i) for i in range(count)])


def gather_blocks(block):
    return [block] + [tensor_moved(block, step) for step in range(1, lax.axis_size("tensor"))]


def after(value, *earlier):
    return lax.optimization_barrier((value, earlier))[0]


def bits_of(axis):
    return range(lax.axis_size(axis).bit_length() - 1)


def partner(array, axis, bit):
    return lax.ppermute(array, axis, [(i, i ^ (1 << bit)) for i in range(lax.axis_size(axis))])


def gather_over_dp(array):
    array = array[None]
    for bit in reversed(bits_of("dp")):
        array = jnp.concatenate([array, partner(array, "dp", bit)], axis=0)
    return array


def sum_over(array, axis):
    for bit in reversed(bits_of(axis)):
        array = array + partner(array, axis, bit)
    return array


def rope_tables(positions):
    lane = jnp.arange(lanes, dtype=jnp.int32)
    place = lane % 32
    freqs = jnp.power(theta, -((place % 16).astype(f32) / 16))
    spot = jnp.where(place[None, :] < 16, positions[0][:, None], positions[1][:, None])
    angles = spot.astype(f32) * freqs[None, :]
    sign = jnp.where(lane % half_lanes < 32, -1.0, 1.0)
    return (jnp.cos(angles), jnp.sin(angles) * sign[None, :])


def feature_lanes(images, valid, count, ones_at):
    lane = (jnp.arange(lanes, dtype=jnp.int32) % half_lanes)[None, :]
    outside = (lane < count) & ((lane != images[:, None]) | ~valid[:, None])
    ones = (lane >= ones_at) & (lane < ones_at + 3)
    return jnp.where(outside, -penalty, jnp.where(ones, 1.0, 0.0)).astype(bf16)


def pad_columns(values, width):
    return jnp.pad(values, ((0, 0), (0, width - values.shape[1])))


def pad_rows(values, height):
    return jnp.pad(values, ((0, height - values.shape[0]), (0, 0)))


def on_device(
    tokens,
    timestep,
    caption,
    caption_mask,
    image_lengths,
    patch_pos,
    ada_weight,
    ada_bias,
    attention_norm,
    attention_post,
    feedforward_norm,
    feedforward_post,
    query_weight,
    key_weight,
    value_weight,
    query_gain,
    key_gain,
    cross_keys,
    cross_values,
    cross_gain,
    cross_gate,
    output_weight,
    gate_weight,
    up_weight,
    down_weight,
    cotangent,
):
    local_rows, model_width = tokens.shape
    tensor_count = lax.axis_size("tensor")
    tensor_place = lax.axis_index("tensor")
    group_tokens = local_rows * tensor_count
    image_count, cap_len, cap_width = caption.shape
    local_heads, head_size = query_gain.shape
    head_columns = local_heads * head_size
    pairs = (local_heads + 1) // 2
    pair_columns = pairs * lanes
    cap_total = image_count * cap_len

    token_blocks = gather_blocks(tokens)

    places = (
        jnp.arange(group_tokens, dtype=jnp.int32) + tensor_place * local_rows
    ) % group_tokens
    image_all = jnp.zeros((group_tokens,), jnp.int32)
    end = jnp.zeros((), jnp.int32)
    for image in range(image_count - 1):
        end = end + image_lengths[image]
        image_all = image_all + (places >= end).astype(jnp.int32)
    image_own = image_all[:local_rows]
    positions = jnp.roll(patch_pos, -tensor_place * local_rows, axis=1)
    cosine, sine = rope_tables(positions)
    lane = (jnp.arange(lanes, dtype=jnp.int32) % half_lanes)[None, :]
    query_features = (lane == image_all[:, None]).astype(bf16)
    everywhere = jnp.ones((group_tokens,), jnp.bool_)
    key_features = feature_lanes(image_all, everywhere, image_count, 3)
    cap_features = feature_lanes(
        jnp.arange(cap_total, dtype=jnp.int32) // cap_len,
        caption_mask.reshape(-1) > 0,
        image_count,
        6,
    )
    block_total = -(-group_tokens // query_block)
    block_place = jnp.arange(group_tokens, dtype=jnp.int32) // query_block
    hit = (block_place[None, None, :] == jnp.arange(block_total)[:, None, None]) & (
        image_all[None, None, :] == jnp.arange(image_count)[None, :, None]
    )
    present = jnp.max(hit.astype(jnp.int32), axis=2).reshape(-1)
    head_gate = jnp.tanh(cross_gate)
    gain_rows = jnp.stack(
        [
            query_gain.reshape(-1),
            key_gain.reshape(-1),
            cross_gain.reshape(-1),
            jnp.repeat(head_gate, head_size),
        ]
    )
    gains = (
        jnp.pad(gain_rows, ((0, 4), (0, pair_columns - head_columns)))
        .reshape(8, pairs, lanes)
        .transpose(1, 0, 2)
    )
    tables = (cosine, sine, query_features, key_features, cap_features)

    time_float = timestep.astype(f32)
    silu_time = (time_float * sigmoid_of(time_float)).astype(bf16)
    mod_part = dot_nn(silu_time, ada_weight) + ada_bias
    mod_stack = jnp.roll(jnp.stack(gather_blocks(mod_part)), tensor_place, axis=0)
    modulation = mod_stack.transpose(1, 0, 2).reshape(image_count, 4 * model_width)
    scale_attn = 1.0 + modulation[:, :model_width]
    gate_attn = jnp.tanh(modulation[:, model_width : 2 * model_width])
    scale_ffn = 1.0 + modulation[:, 2 * model_width : 3 * model_width]
    gate_ffn = jnp.tanh(modulation[:, 3 * model_width :])
    norm_attn = scale_attn * attention_norm
    post_attn = gate_attn * attention_post
    norm_ffn = scale_ffn * feedforward_norm
    post_ffn = gate_ffn * feedforward_post

    cap_flat = caption.reshape(cap_total, cap_width)
    ck_raw = pad_columns(dot_nn(cap_flat, cross_keys), pair_columns)
    cap_values = pad_columns(dot_nn(cap_flat, cross_values).astype(bf16), pair_columns)

    normed, q_raw, k_raw, values = [], [], [], []
    for index, block in enumerate(token_blocks):
        images = image_all[index * local_rows : (index + 1) * local_rows]
        (rows,) = row_stage(normed_body, [[block]], [norm_attn], images, [bf16], 0, "normed_in")
        normed.append(rows)
        q_raw.append(pad_columns(dot_nn(rows, query_weight), pair_columns))
        k_raw.append(pad_columns(dot_nn(rows, key_weight), pair_columns))
        values.append(pad_columns(dot_nn(rows, value_weight).astype(bf16), pair_columns))

    mixed, *kept = attention_forward(
        present, q_raw, k_raw, values, ck_raw, cap_values, gains, tables, image_count
    )
    chunks = 2 if local_rows % 32 == 0 else 1
    chunk_rows = local_rows // chunks
    steps = range(1, tensor_count)
    cuts = range(chunks)
    bits = jnp.stack([(lax.axis_index("dp") >> bit) & 1 for bit in bits_of("dp")]).astype(jnp.int32)
    shards = lax.axis_size("dp")

    def piece_of(array, step, cut):
        start = step * local_rows + cut * chunk_rows
        return array[start : start + chunk_rows]

    def returned(parts):
        return [tensor_moved(part, -step) for step, part in enumerate(parts, 1)]

    def moved_in(array):
        return [tensor_moved(array, step) for step in steps]

    output_rows = pad_rows(output_weight, pair_columns)
    tokens_cut = [piece_of(tokens, 0, cut) for cut in cuts]
    cotangent_cut = [piece_of(cotangent, 0, cut) for cut in cuts]
    images_cut = [piece_of(image_own, 0, cut) for cut in cuts]

    attn_moved = [
        returned([dot_nn(piece_of(mixed, step, cut), output_rows).astype(bf16) for step in steps])
        for cut in cuts
    ]
    attn_kept = [dot_nn(piece_of(mixed, 0, cut), output_rows) for cut in cuts]
    attn, hidden, ffn_in = [], [], []
    for cut in cuts:
        attn_rows, hidden_rows, rows = row_stage(
            hidden_body,
            [[attn_kept[cut]] + attn_moved[cut], [tokens_cut[cut]]],
            [post_attn, norm_ffn],
            images_cut[cut],
            [f32, f32, bf16],
            0,
            "hidden",
        )
        attn.append(attn_rows)
        hidden.append(hidden_rows)
        ffn_in.append([rows] + moved_in(rows))

    def feed_forward(rows):
        gate = dot_nn(rows, gate_weight)
        up = dot_nn(rows, up_weight)
        inner = (gate * sigmoid_of(gate) * up).astype(bf16)
        return gate.astype(bf16), up.astype(bf16), inner, dot_nn(inner, down_weight)

    latest = ()
    forward, ffn_moved = [], []
    for cut in cuts:
        pieces = []
        for step in range(tensor_count):
            ffn_in[cut][step] = after(ffn_in[cut][step], *latest)
            gate, up, inner, part = feed_forward(ffn_in[cut][step])
            part = part if step == 0 else part.astype(bf16)
            pieces.append((gate, up, inner, part))
            latest = (part,)
        forward.append(pieces)
        ffn_moved.append(returned([piece[3] for piece in pieces[1:]]))

    layer_out, sums_ffn_post, grad_ffn = [], [], []
    for cut in cuts:
        out_rows, rows, sums = row_stage(
            output_body,
            [[forward[cut][0][3]] + ffn_moved[cut], [hidden[cut]], [cotangent_cut[cut]]],
            [post_ffn],
            images_cut[cut],
            [bf16, bf16],
            1,
            "layer_out",
        )
        layer_out.append(out_rows)
        sums_ffn_post.append(sums)
        grad_ffn.append([rows] + moved_in(rows))

    def feed_back(rows, kept):
        gate, up = kept[0].astype(f32), kept[1].astype(f32)
        grad_inner = dot_nt(rows, down_weight)
        sig = sigmoid_of(gate)
        grad_up = (grad_inner * (gate * sig)).astype(bf16)
        grad_gate = (grad_inner * up * sig * (1.0 + gate * (1.0 - sig))).astype(bf16)
        return grad_gate, grad_up, dot_nt(grad_gate, gate_weight) + dot_nt(grad_up, up_weight)

    latest = ()
    backward, grad_in_moved = [], []
    for cut in cuts:
        pieces = []
        for step in range(tensor_count):
            grad_ffn[cut][step] = after(grad_ffn[cut][step], *latest)
            grad_gate, grad_up, part = feed_back(grad_ffn[cut][step], forward[cut][step])
            part = part if step == 0 else part.astype(bf16)
            pieces.append((grad_gate, grad_up, part))
            latest = (part,)
        backward.append(pieces)
        grad_in_moved.append(returned([piece[2] for piece in pieces[1:]]))

    def whole_right(pieces):
        return pieces, 0, pieces[0].shape[1]

    def group_pieces(of):
        return [of(cut, step) for step in range(tensor_count) for cut in cuts]

    grad_hidden, sums_ffn_norm, sums_attn_post, grad_attn = [], [], [], []
    for cut in cuts:
        if cut == chunks - 1:
            lefts = group_pieces(lambda cut, step: grad_ffn[cut][step])
            lefts[0] = after(lefts[0], latest)
            down_sum = DpSum(
                bits,
                weight_grad(
                    bits,
                    shards,
                    lefts,
                    [whole_right(group_pieces(lambda cut, step: forward[cut][step][2]))],
                    "down_grad",
                ),
            )
            down_sum.send()
            grad_in_moved[cut] = [after(moved, down_sum.sent) for moved in grad_in_moved[cut]]
        hidden_grad, rows, norm_sums, post_sums = row_stage(
            middle_body,
            [
                [backward[cut][0][2]] + grad_in_moved[cut],
                [hidden[cut]],
                [attn[cut]],
                [cotangent_cut[cut]],
            ],
            [norm_ffn, post_attn],
            images_cut[cut],
            [f32, bf16],
            2,
            "hidden_grad",
        )
        grad_hidden.append(hidden_grad)
        sums_ffn_norm.append(norm_sums)
        sums_attn_post.append(post_sums)
        grad_attn.append([rows] + moved_in(rows))
        latest = rows
    lefts = group_pieces(lambda cut, step: ffn_in[cut][step])
    lefts[0] = after(lefts[0], latest)
    gate_up_sum = DpSum(
        bits,
        weight_grad(
            bits,
            shards,
            lefts,
            [
                whole_right(group_pieces(lambda cut, step: backward[cut][step][k]))
                for k in (0, 1)
            ],
            "gate_up_grad",
        ),
    )
    gate_up_sum.send()
    down_sum.add(gate_up_sum.sent)

    grad_attn = group_pieces(lambda cut, step: grad_attn[cut][step])
    grad_attn[-1] = after(grad_attn[-1], down_sum.sent)
    grad_mixed = jnp.concatenate(
        [dot_nt(piece, output_rows).astype(bf16) for piece in grad_attn], axis=0
    )
    output_sum = DpSum(
        bits,
        weight_grad(
            bits,
            shards,
            grad_attn,
            [whole_right([mixed])],
            "output_grad",
        ),
    )
    output_sum.send()
    gate_up_sum.add(output_sum.sent)
    grad_mixed = after(grad_mixed, gate_up_sum.sent)

    def projection_sum(parts, start, width):
        rights = [([part], start, width) for part in parts[:3]]
        return DpSum(bits, weight_grad(bits, shards, normed, rights, "projection_grad"))

    def caption_sum(parts, start, width):
        rights = [([part], start, width) for part in parts[3:5]]
        return DpSum(bits, weight_grad(bits, shards, [cap_flat], rights, "caption_grad"))

    parts = None
    first = 0
    call_sizes = [2] * (pairs // 2) if pairs % 2 == 0 and pairs > 2 else [1] * pairs
    for call, size in enumerate(call_sizes):
        parts = attention_backward(
            present,
            first,
            size,
            parts,
            q_raw,
            k_raw,
            values,
            ck_raw,
            cap_values,
            gains,
            tables,
            kept,
            grad_mixed,
            image_count,
        )
        first += size
        if call == 0:
            down_sum.add(parts[0])
            output_sum.add(parts[0])
            grad_mixed = after(grad_mixed, down_sum.sent, output_sum.sent)
        if call == len(call_sizes) - 2:
            early = first * lanes
            query_early = projection_sum(parts, 0, early)
            query_early.send()
            caption_early = caption_sum(parts, 0, early)
            caption_early.send()
            gate_up_sum.add(parts[0])
            down_sum.add(gate_up_sum.sent)
            query_early.add(down_sum.sent, caption_early.sent)
            output_sum.add(query_early.sent)
            caption_early.add(output_sum.sent)
            parts = [parts[0]] + list(after(tuple(parts[1:]), caption_early.sent))
            grad_mixed = after(grad_mixed, caption_early.sent)
    grad_q, grad_k, grad_v, grad_ck, grad_cv, stats = parts
    stats = stats.transpose(1, 0, 2).reshape(8, pair_columns)[:, :head_columns]
    stats = stats.reshape(8, local_heads, head_size)
    grad_head_gate = jnp.sum(stats[3], axis=1) * (1.0 - head_gate * head_gate)

    weights_in = [
        pad_columns(weight, pair_columns) for weight in (query_weight, key_weight, value_weight)
    ]

    def input_part(step, cut):
        return sum(
            dot_nt(piece_of(part, step, cut), weight)
            for part, weight in zip((grad_q, grad_k, grad_v), weights_in)
        )

    sent = [[input_part(step, cut).astype(bf16) for step in steps] for cut in cuts]
    grad_normed_moved = [returned(part) for part in sent]
    late = pair_columns - early
    query_late = projection_sum([after(grad_q, sent), grad_k, grad_v], early, late)
    query_late.send()
    grad_ck = after(grad_ck, query_late.sent)
    caption_late = caption_sum([grad_q, grad_k, grad_v, grad_ck, grad_cv], early, late)
    caption_late.send()
    query_late.add(caption_late.sent)
    gate_up_sum.add(query_late.sent)
    caption_late.add(gate_up_sum.sent)
    output_sum.add(caption_late.sent)
    query_early.add(output_sum.sent)
    grad_q = after(grad_q, query_early.sent)
    grad_normed_kept = [input_part(0, cut) for cut in cuts]
    sums_attn_norm, tokens_grad = [], []
    for cut in cuts:
        rows, sums = row_stage(
            input_body,
            [[grad_normed_kept[cut]] + grad_normed_moved[cut], [tokens_cut[cut]], [grad_hidden[cut]]],
            [norm_attn],
            images_cut[cut],
            [f32],
            1,
            "tokens_grad",
        )
        tokens_grad.append(rows)
        sums_attn_norm.append(sums)
    sums_all = (
        down_sum,
        gate_up_sum,
        output_sum,
        query_early,
        caption_early,
        query_late,
        caption_late,
    )
    for level in range(query_late.levels + 1):
        for running in sums_all:
            if running.level < level:
                running.add()

    def both_totals(first_sum, second_sum, index):
        return jnp.concatenate(
            [
                first_sum.total[:, index * early : (index + 1) * early],
                second_sum.total[:, index * late : (index + 1) * late],
            ],
            axis=1,
        )[:, :head_columns]

    sums = jnp.concatenate(
        [sum(part) for part in (sums_attn_norm, sums_attn_post, sums_ffn_norm, sums_ffn_post)],
        axis=1,
    )
    sums = sum_over(sums, "tensor")
    widths = [sums[:, k * model_width : (k + 1) * model_width] for k in range(4)]
    norm_parts = jnp.concatenate(
        [
            jnp.sum(part * factor, axis=0)
            for part, factor in zip(widths, (scale_attn, gate_attn, scale_ffn, gate_ffn))
        ]
    )
    grad_mod = jnp.concatenate(
        [
            widths[0] * attention_norm,
            widths[1] * attention_post * (1.0 - gate_attn * gate_attn),
            widths[2] * feedforward_norm,
            widths[3] * feedforward_post * (1.0 - gate_ffn * gate_ffn),
        ],
        axis=1,
    )
    mod_columns = ada_weight.shape[1]
    grad_mod_own = lax.dynamic_slice_in_dim(
        grad_mod, tensor_place * mod_columns, mod_columns, axis=1
    )
    dp_count = lax.axis_size("dp")
    ada_width = silu_time.shape[1]
    ada_rows = ada_width // dp_count
    gathered = gather_over_dp(
        jnp.concatenate([grad_mod_own.astype(bf16), silu_time], axis=1).reshape(-1, lanes)
    ).reshape(dp_count * image_count, mod_columns + ada_width)
    time_own = lax.dynamic_slice_in_dim(
        gathered, mod_columns + lax.axis_index("dp") * ada_rows, ada_rows, axis=1
    )
    ada_grad = dot_tn(time_own, gathered[:, :mod_columns])
    small = jnp.concatenate(
        [
            norm_parts,
            jnp.sum(grad_mod_own, axis=0),
            stats[:3].reshape(-1),
            jnp.pad(grad_head_gate, (0, -local_heads % lanes)),
        ]
    )
    length = small.shape[0]
    small = sum_over(jnp.pad(small, (0, -length % 1024)).reshape(-1, lanes), "dp").reshape(-1)
    norm_sums = small[: 4 * model_width].reshape(4, model_width)
    bias_own = small[4 * model_width : 4 * model_width + mod_columns]
    start = 4 * model_width + mod_columns
    gain_sums = small[start : start + 3 * head_columns].reshape(3, local_heads, head_size)
    start = start + 3 * head_columns
    gate_own = small[start : start + local_heads]
    hidden_columns = gate_weight.shape[1]
    return (
        jnp.concatenate(layer_out, axis=0),
        jnp.concatenate(tokens_grad, axis=0),
        ada_grad,
        bias_own,
        norm_sums[0],
        norm_sums[1],
        norm_sums[2],
        norm_sums[3],
        both_totals(query_early, query_late, 0),
        both_totals(query_early, query_late, 1),
        both_totals(query_early, query_late, 2),
        gain_sums[0],
        gain_sums[1],
        both_totals(caption_early, caption_late, 0),
        both_totals(caption_early, caption_late, 1),
        gain_sums[2],
        gate_own,
        output_sum.total.T[:head_columns],
        gate_up_sum.total[:, :hidden_columns],
        gate_up_sum.total[:, hidden_columns:],
        down_sum.total.T,
    )


def solution(mesh):
    placed = (
        P(("dp", "tensor"), None),
        P("dp", None),
        P("dp", None, None),
        P("dp", None),
        P("dp"),
        P(None, "dp"),
        P(None, "tensor"),
        P("tensor"),
        P(),
        P(),
        P(),
        P(),
        P(None, "tensor"),
        P(None, "tensor"),
        P(None, "tensor"),
        P("tensor", None),
        P("tensor", None),
        P(None, "tensor"),
        P(None, "tensor"),
        P("tensor", None),
        P("tensor"),
        P("tensor", None),
        P(None, "tensor"),
        P(None, "tensor"),
        P("tensor", None),
        P(("dp", "tensor"), None),
    )
    return jax.shard_map(
        on_device,
        mesh=mesh,
        in_specs=placed,
        out_specs=(
            P(("dp", "tensor"), None),
            P(("dp", "tensor"), None),
            P("dp", "tensor"),
            P("tensor"),
            P(),
            P(),
            P(),
            P(),
            P("dp", "tensor"),
            P("dp", "tensor"),
            P("dp", "tensor"),
            P("tensor", None),
            P("tensor", None),
            P("dp", "tensor"),
            P("dp", "tensor"),
            P("tensor", None),
            P("tensor"),
            P("tensor", "dp"),
            P("dp", "tensor"),
            P("dp", "tensor"),
            P("tensor", "dp"),
        ),
        check_vma=False,
    )
```

```python
import math

import jax
import jax.numpy as jnp
from jax import lax
from jax.experimental import pallas as pl
from jax.experimental.pallas import tpu as pltpu
from jax.sharding import PartitionSpec as P

epsilon = 1e-05
penalty = 1024.0
theta = 10000.0
lanes = 128
half_lanes = 64
query_block = 384
bf16 = jnp.bfloat16
f32 = jnp.float32
vmem_bytes = 60 * 1024 * 1024


def sigmoid_of(values):
    return 1.0 / (1.0 + jnp.exp(-values))


def unit_rows(values):
    factor = lax.rsqrt(jnp.mean(values * values, axis=-1, keepdims=True) + epsilon)
    return (values * factor, factor)


def unit_back(gradient, normed, factor):
    return factor * (gradient - normed * jnp.mean(gradient * normed, axis=-1, keepdims=True))


def dot_nn(left, right):
    return lax.dot_general(left, right, (((1,), (0,)), ((), ())), preferred_element_type=f32)


def dot_nt(left, right):
    return lax.dot_general(left, right, (((1,), (1,)), ((), ())), preferred_element_type=f32)


def dot_tn(left, right):
    return lax.dot_general(left, right, (((0,), (0,)), ((), ())), preferred_element_type=f32)


def lane_index(rows):
    return lax.broadcasted_iota(jnp.int32, (rows, lanes), 1)


def halves_matrix(crossed):
    row = lax.broadcasted_iota(jnp.int32, (lanes, lanes), 0) // half_lanes
    col = lax.broadcasted_iota(jnp.int32, (lanes, lanes), 1) // half_lanes
    same = (row != col) if crossed else (row == col)
    return jnp.where(same, 1.0, 0.0).astype(bf16)


def half_sums(values, matrix):
    high = values.astype(bf16)
    rest = (values - high.astype(f32)).astype(bf16)
    return dot_nn(high, matrix) + dot_nn(rest, matrix)


def head_unit(values, matrix):
    factor = lax.rsqrt(half_sums(values * values, matrix) * (1.0 / half_lanes) + epsilon)
    return values * factor, factor


def head_unit_back(gradient, normed, factor, matrix):
    mean = half_sums(gradient * normed, matrix) * (1.0 / half_lanes)
    return factor * (gradient - normed * mean)


def swap_quarters(values):
    lane = lane_index(values.shape[0])
    ahead = pltpu.roll(values, lanes - 32, 1)
    behind = pltpu.roll(values, 32, 1)
    return jnp.where(lane % half_lanes < 32, ahead, behind)


def three_parts(values):
    first = values.astype(bf16)
    rest = values - first.astype(f32)
    second = rest.astype(bf16)
    third = (rest - second.astype(f32)).astype(bf16)
    return first, second, third


def put_lanes(target, place, head, values):
    lane = lane_index(target.shape[0])
    base = half_lanes * (1 - head) + place
    for offset, part in enumerate(three_parts(values)):
        target = jnp.where(lane == base + offset, part, target)
    return target


def both(head_zero, head_one):
    return jnp.where(lane_index(head_zero.shape[0]) < half_lanes, head_zero, head_one)


def pair_operands(values, features):
    return both(values, features), both(features, values)


def blocks_of(rows):
    starts = list(range(0, rows, query_block))
    return [(start, min(query_block, rows - start)) for start in starts]


def forward_kernel(block_count, image_count, present, *refs):
    q_refs = refs[:block_count]
    k_refs = refs[block_count : 2 * block_count]
    v_refs = refs[2 * block_count : 3 * block_count]
    (
        ck_ref,
        cv_ref,
        gain_ref,
        cos_ref,
        sin_ref,
        fq_ref,
        fk_ref,
        fc_ref,
        mixed_ref,
        so_ref,
        co_ref,
        qa_ref,
        ka_ref,
        ca_ref,
        va_ref,
        cva_ref,
        acc_ref,
    ) = refs[3 * block_count :]
    rows = cos_ref.shape[0]
    cap_rows = ck_ref.shape[0] // image_count
    same = halves_matrix(False)
    q_raw = jnp.concatenate([ref[...] for ref in q_refs], axis=0).astype(f32)
    k_raw = jnp.concatenate([ref[...] for ref in k_refs], axis=0).astype(f32)
    cosine = cos_ref[...]
    sine = sin_ref[...]
    q_gained = head_unit(q_raw, same)[0] * gain_ref[0, 0:1, :]
    q_turned = q_gained * cosine + swap_quarters(q_gained) * sine
    queries = (q_turned.astype(bf16).astype(f32) * (1.0 / math.sqrt(half_lanes))).astype(bf16)
    k_gained = head_unit(k_raw, same)[0] * gain_ref[0, 1:2, :]
    keys = (k_gained * cosine + swap_quarters(k_gained) * sine).astype(bf16)
    cap_keys = (head_unit(ck_ref[...].astype(f32), same)[0] * gain_ref[0, 2:3, :]).astype(bf16)
    values = jnp.concatenate([ref[...] for ref in v_refs], axis=0)
    cap_values = cv_ref[...]
    ones = jnp.ones_like(values)
    cap_ones = jnp.ones_like(cap_values)
    for head, (qa, ka, ca, va, cva) in enumerate(
        zip(
            pair_operands(queries, fq_ref[...]),
            pair_operands(keys, fk_ref[...]),
            pair_operands(cap_keys, fc_ref[...]),
            pair_operands(values, ones),
            pair_operands(cap_values, cap_ones),
        )
    ):
        span = slice(head * lanes, (head + 1) * lanes)
        qa_ref[:, span] = qa
        ka_ref[:, span] = ka
        ca_ref[:, span] = ca
        va_ref[:, span] = va
        cva_ref[:, span] = cva
    gate = gain_ref[0, 3:4, :]
    for index, (start, size) in enumerate(blocks_of(rows)):
        own = slice(start, start + size)
        self_parts = []
        for head in range(2):
            span = slice(head * lanes, (head + 1) * lanes)
            scores = dot_nt(qa_ref[own, span], ka_ref[:, span])
            self_parts.append(dot_nn(jnp.exp(scores).astype(bf16), va_ref[:, span]))
        first_image = pl.multiple_of(present[index * (image_count + 1) + image_count] * cap_rows, 16)
        for head in range(2):
            span = slice(head * lanes, (head + 1) * lanes)
            caps = pl.ds(first_image, cap_rows)
            scores = dot_nt(qa_ref[own, span], ca_ref[caps, span])
            acc_ref[0:size, span] = dot_nn(jnp.exp(scores).astype(bf16), cva_ref[caps, span])
        for image in range(image_count):

            @pl.when(present[index * (image_count + 1) + image] > 0)
            def _():
                caps = slice(image * cap_rows, (image + 1) * cap_rows)
                for head in range(2):
                    span = slice(head * lanes, (head + 1) * lanes)
                    scores = dot_nt(qa_ref[own, span], ca_ref[caps, span])
                    acc_ref[0:size, span] += dot_nn(
                        jnp.exp(scores).astype(bf16), cva_ref[caps, span]
                    )

        cross_parts = [acc_ref[0:size, 0:lanes], acc_ref[0:size, lanes:]]
        outs = []
        for parts in (self_parts, cross_parts):
            total = pltpu.roll(both(parts[1], parts[0]), half_lanes, 1)
            outs.append(both(parts[0], parts[1]) / total)
        so_ref[own, :] = outs[0].astype(bf16)
        co_ref[own, :] = outs[1].astype(bf16)
        mixed_ref[own, :] = (outs[0] + gate * outs[1]).astype(bf16)
        for head in range(2):
            span = slice(head * lanes, (head + 1) * lanes)
            qa = qa_ref[own, span]
            qa = put_lanes(qa, 3, head, -jnp.log(self_parts[head]))
            qa = put_lanes(qa, 6, head, -jnp.log(cross_parts[head]))
            qa_ref[own, span] = qa


def backward_kernel(block_count, image_count, present, *refs):
    q_refs = refs[:block_count]
    k_refs = refs[block_count : 2 * block_count]
    v_refs = refs[2 * block_count : 3 * block_count]
    (
        ck_ref,
        cv_ref,
        gain_ref,
        cos_ref,
        sin_ref,
        so_ref,
        co_ref,
        qa_ref,
        ka_ref,
        ca_ref,
        gm_ref,
        gq_ref,
        gk_ref,
        gv_ref,
        gck_ref,
        gcv_ref,
        stat_ref,
        ga_ref,
        va_ref,
        cva_ref,
        kt_ref,
        ct_ref,
        dq_ref,
        dk_ref,
        dv_ref,
        dck_ref,
        dcv_ref,
    ) = refs[3 * block_count :]
    rows = cos_ref.shape[0]
    cap_rows = ck_ref.shape[0] // image_count
    same = halves_matrix(False)
    crossed = halves_matrix(True)
    grads = gm_ref[...]
    grads_float = grads.astype(f32)
    cross_product = grads_float * co_ref[...].astype(f32)
    self_delta = half_sums(grads_float * so_ref[...].astype(f32), crossed)
    cross_delta = half_sums(cross_product, crossed)
    values = jnp.concatenate([ref[...] for ref in v_refs], axis=0)
    blank = jnp.zeros_like(grads)
    lane = lane_index(rows) % half_lanes
    self_ones = jnp.where(lane < 3, 1.0, 0.0).astype(bf16)
    lane_cap = lane_index(ck_ref.shape[0]) % half_lanes
    cross_ones = jnp.where((lane_cap >= 3) & (lane_cap < 6), 1.0, 0.0).astype(bf16)
    for head, (ga, va, cva) in enumerate(
        zip(
            pair_operands(grads, blank),
            pair_operands(values, self_ones),
            pair_operands(cv_ref[...], cross_ones),
        )
    ):
        span = slice(head * lanes, (head + 1) * lanes)
        ga = put_lanes(ga, 0, head, -self_delta)
        ga = put_lanes(ga, 3, head, -cross_delta)
        ga_ref[:, span] = ga
        va_ref[:, span] = va
        cva_ref[:, span] = cva
        kt_ref[span, :] = ka_ref[:, span].astype(f32).T.astype(bf16)
        ct_ref[span, :] = ca_ref[:, span].astype(f32).T.astype(bf16)
    dk_ref[...] = jnp.zeros_like(dk_ref)
    dv_ref[...] = jnp.zeros_like(dv_ref)
    dck_ref[...] = jnp.zeros_like(dck_ref)
    dcv_ref[...] = jnp.zeros_like(dcv_ref)
    for index, (start, size) in enumerate(blocks_of(rows)):
        own = slice(start, start + size)
        for head in range(2):
            span = slice(head * lanes, (head + 1) * lanes)
            top = head * half_lanes
            place = slice(head * lanes + top, head * lanes + top + half_lanes)
            qa = qa_ref[own, span]
            ga = ga_ref[own, span]
            probs = jnp.exp(dot_nt(ka_ref[:, span], qa))
            grad_scores = (probs * dot_nt(va_ref[:, span], ga)).astype(bf16)
            dv_ref[:, span] += dot_nn(probs.astype(bf16), ga)
            dk_ref[:, span] += dot_nn(grad_scores, qa)
            dq_ref[top : top + half_lanes, own] = dot_nn(kt_ref[place, :], grad_scores)
        def cross_part(caps):
            for head in range(2):
                span = slice(head * lanes, (head + 1) * lanes)
                top = head * half_lanes
                place = slice(head * lanes + top, head * lanes + top + half_lanes)
                gate = gain_ref[0, 3:4, top : top + 1]
                qa = qa_ref[own, span]
                ga = ga_ref[own, span]
                probs = jnp.exp(dot_nt(ca_ref[caps, span], qa))
                grad_scores = (probs * dot_nt(cva_ref[caps, span], ga)).astype(bf16)
                dcv_ref[caps, span] += dot_nn(probs.astype(bf16), ga)
                dck_ref[caps, span] += dot_nn(grad_scores, qa)
                dq_ref[top : top + half_lanes, own] += gate * dot_nn(
                    ct_ref[place, caps], grad_scores
                )

        base = index * (image_count + 1)
        for image in range(image_count):

            @pl.when((present[base + image] > 0) | (present[base + image_count] == image))
            def _():
                cross_part(slice(image * cap_rows, (image + 1) * cap_rows))

    cosine = cos_ref[...]
    sine = sin_ref[...]
    gate_row = gain_ref[0, 3:4, :]
    scale = 1.0 / math.sqrt(half_lanes)
    sums = []
    for refs_of, place, out_ref, grad in (
        (q_refs, 0, gq_ref, dq_ref[...].T * scale),
        (k_refs, 1, gk_ref, both(dk_ref[:, 0:lanes], dk_ref[:, lanes:])),
    ):
        raw = jnp.concatenate([ref[...] for ref in refs_of], axis=0).astype(f32)
        normed, factor = head_unit(raw, same)
        turned = grad * cosine - swap_quarters(grad) * sine
        sums.append(jnp.sum(turned * normed, axis=0, keepdims=True))
        gain = gain_ref[0, place : place + 1, :]
        out_ref[...] = head_unit_back(turned * gain, normed, factor, same).astype(bf16)
    gv_ref[...] = both(dv_ref[:, 0:lanes], dv_ref[:, lanes:]).astype(bf16)
    grad = both(dck_ref[:, 0:lanes], dck_ref[:, lanes:]) * gate_row
    normed, factor = head_unit(ck_ref[...].astype(f32), same)
    sums.append(jnp.sum(grad * normed, axis=0, keepdims=True))
    gck_ref[...] = head_unit_back(grad * gain_ref[0, 2:3, :], normed, factor, same).astype(bf16)
    gcv_ref[...] = (both(dcv_ref[:, 0:lanes], dcv_ref[:, lanes:]) * gate_row).astype(bf16)
    sums.append(jnp.sum(cross_product, axis=0, keepdims=True))
    stat_ref[0] = jnp.concatenate(sums + [jnp.zeros((4, lanes), f32)], axis=0)


def cost_of(seconds):
    return pl.CostEstimate(
        flops=int(1.0 * seconds * 1.1e15), bytes_accessed=int(1.0 * seconds * 3e12), transcendentals=0
    )


def columns_spec(rows, width):
    return pl.BlockSpec((rows, width), lambda pair, *_: (0, pair))


def whole_spec(rows):
    return pl.BlockSpec((rows, lanes), lambda pair, *_: (0, 0))


def gain_spec():
    return pl.BlockSpec((1, 8, lanes), lambda pair, *_: (pair, 0, 0))


def attention_forward(present, q_raw, k_raw, values, ck_raw, cap_values, gains, tables, images):
    cosine, sine, fq, fk, fc = tables
    count = len(q_raw)
    local = q_raw[0].shape[0]
    rows = local * count
    caps = ck_raw.shape[0]
    pairs = q_raw[0].shape[1] // lanes
    width = pairs * lanes
    grid = pltpu.PrefetchScalarGridSpec(
        num_scalar_prefetch=1,
        grid=(pairs,),
        in_specs=[columns_spec(local, lanes)] * (3 * count)
        + [columns_spec(caps, lanes)] * 2
        + [gain_spec()]
        + [whole_spec(rows)] * 4
        + [whole_spec(caps)],
        out_specs=[columns_spec(rows, lanes)] * 3
        + [columns_spec(rows, 2 * lanes)] * 2
        + [columns_spec(caps, 2 * lanes)],
        scratch_shapes=[
            pltpu.VMEM((rows, 2 * lanes), bf16),
            pltpu.VMEM((caps, 2 * lanes), bf16),
            pltpu.VMEM((query_block, 2 * lanes), f32),
        ],
    )
    return pl.pallas_call(
        lambda *refs: forward_kernel(count, images, *refs),
        grid_spec=grid,
        out_shape=[jax.ShapeDtypeStruct((rows, width), bf16)] * 3
        + [jax.ShapeDtypeStruct((rows, 2 * width), bf16)] * 2
        + [jax.ShapeDtypeStruct((caps, 2 * width), bf16)],
        compiler_params=pltpu.CompilerParams(vmem_limit_bytes=vmem_bytes),
        cost_estimate=cost_of(44e-6),
        name="attention_forward",
    )(present, *q_raw, *k_raw, *values, ck_raw, cap_values, gains, cosine, sine, fq, fk, fc)


def attention_backward(
    present,
    first,
    calls_pairs,
    earlier,
    q_raw,
    k_raw,
    values,
    ck_raw,
    cap_values,
    gains,
    tables,
    kept,
    grad_mixed,
    images,
    seconds,
):
    cosine, sine = tables[:2]
    self_out, cross_out, qa, ka, ca = kept
    count = len(q_raw)
    local = q_raw[0].shape[0]
    rows = local * count
    caps = ck_raw.shape[0]
    pairs = q_raw[0].shape[1] // lanes
    width = pairs * lanes

    def columns(rows, width):
        return pl.BlockSpec((rows, width), lambda pair, *_: (0, first + pair))

    own_gains = pl.BlockSpec((1, 8, lanes), lambda pair, *_: (first + pair, 0, 0))
    inputs = [
        *q_raw,
        *k_raw,
        *values,
        ck_raw,
        cap_values,
        gains,
        cosine,
        sine,
        self_out,
        cross_out,
        qa,
        ka,
        ca,
        grad_mixed,
    ]
    earlier = list(earlier or [])
    grid = pltpu.PrefetchScalarGridSpec(
        num_scalar_prefetch=1,
        grid=(calls_pairs,),
        in_specs=[columns(local, lanes)] * (3 * count)
        + [columns(caps, lanes)] * 2
        + [own_gains]
        + [whole_spec(rows)] * 2
        + [columns(rows, lanes)] * 2
        + [columns(rows, 2 * lanes)] * 2
        + [columns(caps, 2 * lanes)]
        + [columns(rows, lanes)]
        + [pl.BlockSpec(memory_space=pl.ANY)] * len(earlier),
        out_specs=[columns(rows, lanes)] * 3 + [columns(caps, lanes)] * 2 + [own_gains],
        scratch_shapes=[
            pltpu.VMEM((rows, 2 * lanes), bf16),
            pltpu.VMEM((rows, 2 * lanes), bf16),
            pltpu.VMEM((caps, 2 * lanes), bf16),
            pltpu.VMEM((2 * lanes, rows), bf16),
            pltpu.VMEM((2 * lanes, caps), bf16),
            pltpu.VMEM((lanes, rows), f32),
            pltpu.VMEM((rows, 2 * lanes), f32),
            pltpu.VMEM((rows, 2 * lanes), f32),
            pltpu.VMEM((caps, 2 * lanes), f32),
            pltpu.VMEM((caps, 2 * lanes), f32),
        ],
    )

    def kernel(present_ref, *refs):
        inside = len(inputs)
        backward_kernel(count, images, present_ref, *refs[:inside], *refs[inside + len(earlier) :])

    return pl.pallas_call(
        kernel,
        grid_spec=grid,
        out_shape=[jax.ShapeDtypeStruct((rows, width), bf16)] * 3
        + [jax.ShapeDtypeStruct((caps, width), bf16)] * 2
        + [jax.ShapeDtypeStruct((pairs, 8, lanes), f32)],
        input_output_aliases={1 + len(inputs) + k: k for k in range(len(earlier))},
        compiler_params=pltpu.CompilerParams(vmem_limit_bytes=vmem_bytes),
        cost_estimate=cost_of(seconds * calls_pairs),
        name="attention_backward",
    )(present, *inputs, *earlier)


def pick(table_ref, images):
    rows = table_ref[0:1, :]
    for image in range(1, table_ref.shape[0]):
        rows = jnp.where(images == image, table_ref[image : image + 1, :], rows)
    return rows


def unit_of(values):
    factor = lax.rsqrt(jnp.mean(values * values, axis=-1, keepdims=True) + epsilon)
    return values * factor, factor


def total_of(refs):
    total = refs[0][...].astype(f32)
    for ref in refs[1:]:
        total = total + ref[...].astype(f32)
    return total


def row_stage(body, rows_in, tables, images, rows_out, sum_count, name, seconds=3e-7):
    count, width = rows_in[0][0].shape
    image_count = tables[0].shape[0]
    tile = next(size for size in (96, 48, 16) if count % size == 0)
    flat = [array for group in rows_in for array in group]
    lengths = [len(group) for group in rows_in]

    def kernel(*refs):
        refs = list(refs)
        groups = []
        for length in lengths:
            groups.append(refs[:length])
            refs = refs[length:]
        table_refs, refs = refs[: len(tables)], refs[len(tables) :]
        images_ref, refs = refs[0], refs[1:]
        outs, sums = refs[: len(rows_out)], refs[len(rows_out) :]
        images_here = images_ref[...]
        if sum_count:

            @pl.when(pl.program_id(0) == 0)
            def _():
                for ref in sums:
                    ref[...] = jnp.zeros_like(ref)

        def add(index, values):
            for image in range(image_count):
                part = jnp.where(images_here == image, values, 0.0)
                sums[index][image : image + 1, :] += jnp.sum(part, axis=0, keepdims=True)

        body(groups, table_refs, images_here, outs, add)

    row_spec = pl.BlockSpec((tile, width), lambda i: (i, 0))
    return pl.pallas_call(
        kernel,
        grid=(count // tile,),
        in_specs=[row_spec] * len(flat)
        + [pl.BlockSpec(table.shape, lambda i: (0, 0)) for table in tables]
        + [pl.BlockSpec((tile, 1), lambda i: (i, 0))],
        out_specs=[row_spec] * len(rows_out)
        + [pl.BlockSpec((image_count, width), lambda i: (0, 0))] * sum_count,
        out_shape=[jax.ShapeDtypeStruct((count, width), kind) for kind in rows_out]
        + [jax.ShapeDtypeStruct((image_count, width), f32)] * sum_count,
        compiler_params=pltpu.CompilerParams(vmem_limit_bytes=vmem_bytes),
        cost_estimate=cost_of(seconds),
        name=name,
    )(*flat, *tables, images[:, None])


def normed_body(groups, tables, images, outs, add):
    (tokens,) = groups
    unit, _ = unit_of(total_of(tokens))
    outs[0][...] = (unit * pick(tables[0], images)).astype(bf16)


def hidden_body(groups, tables, images, outs, add):
    attn_parts, tokens = groups
    attn = total_of(attn_parts)
    unit, _ = unit_of(attn)
    hidden = total_of(tokens) + unit * pick(tables[0], images)
    outs[0][...] = attn
    outs[1][...] = hidden
    unit, _ = unit_of(hidden)
    outs[2][...] = (unit * pick(tables[1], images)).astype(bf16)


def output_body(groups, tables, images, outs, add):
    ffn_parts, hidden, cotangent = groups
    unit, factor = unit_of(total_of(ffn_parts))
    post = pick(tables[0], images)
    grad_out = total_of(cotangent)
    outs[0][...] = (total_of(hidden) + unit * post).astype(bf16)
    add(0, grad_out * unit)
    outs[1][...] = unit_back(grad_out * post, unit, factor).astype(bf16)


def middle_body(groups, tables, images, outs, add):
    grad_parts, hidden, attn, cotangent = groups
    grad_in = total_of(grad_parts)
    unit, factor = unit_of(total_of(hidden))
    add(0, grad_in * unit)
    grad_hidden = total_of(cotangent) + unit_back(
        grad_in * pick(tables[0], images), unit, factor
    )
    outs[0][...] = grad_hidden
    unit, factor = unit_of(total_of(attn))
    add(1, grad_hidden * unit)
    outs[1][...] = unit_back(grad_hidden * pick(tables[1], images), unit, factor).astype(bf16)


def input_body(groups, tables, images, outs, add):
    grad_parts, tokens, grad_hidden = groups
    grad_in = total_of(grad_parts)
    unit, factor = unit_of(total_of(tokens))
    add(0, grad_in * unit)
    outs[0][...] = total_of(grad_hidden) + unit_back(
        grad_in * pick(tables[0], images), unit, factor
    )


def weight_grad(bits, shards, lefts, rights, name, tile, height=None, offset=0, into=None):
    depth = lefts[0].shape[1]
    rows = sum(left.shape[0] for left in lefts)
    shard_rows = depth // shards
    spans = [right[1:] for right in rights]
    rights = [right[0] for right in rights]
    widths = [width for _, width in spans]
    starts = [sum(widths[:k]) // tile for k in range(len(widths) + 1)]
    ends = [len(lefts) + sum(len(pieces) for pieces in rights[:k]) for k in range(len(rights) + 1)]
    height = height or starts[-1] * shard_rows
    into = list(into or [])

    def kernel(bits_ref, *refs):
        left_refs = refs[: len(lefts)]
        kept_ref, sent_ref, turned_ref, total_ref = refs[ends[-1] + len(into) :]
        step = pl.program_id(0)
        bit = bits_ref[0]

        @pl.when(step == 0)
        def _():
            left = jnp.concatenate([ref[...] for ref in left_refs], axis=0)
            turned_ref[...] = left.astype(f32).T.astype(bf16)

        for index in range(len(rights)):

            @pl.when((step >= starts[index]) & (step < starts[index + 1]))
            def _():
                own = refs[ends[index] : ends[index + 1]]
                right = jnp.concatenate([ref[...] for ref in own], axis=0)
                total_ref[...] = dot_nn(turned_ref[...], right)

        for place in range(shards // 2):
            kept = pl.multiple_of((2 * place + bit) * shard_rows, 8)
            sent = pl.multiple_of((2 * place + 1 - bit) * shard_rows, 8)
            kept_ref[place] = total_ref[pl.ds(kept, shard_rows), :].astype(bf16)
            sent_ref[place] = total_ref[pl.ds(sent, shard_rows), :].astype(bf16)

    def right_spec(index, count):
        first, last = starts[index], starts[index + 1] - starts[index] - 1
        base = spans[index][0] // tile
        return pl.BlockSpec((count, tile), lambda j, s: (0, base + jnp.clip(j - first, 0, last)))

    out = jax.ShapeDtypeStruct((shards // 2, height, tile), bf16)
    above = offset // shard_rows
    out_spec = pl.BlockSpec((shards // 2, shard_rows, tile), lambda j, s: (0, above + j, 0))
    aliased = 1 + ends[-1]
    return pl.pallas_call(
        kernel,
        grid_spec=pltpu.PrefetchScalarGridSpec(
            num_scalar_prefetch=1,
            grid=(starts[-1],),
            in_specs=[pl.BlockSpec(left.shape, lambda j, s: (0, 0)) for left in lefts]
            + [
                right_spec(index, piece.shape[0])
                for index, pieces in enumerate(rights)
                for piece in pieces
            ]
            + [pl.BlockSpec(memory_space=pl.ANY)] * len(into),
            out_specs=[out_spec, out_spec],
            scratch_shapes=[pltpu.VMEM((depth, rows), bf16), pltpu.VMEM((depth, tile), f32)],
        ),
        out_shape=[out, out],
        input_output_aliases={aliased + k: k for k in range(len(into))},
        compiler_params=pltpu.CompilerParams(vmem_limit_bytes=vmem_bytes),
        cost_estimate=cost_of(5.2e-6 * starts[-1] * tile / 768),
        name=name,
    )(bits, *lefts, *[piece for pieces in rights for piece in pieces], *into)


def add_and_split(bits, level, kept, moved):
    shards, rows, width = kept.shape

    def kernel(bits_ref, kept_stay, moved_stay, kept_go, moved_go, stay_ref, go_ref):
        stay_ref[...] = (kept_stay[...].astype(f32) + moved_stay[...].astype(f32)).astype(bf16)
        go_ref[...] = (kept_go[...].astype(f32) + moved_go[...].astype(f32)).astype(bf16)

    stay = pl.BlockSpec((1, rows, width), lambda j, s: (2 * j + s[level], 0, 0))
    go = pl.BlockSpec((1, rows, width), lambda j, s: (2 * j + 1 - s[level], 0, 0))
    put = pl.BlockSpec((1, rows, width), lambda j, s: (j, 0, 0))
    out = jax.ShapeDtypeStruct((shards // 2, rows, width), bf16)
    return pl.pallas_call(
        kernel,
        grid_spec=pltpu.PrefetchScalarGridSpec(
            num_scalar_prefetch=1,
            grid=(shards // 2,),
            in_specs=[stay, stay, go, go],
            out_specs=[put, put],
        ),
        out_shape=[out, out],
        compiler_params=pltpu.CompilerParams(vmem_limit_bytes=vmem_bytes),
        cost_estimate=cost_of(1e-8),
        name="add_and_split",
    )(bits, kept, moved, kept, moved)


class DpSum:
    def __init__(self, bits, halves):
        self.bits = bits
        self.kept, self.sent = halves
        self.level = 0
        self.levels = len(bits_of("dp"))

    def send(self):
        self.moved = partner(self.sent, "dp", self.level)

    def add(self, *earlier):
        moved = after(self.moved, *earlier) if earlier else self.moved
        self.level += 1
        if self.level < self.levels:
            self.kept, self.sent = add_and_split(self.bits, self.level, self.kept, moved)
            self.send()
        else:
            self.total = self.kept[0].astype(f32) + moved[0].astype(f32)
            self.sent = self.total

    def finish(self, *earlier):
        while self.level < self.levels:
            self.add(*earlier)

    def finish_before(self, value):
        while self.level < self.levels - 1:
            self.add()
        value, moved = lax.optimization_barrier((value, self.moved))
        self.moved = moved
        self.level += 1
        self.total = self.kept[0].astype(f32) + moved[0].astype(f32)
        return value

    def columns(self, offset, shard_rows, width):
        tile = self.total.shape[1]
        parts = [
            self.total[offset + k * shard_rows : offset + (k + 1) * shard_rows]
            for k in range(width // tile)
        ]
        return jnp.concatenate(parts, axis=1)


def assembled(early, late, layout, shapes, name):
    tile = early[0].shape[2]

    def kernel(early_kept, early_moved, late_kept, late_moved, *outs):
        refs = ((early_kept, early_moved), (late_kept, late_moved))
        for out, tiles in zip(outs, layout):
            rows, width = out.shape
            for column, (which, row) in enumerate(tiles):
                left = column * tile
                size = min(tile, width - left)
                if size > 0:
                    kept, moved = refs[which]
                    place = slice(row, row + rows)
                    out[:, left : left + size] = (
                        kept[0, place, 0:size].astype(f32) + moved[0, place, 0:size].astype(f32)
                    )

    return pl.pallas_call(
        kernel,
        out_shape=[jax.ShapeDtypeStruct(shape, f32) for shape in shapes],
        compiler_params=pltpu.CompilerParams(vmem_limit_bytes=vmem_bytes),
        cost_estimate=cost_of(1e-6),
        name=name,
    )(*early, *late)


def tensor_moved(array, step):
    count = lax.axis_size("tensor")
    return lax.ppermute(array, "tensor", [((i + step) % count, i) for i in range(count)])


def gather_blocks(block):
    return [block] + [tensor_moved(block, step) for step in range(1, lax.axis_size("tensor"))]


def after(value, *earlier):
    return lax.optimization_barrier((value, earlier))[0]


def bits_of(axis):
    return range(lax.axis_size(axis).bit_length() - 1)


def partner(array, axis, bit):
    return lax.ppermute(array, axis, [(i, i ^ (1 << bit)) for i in range(lax.axis_size(axis))])


def gather_and_sum(between, own, part):
    for bit in reversed(bits_of("dp")):
        moved = partner(jnp.concatenate([own, part], axis=0), "dp", bit)
        step = between.pop(0) if between else None
        if step:
            moved = step(moved)
        own = jnp.concatenate([own, moved[: own.shape[0]]], axis=0)
        part = part + moved[moved.shape[0] - part.shape[0] :]
    return own, part


def sum_over(array, axis):
    for bit in reversed(bits_of(axis)):
        array = array + partner(array, axis, bit)
    return array


def rope_tables(positions):
    lane = jnp.arange(lanes, dtype=jnp.int32)
    place = lane % 32
    freqs = jnp.power(theta, -((place % 16).astype(f32) / 16))
    spot = jnp.where(place[None, :] < 16, positions[0][:, None], positions[1][:, None])
    angles = spot.astype(f32) * freqs[None, :]
    sign = jnp.where(lane % half_lanes < 32, -1.0, 1.0)
    return (jnp.cos(angles), jnp.sin(angles) * sign[None, :])


def feature_lanes(images, valid, count, ones_at):
    lane = (jnp.arange(lanes, dtype=jnp.int32) % half_lanes)[None, :]
    outside = (lane < count) & ((lane != images[:, None]) | ~valid[:, None])
    ones = (lane >= ones_at) & (lane < ones_at + 3)
    return jnp.where(outside, -penalty, jnp.where(ones, 1.0, 0.0)).astype(bf16)


def pad_columns(values, width):
    return jnp.pad(values, ((0, 0), (0, width - values.shape[1])))


def pad_rows(values, height):
    return jnp.pad(values, ((0, height - values.shape[0]), (0, 0)))


def on_device(
    tokens,
    timestep,
    caption,
    caption_mask,
    image_lengths,
    patch_pos,
    ada_weight,
    ada_bias,
    attention_norm,
    attention_post,
    feedforward_norm,
    feedforward_post,
    query_weight,
    key_weight,
    value_weight,
    query_gain,
    key_gain,
    cross_keys,
    cross_values,
    cross_gain,
    cross_gate,
    output_weight,
    gate_weight,
    up_weight,
    down_weight,
    cotangent,
):
    local_rows, model_width = tokens.shape
    tensor_count = lax.axis_size("tensor")
    tensor_place = lax.axis_index("tensor")
    group_tokens = local_rows * tensor_count
    image_count, cap_len, cap_width = caption.shape
    local_heads, head_size = query_gain.shape
    head_columns = local_heads * head_size
    pairs = (local_heads + 1) // 2
    pair_columns = pairs * lanes
    cap_total = image_count * cap_len

    token_blocks = gather_blocks(tokens)

    places = (
        jnp.arange(group_tokens, dtype=jnp.int32) + tensor_place * local_rows
    ) % group_tokens
    image_all = jnp.zeros((group_tokens,), jnp.int32)
    end = jnp.zeros((), jnp.int32)
    for image in range(image_count - 1):
        end = end + image_lengths[image]
        image_all = image_all + (places >= end).astype(jnp.int32)
    image_own = image_all[:local_rows]
    positions = jnp.roll(patch_pos, -tensor_place * local_rows, axis=1)
    cosine, sine = rope_tables(positions)
    lane = (jnp.arange(lanes, dtype=jnp.int32) % half_lanes)[None, :]
    query_features = (lane == image_all[:, None]).astype(bf16)
    everywhere = jnp.ones((group_tokens,), jnp.bool_)
    key_features = feature_lanes(image_all, everywhere, image_count, 3)
    cap_features = feature_lanes(
        jnp.arange(cap_total, dtype=jnp.int32) // cap_len,
        caption_mask.reshape(-1) > 0,
        image_count,
        6,
    )
    block_total = -(-group_tokens // query_block)
    block_place = jnp.arange(group_tokens, dtype=jnp.int32) // query_block
    hit = (block_place[None, None, :] == jnp.arange(block_total)[:, None, None]) & (
        image_all[None, None, :] == jnp.arange(image_count)[None, :, None]
    )
    hit = jnp.max(hit.astype(jnp.int32), axis=2)
    first_image = jnp.argmax(hit, axis=1).astype(jnp.int32)[:, None]
    beyond = jnp.where(jnp.arange(image_count)[None, :] == first_image, 0, hit)
    present = jnp.concatenate([beyond, first_image], axis=1).reshape(-1)
    head_gate = jnp.tanh(cross_gate)
    gain_rows = jnp.stack(
        [
            query_gain.reshape(-1),
            key_gain.reshape(-1),
            cross_gain.reshape(-1),
            jnp.repeat(head_gate, head_size),
        ]
    )
    gains = (
        jnp.pad(gain_rows, ((0, 4), (0, pair_columns - head_columns)))
        .reshape(8, pairs, lanes)
        .transpose(1, 0, 2)
    )
    tables = (cosine, sine, query_features, key_features, cap_features)

    time_float = timestep.astype(f32)
    silu_time = (time_float * sigmoid_of(time_float)).astype(bf16)
    mod_part = dot_nn(silu_time, ada_weight) + ada_bias
    mod_stack = jnp.roll(jnp.stack(gather_blocks(mod_part)), tensor_place, axis=0)
    modulation = mod_stack.transpose(1, 0, 2).reshape(image_count, 4 * model_width)
    scale_attn = 1.0 + modulation[:, :model_width]
    gate_attn = jnp.tanh(modulation[:, model_width : 2 * model_width])
    scale_ffn = 1.0 + modulation[:, 2 * model_width : 3 * model_width]
    gate_ffn = jnp.tanh(modulation[:, 3 * model_width :])
    norm_attn = scale_attn * attention_norm
    post_attn = gate_attn * attention_post
    norm_ffn = scale_ffn * feedforward_norm
    post_ffn = gate_ffn * feedforward_post

    cap_flat = caption.reshape(cap_total, cap_width)
    ck_raw = pad_columns(dot_nn(cap_flat, cross_keys), pair_columns)
    cap_values = pad_columns(dot_nn(cap_flat, cross_values).astype(bf16), pair_columns)

    normed, q_raw, k_raw, values = [], [], [], []
    for index, block in enumerate(token_blocks):
        images = image_all[index * local_rows : (index + 1) * local_rows]
        (rows,) = row_stage(normed_body, [[block]], [norm_attn], images, [bf16], 0, "normed_in")
        normed.append(rows)
        q_raw.append(pad_columns(dot_nn(rows, query_weight), pair_columns))
        k_raw.append(pad_columns(dot_nn(rows, key_weight), pair_columns))
        values.append(pad_columns(dot_nn(rows, value_weight).astype(bf16), pair_columns))

    mixed, *kept = attention_forward(
        present, q_raw, k_raw, values, ck_raw, cap_values, gains, tables, image_count
    )
    chunks = 2 if local_rows % 32 == 0 else 1
    chunk_rows = local_rows // chunks
    steps = range(1, tensor_count)
    cuts = range(chunks)
    bits = jnp.stack([(lax.axis_index("dp") >> bit) & 1 for bit in bits_of("dp")]).astype(jnp.int32)
    shards = lax.axis_size("dp")
    hidden_columns = gate_weight.shape[1]
    wide_tile = 256 if hidden_columns % 256 == 0 else lanes

    def piece_of(array, step, cut):
        start = step * local_rows + cut * chunk_rows
        return array[start : start + chunk_rows]

    def returned(parts):
        return [tensor_moved(part, -step) for step, part in enumerate(parts, 1)]

    def moved_in(array):
        return [tensor_moved(array, step) for step in steps]

    output_rows = pad_rows(output_weight, pair_columns)
    output_rows = [output_rows] + [tensor_moved(output_rows, -step) for step in steps]
    tokens_cut = [piece_of(tokens, 0, cut) for cut in cuts]
    cotangent_cut = [piece_of(cotangent, 0, cut) for cut in cuts]
    images_cut = [piece_of(image_own, 0, cut) for cut in cuts]

    mixed_own = [
        [piece_of(mixed, 0, cut)] + returned([piece_of(mixed, step, cut) for step in steps])
        for cut in cuts
    ]
    attn, hidden, ffn_in = [], [], []
    for cut in cuts:
        attn_rows, hidden_rows, rows = row_stage(
            hidden_body,
            [
                [sum(dot_nn(part, rows) for part, rows in zip(mixed_own[cut], output_rows))],
                [tokens_cut[cut]],
            ],
            [post_attn, norm_ffn],
            images_cut[cut],
            [f32, f32, bf16],
            0,
            "hidden",
        )
        attn.append(attn_rows)
        hidden.append(hidden_rows)
        ffn_in.append([rows] + moved_in(rows))

    def feed_forward(rows):
        gate = dot_nn(rows, gate_weight)
        up = dot_nn(rows, up_weight)
        inner = (gate * sigmoid_of(gate) * up).astype(bf16)
        return gate.astype(bf16), up.astype(bf16), inner, dot_nn(inner, down_weight)

    latest = ()
    forward, ffn_moved = [], []
    for cut in cuts:
        pieces = []
        for step in range(tensor_count):
            ffn_in[cut][step] = after(ffn_in[cut][step], *latest)
            gate, up, inner, part = feed_forward(ffn_in[cut][step])
            part = part if step == 0 else part.astype(bf16)
            pieces.append((gate, up, inner, part))
            latest = (part,)
        forward.append(pieces)
        ffn_moved.append(returned([piece[3] for piece in pieces[1:]]))

    layer_out, sums_ffn_post, grad_ffn = [], [], []
    for cut in cuts:
        out_rows, rows, sums = row_stage(
            output_body,
            [[forward[cut][0][3]] + ffn_moved[cut], [hidden[cut]], [cotangent_cut[cut]]],
            [post_ffn],
            images_cut[cut],
            [bf16, bf16],
            1,
            "layer_out",
        )
        layer_out.append(out_rows)
        sums_ffn_post.append(sums)
        grad_ffn.append([rows] + moved_in(rows))

    def feed_back(rows, kept):
        gate, up = kept[0].astype(f32), kept[1].astype(f32)
        grad_inner = dot_nt(rows, down_weight)
        sig = sigmoid_of(gate)
        grad_up = (grad_inner * (gate * sig)).astype(bf16)
        grad_gate = (grad_inner * up * sig * (1.0 + gate * (1.0 - sig))).astype(bf16)
        return grad_gate, grad_up, dot_nt(grad_gate, gate_weight) + dot_nt(grad_up, up_weight)

    latest = ()
    backward, grad_in_moved = [], []
    for cut in cuts:
        pieces = []
        for step in range(tensor_count):
            grad_ffn[cut][step] = after(grad_ffn[cut][step], *latest)
            grad_gate, grad_up, part = feed_back(grad_ffn[cut][step], forward[cut][step])
            part = part if step == 0 else part.astype(bf16)
            pieces.append((grad_gate, grad_up, part))
            latest = (part,)
        backward.append(pieces)
        grad_in_moved.append(returned([piece[2] for piece in pieces[1:]]))

    def whole_right(pieces):
        return pieces, 0, pieces[0].shape[1]

    def group_pieces(of):
        return [of(cut, step) for step in range(tensor_count) for cut in cuts]

    grad_hidden, sums_ffn_norm, sums_attn_post, grad_attn = [], [], [], []
    grad_mixed_own, grad_mixed_moved = [], []
    for cut in cuts:
        if cut == chunks - 1:
            lefts = group_pieces(lambda cut, step: grad_ffn[cut][step])
            lefts[0] = after(
                lefts[0], latest, grad_mixed_own, [piece[2] for piece in backward[cut]]
            )
            down_sum = DpSum(
                bits,
                weight_grad(
                    bits,
                    shards,
                    lefts,
                    [whole_right(group_pieces(lambda cut, step: forward[cut][step][2]))],
                    "down_grad",
                    wide_tile,
                ),
            )
            down_sum.send()
            grad_in_moved[cut] = [after(moved, down_sum.sent) for moved in grad_in_moved[cut]]
        hidden_grad, rows, norm_sums, post_sums = row_stage(
            middle_body,
            [
                [backward[cut][0][2]] + grad_in_moved[cut],
                [hidden[cut]],
                [attn[cut]],
                [cotangent_cut[cut]],
            ],
            [norm_ffn, post_attn],
            images_cut[cut],
            [f32, bf16],
            2,
            "hidden_grad",
        )
        grad_hidden.append(hidden_grad)
        sums_ffn_norm.append(norm_sums)
        sums_attn_post.append(post_sums)
        grad_attn.append(rows)
        grad_mixed_own.append([dot_nt(rows, weight).astype(bf16) for weight in output_rows])
        grad_mixed_moved.append(
            [tensor_moved(part, step) for step, part in enumerate(grad_mixed_own[cut][1:], 1)]
        )
        latest = (rows, grad_mixed_own[cut])
    lefts = group_pieces(lambda cut, step: ffn_in[cut][step])

    def hidden_sum(index, *earlier):
        rights = [whole_right(group_pieces(lambda cut, step: backward[cut][step][index]))]
        own = [after(lefts[0], *earlier)] + lefts[1:]
        return DpSum(bits, weight_grad(bits, shards, own, rights, "gate_up_grad", wide_tile))

    gate_sum = hidden_sum(0, latest)
    gate_sum.send()
    up_sum = hidden_sum(1, gate_sum.sent, grad_mixed_moved)
    up_sum.send()
    down_sum.add(up_sum.sent)
    grad_mixed = jnp.concatenate(
        [grad_mixed_own[cut][0] for cut in cuts]
        + [grad_mixed_moved[cut][step - 1] for step in steps for cut in cuts],
        axis=0,
    )
    grad_mixed = after(grad_mixed, down_sum.sent)
    grad_attn = [
        [rows] + moved_in(after(rows, *[m for moved in grad_mixed_moved for m in moved]))
        for rows in grad_attn
    ]
    grad_attn = group_pieces(lambda cut, step: grad_attn[cut][step])

    width_rows, cap_rows = model_width // shards, cap_width // shards

    def side_by_side(parts, start, width, with_output, earlier, between=None):
        tile = 256 if start % 256 == 0 and width % 256 == 0 else lanes
        tiles = width // tile
        ahead = 2 * tiles * cap_rows
        projection_at = -(-ahead // width_rows) * width_rows
        output_at = projection_at + 3 * tiles * width_rows
        height = output_at + (pair_columns // tile * width_rows if with_output else 0)
        lefts = [after(normed[0], *earlier)] + list(normed[1:])
        halves = weight_grad(
            bits,
            shards,
            lefts,
            [([part], start, width) for part in parts[:3]],
            "projection_grad",
            tile,
            height,
            projection_at,
        )
        halves = weight_grad(
            bits,
            shards,
            [cap_flat],
            [([part], start, width) for part in parts[3:5]],
            "caption_grad",
            tile,
            height,
            0,
            halves,
        )
        if with_output:
            own = [after(grad_attn[0], between(halves))] + grad_attn[1:]
            halves = weight_grad(
                bits,
                shards,
                own,
                [whole_right([mixed])],
                "output_grad",
                tile,
                height,
                output_at,
                halves,
            )
        places = [projection_at + k * tiles * width_rows for k in range(3)]
        places += [k * tiles * cap_rows for k in range(2)] + [output_at]
        return DpSum(bits, halves), places

    parts = None
    first = 0
    call_sizes = [2] * (pairs // 2) if pairs % 2 == 0 and pairs > 2 else [1] * pairs
    for call, size in enumerate(call_sizes):
        parts = attention_backward(
            present,
            first,
            size,
            parts,
            q_raw,
            k_raw,
            values,
            ck_raw,
            cap_values,
            gains,
            tables,
            kept,
            grad_mixed,
            image_count,
            15e-6 if call == len(call_sizes) - 1 else 3e-6,
        )
        first += size
        if call == 0:
            gate_sum.add(parts[0])
            down_sum.add(gate_sum.sent)
            up_sum.add(down_sum.sent)
            grad_mixed = after(grad_mixed, up_sum.sent)
        if call == len(call_sizes) - 2:
            early = first * lanes
            gate_sum.add(parts[0])
            down_sum.add(gate_sum.sent)
            early_sum, early_places = side_by_side(
                parts,
                0,
                early,
                True,
                (down_sum.sent,),
                lambda halves: gate_sum.add(halves) or up_sum.add(gate_sum.sent) or up_sum.sent,
            )
            early_sum.send()
            early_sum.add()
            parts = [parts[0]] + list(after(tuple(parts[1:]), early_sum.sent))
            grad_mixed = after(grad_mixed, early_sum.sent)
    parts = gate_sum.finish_before(down_sum.finish_before(tuple(parts)))
    up_sum.add(parts[0])
    parts = after(parts, up_sum.sent)
    grad_q, grad_k, grad_v, grad_ck, grad_cv, stats = parts
    stats = stats.transpose(1, 0, 2).reshape(8, pair_columns)[:, :head_columns]
    stats = stats.reshape(8, local_heads, head_size)
    grad_head_gate = jnp.sum(stats[3], axis=1) * (1.0 - head_gate * head_gate)

    weights_in = [
        pad_columns(weight, pair_columns) for weight in (query_weight, key_weight, value_weight)
    ]

    def input_part(step, cut):
        return sum(
            dot_nt(piece_of(part, step, cut), weight)
            for part, weight in zip((grad_q, grad_k, grad_v), weights_in)
        )

    sent = [[input_part(step, cut).astype(bf16) for step in steps] for cut in cuts]
    grad_normed_moved = [returned(part) for part in sent]
    late = pair_columns - early
    late_sum, late_places = side_by_side(
        [grad_q, grad_k, grad_v, grad_ck, grad_cv], early, late, False, (sent,)
    )
    late_sum.send()
    up_sum.finish(late_sum.sent)
    early_sum.add(late_sum.sent, up_sum.sent)
    grad_q = after(grad_q, early_sum.sent)
    grad_normed_kept = [input_part(0, cut) for cut in cuts]
    late_sum.add(grad_normed_kept)
    grad_normed_moved = [
        [after(moved, late_sum.sent) for moved in part] for part in grad_normed_moved
    ]
    sums_attn_norm, tokens_grad = [], []
    for cut in cuts:
        if cut == chunks - 1 and cut > 0:
            early_sum.add(tokens_grad)
            grad_normed_moved[cut] = [
                after(moved, early_sum.sent) for moved in grad_normed_moved[cut]
            ]
        rows, sums = row_stage(
            input_body,
            [[grad_normed_kept[cut]] + grad_normed_moved[cut], [tokens_cut[cut]], [grad_hidden[cut]]],
            [norm_attn],
            images_cut[cut],
            [f32],
            1,
            "tokens_grad",
            12e-6,
        )
        tokens_grad.append(rows)
        sums_attn_norm.append(sums)
    def totals():
        tile = early_sum.kept.shape[2]
        layout = [
            [(0, early_places[k] + c * rows) for c in range(early // tile)]
            + [(1, late_places[k] + c * rows) for c in range(late // tile)]
            for k, rows in enumerate([width_rows] * 3 + [cap_rows] * 2)
        ]
        return assembled(
            (early_sum.kept, early_sum.moved),
            (late_sum.kept, late_sum.moved),
            layout,
            [(width_rows, head_columns)] * 3 + [(cap_rows, head_columns)] * 2,
            "assembled",
        )

    sums = jnp.concatenate(
        [sum(part) for part in (sums_attn_norm, sums_attn_post, sums_ffn_norm, sums_ffn_post)],
        axis=1,
    )
    late_sum.add(tokens_grad)
    sums = sum_over(after(sums, late_sum.sent), "tensor")
    between = [
        early_sum.finish_before,
        lambda moved: late_sum.add(moved) or after(moved, late_sum.sent),
    ]
    widths = [sums[:, k * model_width : (k + 1) * model_width] for k in range(4)]
    norm_parts = jnp.concatenate(
        [
            jnp.sum(part * factor, axis=0)
            for part, factor in zip(widths, (scale_attn, gate_attn, scale_ffn, gate_ffn))
        ]
    )
    grad_mod = jnp.concatenate(
        [
            widths[0] * attention_norm,
            widths[1] * attention_post * (1.0 - gate_attn * gate_attn),
            widths[2] * feedforward_norm,
            widths[3] * feedforward_post * (1.0 - gate_ffn * gate_ffn),
        ],
        axis=1,
    )
    mod_columns = ada_weight.shape[1]
    grad_mod_own = lax.dynamic_slice_in_dim(
        grad_mod, tensor_place * mod_columns, mod_columns, axis=1
    )
    dp_count = lax.axis_size("dp")
    ada_width = silu_time.shape[1]
    ada_rows = ada_width // dp_count
    small = jnp.concatenate(
        [
            norm_parts,
            jnp.sum(grad_mod_own, axis=0),
            stats[:3].reshape(-1),
            jnp.pad(grad_head_gate, (0, -local_heads % lanes)),
        ]
    )
    length = small.shape[0]
    gathered, small = gather_and_sum(
        between,
        jnp.concatenate([grad_mod_own, silu_time.astype(f32)], axis=1).reshape(-1, lanes),
        jnp.pad(small, (0, -length % 1024)).reshape(-1, lanes),
    )
    gathered = gathered.astype(bf16).reshape(dp_count * image_count, mod_columns + ada_width)
    small = small.reshape(-1)
    time_own = lax.dynamic_slice_in_dim(
        gathered, mod_columns + lax.axis_index("dp") * ada_rows, ada_rows, axis=1
    )
    ada_grad = dot_tn(time_own, gathered[:, :mod_columns])
    for running in (down_sum, gate_sum, up_sum, early_sum):
        running.finish(small)
    while late_sum.level < late_sum.levels - 1:
        late_sum.add()
    projections = totals()
    norm_sums = small[: 4 * model_width].reshape(4, model_width)
    bias_own = small[4 * model_width : 4 * model_width + mod_columns]
    start = 4 * model_width + mod_columns
    gain_sums = small[start : start + 3 * head_columns].reshape(3, local_heads, head_size)
    start = start + 3 * head_columns
    gate_own = small[start : start + local_heads]
    return (
        jnp.concatenate(layer_out, axis=0),
        jnp.concatenate(tokens_grad, axis=0),
        ada_grad,
        bias_own,
        norm_sums[0],
        norm_sums[1],
        norm_sums[2],
        norm_sums[3],
        *projections[:3],
        gain_sums[0],
        gain_sums[1],
        *projections[3:],
        gain_sums[2],
        gate_own,
        early_sum.columns(early_places[5], width_rows, pair_columns).T[:head_columns],
        gate_sum.columns(0, width_rows, hidden_columns),
        up_sum.columns(0, width_rows, hidden_columns),
        down_sum.columns(0, width_rows, hidden_columns).T,
    )


def solution(mesh):
    placed = (
        P(("dp", "tensor"), None),
        P("dp", None),
        P("dp", None, None),
        P("dp", None),
        P("dp"),
        P(None, "dp"),
        P(None, "tensor"),
        P("tensor"),
        P(),
        P(),
        P(),
        P(),
        P(None, "tensor"),
        P(None, "tensor"),
        P(None, "tensor"),
        P("tensor", None),
        P("tensor", None),
        P(None, "tensor"),
        P(None, "tensor"),
        P("tensor", None),
        P("tensor"),
        P("tensor", None),
        P(None, "tensor"),
        P(None, "tensor"),
        P("tensor", None),
        P(("dp", "tensor"), None),
    )
    return jax.shard_map(
        on_device,
        mesh=mesh,
        in_specs=placed,
        out_specs=(
            P(("dp", "tensor"), None),
            P(("dp", "tensor"), None),
            P("dp", "tensor"),
            P("tensor"),
            P(),
            P(),
            P(),
            P(),
            P("dp", "tensor"),
            P("dp", "tensor"),
            P("dp", "tensor"),
            P("tensor", None),
            P("tensor", None),
            P("dp", "tensor"),
            P("dp", "tensor"),
            P("tensor", None),
            P("tensor"),
            P("tensor", "dp"),
            P("dp", "tensor"),
            P("dp", "tensor"),
            P("tensor", "dp"),
        ),
        check_vma=False,
    )
```

```python
import math

import jax
import jax.numpy as jnp
from jax import lax
from jax.experimental import pallas as pl
from jax.experimental.pallas import tpu as pltpu
from jax.sharding import PartitionSpec as P

epsilon = 1e-05
penalty = 1024.0
theta = 10000.0
lanes = 128
half_lanes = 64
query_block = 384
bf16 = jnp.bfloat16
f32 = jnp.float32
vmem_bytes = 60 * 1024 * 1024


def sigmoid_of(values):
    return 1.0 / (1.0 + jnp.exp(-values))


def unit_rows(values):
    factor = lax.rsqrt(jnp.mean(values * values, axis=-1, keepdims=True) + epsilon)
    return (values * factor, factor)


def unit_back(gradient, normed, factor):
    return factor * (gradient - normed * jnp.mean(gradient * normed, axis=-1, keepdims=True))


def dot_nn(left, right):
    return lax.dot_general(left, right, (((1,), (0,)), ((), ())), preferred_element_type=f32)


def dot_nt(left, right):
    return lax.dot_general(left, right, (((1,), (1,)), ((), ())), preferred_element_type=f32)


def dot_tn(left, right):
    return lax.dot_general(left, right, (((0,), (0,)), ((), ())), preferred_element_type=f32)


def lane_index(rows):
    return lax.broadcasted_iota(jnp.int32, (rows, lanes), 1)


def halves_matrix(crossed):
    row = lax.broadcasted_iota(jnp.int32, (lanes, lanes), 0) // half_lanes
    col = lax.broadcasted_iota(jnp.int32, (lanes, lanes), 1) // half_lanes
    same = (row != col) if crossed else (row == col)
    return jnp.where(same, 1.0, 0.0).astype(bf16)


def half_sums(values, matrix):
    high = values.astype(bf16)
    rest = (values - high.astype(f32)).astype(bf16)
    return dot_nn(high, matrix) + dot_nn(rest, matrix)


def head_unit(values, matrix):
    factor = lax.rsqrt(half_sums(values * values, matrix) * (1.0 / half_lanes) + epsilon)
    return values * factor, factor


def head_unit_back(gradient, normed, factor, matrix):
    mean = half_sums(gradient * normed, matrix) * (1.0 / half_lanes)
    return factor * (gradient - normed * mean)


def swap_quarters(values):
    lane = lane_index(values.shape[0])
    ahead = pltpu.roll(values, lanes - 32, 1)
    behind = pltpu.roll(values, 32, 1)
    return jnp.where(lane % half_lanes < 32, ahead, behind)


def three_parts(values):
    first = values.astype(bf16)
    rest = values - first.astype(f32)
    second = rest.astype(bf16)
    third = (rest - second.astype(f32)).astype(bf16)
    return first, second, third


def put_lanes(target, place, head, values):
    lane = lane_index(target.shape[0])
    base = half_lanes * (1 - head) + place
    for offset, part in enumerate(three_parts(values)):
        target = jnp.where(lane == base + offset, part, target)
    return target


def both(head_zero, head_one):
    return jnp.where(lane_index(head_zero.shape[0]) < half_lanes, head_zero, head_one)


def pair_operands(values, features):
    return both(values, features), both(features, values)


def blocks_of(rows):
    starts = list(range(0, rows, query_block))
    return [(start, min(query_block, rows - start)) for start in starts]


def forward_kernel(block_count, image_count, present, *refs):
    q_refs = refs[:block_count]
    k_refs = refs[block_count : 2 * block_count]
    v_refs = refs[2 * block_count : 3 * block_count]
    (
        ck_ref,
        cv_ref,
        gain_ref,
        cos_ref,
        sin_ref,
        fq_ref,
        fk_ref,
        fc_ref,
        mixed_ref,
        so_ref,
        co_ref,
        qa_ref,
        ka_ref,
        ca_ref,
        va_ref,
        cva_ref,
        acc_ref,
    ) = refs[3 * block_count :]
    rows = cos_ref.shape[0]
    cap_rows = ck_ref.shape[0] // image_count
    same = halves_matrix(False)
    q_raw = jnp.concatenate([ref[...] for ref in q_refs], axis=0).astype(f32)
    k_raw = jnp.concatenate([ref[...] for ref in k_refs], axis=0).astype(f32)
    cosine = cos_ref[...]
    sine = sin_ref[...]
    q_gained = head_unit(q_raw, same)[0] * gain_ref[0, 0:1, :]
    q_turned = q_gained * cosine + swap_quarters(q_gained) * sine
    queries = (q_turned.astype(bf16).astype(f32) * (1.0 / math.sqrt(half_lanes))).astype(bf16)
    k_gained = head_unit(k_raw, same)[0] * gain_ref[0, 1:2, :]
    keys = (k_gained * cosine + swap_quarters(k_gained) * sine).astype(bf16)
    cap_keys = (head_unit(ck_ref[...].astype(f32), same)[0] * gain_ref[0, 2:3, :]).astype(bf16)
    values = jnp.concatenate([ref[...] for ref in v_refs], axis=0)
    cap_values = cv_ref[...]
    ones = jnp.ones_like(values)
    cap_ones = jnp.ones_like(cap_values)
    for head, (qa, ka, ca, va, cva) in enumerate(
        zip(
            pair_operands(queries, fq_ref[...]),
            pair_operands(keys, fk_ref[...]),
            pair_operands(cap_keys, fc_ref[...]),
            pair_operands(values, ones),
            pair_operands(cap_values, cap_ones),
        )
    ):
        span = slice(head * lanes, (head + 1) * lanes)
        qa_ref[:, span] = qa
        ka_ref[:, span] = ka
        ca_ref[:, span] = ca
        va_ref[:, span] = va
        cva_ref[:, span] = cva
    gate = gain_ref[0, 3:4, :]
    for index, (start, size) in enumerate(blocks_of(rows)):
        own = slice(start, start + size)
        self_parts = []
        for head in range(2):
            span = slice(head * lanes, (head + 1) * lanes)
            scores = dot_nt(qa_ref[own, span], ka_ref[:, span])
            self_parts.append(dot_nn(jnp.exp(scores).astype(bf16), va_ref[:, span]))
        first_image = pl.multiple_of(present[index * (image_count + 1) + image_count] * cap_rows, 16)
        for head in range(2):
            span = slice(head * lanes, (head + 1) * lanes)
            caps = pl.ds(first_image, cap_rows)
            scores = dot_nt(qa_ref[own, span], ca_ref[caps, span])
            acc_ref[0:size, span] = dot_nn(jnp.exp(scores).astype(bf16), cva_ref[caps, span])
        for image in range(image_count):

            @pl.when(present[index * (image_count + 1) + image] > 0)
            def _():
                caps = slice(image * cap_rows, (image + 1) * cap_rows)
                for head in range(2):
                    span = slice(head * lanes, (head + 1) * lanes)
                    scores = dot_nt(qa_ref[own, span], ca_ref[caps, span])
                    acc_ref[0:size, span] += dot_nn(
                        jnp.exp(scores).astype(bf16), cva_ref[caps, span]
                    )

        cross_parts = [acc_ref[0:size, 0:lanes], acc_ref[0:size, lanes:]]
        outs = []
        for parts in (self_parts, cross_parts):
            total = pltpu.roll(both(parts[1], parts[0]), half_lanes, 1)
            outs.append(both(parts[0], parts[1]) / total)
        so_ref[own, :] = outs[0].astype(bf16)
        co_ref[own, :] = outs[1].astype(bf16)
        mixed_ref[own, :] = (outs[0] + gate * outs[1]).astype(bf16)
        for head in range(2):
            span = slice(head * lanes, (head + 1) * lanes)
            qa = qa_ref[own, span]
            qa = put_lanes(qa, 3, head, -jnp.log(self_parts[head]))
            qa = put_lanes(qa, 6, head, -jnp.log(cross_parts[head]))
            qa_ref[own, span] = qa


def backward_kernel(block_count, image_count, present, *refs):
    q_refs = refs[:block_count]
    k_refs = refs[block_count : 2 * block_count]
    v_refs = refs[2 * block_count : 3 * block_count]
    (
        ck_ref,
        cv_ref,
        gain_ref,
        cos_ref,
        sin_ref,
        so_ref,
        co_ref,
        qa_ref,
        ka_ref,
        ca_ref,
        gm_ref,
        gq_ref,
        gk_ref,
        gv_ref,
        gck_ref,
        gcv_ref,
        stat_ref,
        ga_ref,
        va_ref,
        cva_ref,
        kt_ref,
        ct_ref,
        dq_ref,
        dk_ref,
        dv_ref,
        dck_ref,
        dcv_ref,
    ) = refs[3 * block_count :]
    rows = cos_ref.shape[0]
    cap_rows = ck_ref.shape[0] // image_count
    same = halves_matrix(False)
    crossed = halves_matrix(True)
    grads = gm_ref[...]
    grads_float = grads.astype(f32)
    cross_product = grads_float * co_ref[...].astype(f32)
    self_delta = half_sums(grads_float * so_ref[...].astype(f32), crossed)
    cross_delta = half_sums(cross_product, crossed)
    values = jnp.concatenate([ref[...] for ref in v_refs], axis=0)
    blank = jnp.zeros_like(grads)
    lane = lane_index(rows) % half_lanes
    self_ones = jnp.where(lane < 3, 1.0, 0.0).astype(bf16)
    lane_cap = lane_index(ck_ref.shape[0]) % half_lanes
    cross_ones = jnp.where((lane_cap >= 3) & (lane_cap < 6), 1.0, 0.0).astype(bf16)
    for head, (ga, va, cva) in enumerate(
        zip(
            pair_operands(grads, blank),
            pair_operands(values, self_ones),
            pair_operands(cv_ref[...], cross_ones),
        )
    ):
        span = slice(head * lanes, (head + 1) * lanes)
        ga = put_lanes(ga, 0, head, -self_delta)
        ga = put_lanes(ga, 3, head, -cross_delta)
        ga_ref[:, span] = ga
        va_ref[:, span] = va
        cva_ref[:, span] = cva
        kt_ref[span, :] = ka_ref[:, span].astype(f32).T.astype(bf16)
        ct_ref[span, :] = ca_ref[:, span].astype(f32).T.astype(bf16)
    dk_ref[...] = jnp.zeros_like(dk_ref)
    dv_ref[...] = jnp.zeros_like(dv_ref)
    dck_ref[...] = jnp.zeros_like(dck_ref)
    dcv_ref[...] = jnp.zeros_like(dcv_ref)
    for index, (start, size) in enumerate(blocks_of(rows)):
        own = slice(start, start + size)
        for head in range(2):
            span = slice(head * lanes, (head + 1) * lanes)
            top = head * half_lanes
            place = slice(head * lanes + top, head * lanes + top + half_lanes)
            qa = qa_ref[own, span]
            ga = ga_ref[own, span]
            probs = jnp.exp(dot_nt(ka_ref[:, span], qa))
            grad_scores = (probs * dot_nt(va_ref[:, span], ga)).astype(bf16)
            dv_ref[:, span] += dot_nn(probs.astype(bf16), ga)
            dk_ref[:, span] += dot_nn(grad_scores, qa)
            dq_ref[top : top + half_lanes, own] = dot_nn(kt_ref[place, :], grad_scores)
        def cross_part(caps):
            for head in range(2):
                span = slice(head * lanes, (head + 1) * lanes)
                top = head * half_lanes
                place = slice(head * lanes + top, head * lanes + top + half_lanes)
                gate = gain_ref[0, 3:4, top : top + 1]
                qa = qa_ref[own, span]
                ga = ga_ref[own, span]
                probs = jnp.exp(dot_nt(ca_ref[caps, span], qa))
                grad_scores = (probs * dot_nt(cva_ref[caps, span], ga)).astype(bf16)
                dcv_ref[caps, span] += dot_nn(probs.astype(bf16), ga)
                dck_ref[caps, span] += dot_nn(grad_scores, qa)
                dq_ref[top : top + half_lanes, own] += gate * dot_nn(
                    ct_ref[place, caps], grad_scores
                )

        base = index * (image_count + 1)
        for image in range(image_count):

            @pl.when((present[base + image] > 0) | (present[base + image_count] == image))
            def _():
                cross_part(slice(image * cap_rows, (image + 1) * cap_rows))

    cosine = cos_ref[...]
    sine = sin_ref[...]
    gate_row = gain_ref[0, 3:4, :]
    scale = 1.0 / math.sqrt(half_lanes)
    sums = []
    for refs_of, place, out_ref, grad in (
        (q_refs, 0, gq_ref, dq_ref[...].T * scale),
        (k_refs, 1, gk_ref, both(dk_ref[:, 0:lanes], dk_ref[:, lanes:])),
    ):
        raw = jnp.concatenate([ref[...] for ref in refs_of], axis=0).astype(f32)
        normed, factor = head_unit(raw, same)
        turned = grad * cosine - swap_quarters(grad) * sine
        sums.append(jnp.sum(turned * normed, axis=0, keepdims=True))
        gain = gain_ref[0, place : place + 1, :]
        out_ref[...] = head_unit_back(turned * gain, normed, factor, same).astype(bf16)
    gv_ref[...] = both(dv_ref[:, 0:lanes], dv_ref[:, lanes:]).astype(bf16)
    grad = both(dck_ref[:, 0:lanes], dck_ref[:, lanes:]) * gate_row
    normed, factor = head_unit(ck_ref[...].astype(f32), same)
    sums.append(jnp.sum(grad * normed, axis=0, keepdims=True))
    gck_ref[...] = head_unit_back(grad * gain_ref[0, 2:3, :], normed, factor, same).astype(bf16)
    gcv_ref[...] = (both(dcv_ref[:, 0:lanes], dcv_ref[:, lanes:]) * gate_row).astype(bf16)
    sums.append(jnp.sum(cross_product, axis=0, keepdims=True))
    stat_ref[0] = jnp.concatenate(sums + [jnp.zeros((4, lanes), f32)], axis=0)


def cost_of(seconds):
    return pl.CostEstimate(
        flops=int(1.0 * seconds * 1.1e15), bytes_accessed=int(1.0 * seconds * 3e12), transcendentals=0
    )


def columns_spec(rows, width):
    return pl.BlockSpec((rows, width), lambda pair, *_: (0, pair))


def whole_spec(rows):
    return pl.BlockSpec((rows, lanes), lambda pair, *_: (0, 0))


def gain_spec():
    return pl.BlockSpec((1, 8, lanes), lambda pair, *_: (pair, 0, 0))


def attention_forward(present, q_raw, k_raw, values, ck_raw, cap_values, gains, tables, images):
    cosine, sine, fq, fk, fc = tables
    count = len(q_raw)
    local = q_raw[0].shape[0]
    rows = local * count
    caps = ck_raw.shape[0]
    pairs = q_raw[0].shape[1] // lanes
    width = pairs * lanes
    grid = pltpu.PrefetchScalarGridSpec(
        num_scalar_prefetch=1,
        grid=(pairs,),
        in_specs=[columns_spec(local, lanes)] * (3 * count)
        + [columns_spec(caps, lanes)] * 2
        + [gain_spec()]
        + [whole_spec(rows)] * 4
        + [whole_spec(caps)],
        out_specs=[columns_spec(rows, lanes)] * 3
        + [columns_spec(rows, 2 * lanes)] * 2
        + [columns_spec(caps, 2 * lanes)],
        scratch_shapes=[
            pltpu.VMEM((rows, 2 * lanes), bf16),
            pltpu.VMEM((caps, 2 * lanes), bf16),
            pltpu.VMEM((query_block, 2 * lanes), f32),
        ],
    )
    return pl.pallas_call(
        lambda *refs: forward_kernel(count, images, *refs),
        grid_spec=grid,
        out_shape=[jax.ShapeDtypeStruct((rows, width), bf16)] * 3
        + [jax.ShapeDtypeStruct((rows, 2 * width), bf16)] * 2
        + [jax.ShapeDtypeStruct((caps, 2 * width), bf16)],
        compiler_params=pltpu.CompilerParams(vmem_limit_bytes=vmem_bytes),
        cost_estimate=cost_of(44e-6),
        name="attention_forward",
    )(present, *q_raw, *k_raw, *values, ck_raw, cap_values, gains, cosine, sine, fq, fk, fc)


def attention_backward(
    present,
    first,
    calls_pairs,
    earlier,
    q_raw,
    k_raw,
    values,
    ck_raw,
    cap_values,
    gains,
    tables,
    kept,
    grad_mixed,
    images,
    seconds,
):
    cosine, sine = tables[:2]
    self_out, cross_out, qa, ka, ca = kept
    count = len(q_raw)
    local = q_raw[0].shape[0]
    rows = local * count
    caps = ck_raw.shape[0]
    pairs = q_raw[0].shape[1] // lanes
    width = pairs * lanes

    def columns(rows, width):
        return pl.BlockSpec((rows, width), lambda pair, *_: (0, first + pair))

    own_gains = pl.BlockSpec((1, 8, lanes), lambda pair, *_: (first + pair, 0, 0))
    inputs = [
        *q_raw,
        *k_raw,
        *values,
        ck_raw,
        cap_values,
        gains,
        cosine,
        sine,
        self_out,
        cross_out,
        qa,
        ka,
        ca,
        grad_mixed,
    ]
    earlier = list(earlier or [])
    grid = pltpu.PrefetchScalarGridSpec(
        num_scalar_prefetch=1,
        grid=(calls_pairs,),
        in_specs=[columns(local, lanes)] * (3 * count)
        + [columns(caps, lanes)] * 2
        + [own_gains]
        + [whole_spec(rows)] * 2
        + [columns(rows, lanes)] * 2
        + [columns(rows, 2 * lanes)] * 2
        + [columns(caps, 2 * lanes)]
        + [columns(rows, lanes)]
        + [pl.BlockSpec(memory_space=pl.ANY)] * len(earlier),
        out_specs=[columns(rows, lanes)] * 3 + [columns(caps, lanes)] * 2 + [own_gains],
        scratch_shapes=[
            pltpu.VMEM((rows, 2 * lanes), bf16),
            pltpu.VMEM((rows, 2 * lanes), bf16),
            pltpu.VMEM((caps, 2 * lanes), bf16),
            pltpu.VMEM((2 * lanes, rows), bf16),
            pltpu.VMEM((2 * lanes, caps), bf16),
            pltpu.VMEM((lanes, rows), f32),
            pltpu.VMEM((rows, 2 * lanes), f32),
            pltpu.VMEM((rows, 2 * lanes), f32),
            pltpu.VMEM((caps, 2 * lanes), f32),
            pltpu.VMEM((caps, 2 * lanes), f32),
        ],
    )

    def kernel(present_ref, *refs):
        inside = len(inputs)
        backward_kernel(count, images, present_ref, *refs[:inside], *refs[inside + len(earlier) :])

    return pl.pallas_call(
        kernel,
        grid_spec=grid,
        out_shape=[jax.ShapeDtypeStruct((rows, width), bf16)] * 3
        + [jax.ShapeDtypeStruct((caps, width), bf16)] * 2
        + [jax.ShapeDtypeStruct((pairs, 8, lanes), f32)],
        input_output_aliases={1 + len(inputs) + k: k for k in range(len(earlier))},
        compiler_params=pltpu.CompilerParams(vmem_limit_bytes=vmem_bytes),
        cost_estimate=cost_of(seconds * calls_pairs),
        name="attention_backward",
    )(present, *inputs, *earlier)


def pick(table_ref, images):
    rows = table_ref[0:1, :]
    for image in range(1, table_ref.shape[0]):
        rows = jnp.where(images == image, table_ref[image : image + 1, :], rows)
    return rows


def unit_of(values):
    factor = lax.rsqrt(jnp.mean(values * values, axis=-1, keepdims=True) + epsilon)
    return values * factor, factor


def total_of(refs):
    total = refs[0][...].astype(f32)
    for ref in refs[1:]:
        total = total + ref[...].astype(f32)
    return total


def row_stage(body, rows_in, tables, images, rows_out, sum_count, name, seconds=3e-7):
    count, width = rows_in[0][0].shape
    image_count = tables[0].shape[0]
    tile = next(size for size in (96, 48, 16) if count % size == 0)
    flat = [array for group in rows_in for array in group]
    lengths = [len(group) for group in rows_in]

    def kernel(*refs):
        refs = list(refs)
        groups = []
        for length in lengths:
            groups.append(refs[:length])
            refs = refs[length:]
        table_refs, refs = refs[: len(tables)], refs[len(tables) :]
        images_ref, refs = refs[0], refs[1:]
        outs, sums = refs[: len(rows_out)], refs[len(rows_out) :]
        images_here = images_ref[...]
        if sum_count:

            @pl.when(pl.program_id(0) == 0)
            def _():
                for ref in sums:
                    ref[...] = jnp.zeros_like(ref)

        def add(index, values):
            for image in range(image_count):
                part = jnp.where(images_here == image, values, 0.0)
                sums[index][image : image + 1, :] += jnp.sum(part, axis=0, keepdims=True)

        body(groups, table_refs, images_here, outs, add)

    row_spec = pl.BlockSpec((tile, width), lambda i: (i, 0))
    return pl.pallas_call(
        kernel,
        grid=(count // tile,),
        in_specs=[row_spec] * len(flat)
        + [pl.BlockSpec(table.shape, lambda i: (0, 0)) for table in tables]
        + [pl.BlockSpec((tile, 1), lambda i: (i, 0))],
        out_specs=[row_spec] * len(rows_out)
        + [pl.BlockSpec((image_count, width), lambda i: (0, 0))] * sum_count,
        out_shape=[jax.ShapeDtypeStruct((count, width), kind) for kind in rows_out]
        + [jax.ShapeDtypeStruct((image_count, width), f32)] * sum_count,
        compiler_params=pltpu.CompilerParams(vmem_limit_bytes=vmem_bytes),
        cost_estimate=cost_of(seconds),
        name=name,
    )(*flat, *tables, images[:, None])


def normed_body(groups, tables, images, outs, add):
    (tokens,) = groups
    unit, _ = unit_of(total_of(tokens))
    outs[0][...] = (unit * pick(tables[0], images)).astype(bf16)


def hidden_body(groups, tables, images, outs, add):
    attn_parts, tokens = groups
    attn = total_of(attn_parts)
    unit, _ = unit_of(attn)
    hidden = total_of(tokens) + unit * pick(tables[0], images)
    outs[0][...] = attn
    outs[1][...] = hidden
    unit, _ = unit_of(hidden)
    outs[2][...] = (unit * pick(tables[1], images)).astype(bf16)


def output_body(groups, tables, images, outs, add):
    ffn_parts, hidden, cotangent = groups
    unit, factor = unit_of(total_of(ffn_parts))
    post = pick(tables[0], images)
    grad_out = total_of(cotangent)
    outs[0][...] = (total_of(hidden) + unit * post).astype(bf16)
    add(0, grad_out * unit)
    outs[1][...] = unit_back(grad_out * post, unit, factor).astype(bf16)


def middle_body(groups, tables, images, outs, add):
    grad_parts, hidden, attn, cotangent = groups
    grad_in = total_of(grad_parts)
    unit, factor = unit_of(total_of(hidden))
    add(0, grad_in * unit)
    grad_hidden = total_of(cotangent) + unit_back(
        grad_in * pick(tables[0], images), unit, factor
    )
    outs[0][...] = grad_hidden
    unit, factor = unit_of(total_of(attn))
    add(1, grad_hidden * unit)
    outs[1][...] = unit_back(grad_hidden * pick(tables[1], images), unit, factor).astype(bf16)


def input_body(groups, tables, images, outs, add):
    grad_parts, tokens, grad_hidden = groups
    grad_in = total_of(grad_parts)
    unit, factor = unit_of(total_of(tokens))
    add(0, grad_in * unit)
    outs[0][...] = total_of(grad_hidden) + unit_back(
        grad_in * pick(tables[0], images), unit, factor
    )


def weight_grad(bits, shards, lefts, rights, name, tile, height=None, offset=0, into=None):
    depth = lefts[0].shape[1]
    rows = sum(left.shape[0] for left in lefts)
    shard_rows = depth // shards
    spans = [right[1:] for right in rights]
    rights = [right[0] for right in rights]
    widths = [width for _, width in spans]
    starts = [sum(widths[:k]) // tile for k in range(len(widths) + 1)]
    ends = [len(lefts) + sum(len(pieces) for pieces in rights[:k]) for k in range(len(rights) + 1)]
    height = height or starts[-1] * shard_rows
    into = list(into or [])

    def kernel(bits_ref, *refs):
        left_refs = refs[: len(lefts)]
        kept_ref, sent_ref, turned_ref, total_ref = refs[ends[-1] + len(into) :]
        step = pl.program_id(0)
        bit = bits_ref[0]

        @pl.when(step == 0)
        def _():
            left = jnp.concatenate([ref[...] for ref in left_refs], axis=0)
            turned_ref[...] = left.astype(f32).T.astype(bf16)

        for index in range(len(rights)):

            @pl.when((step >= starts[index]) & (step < starts[index + 1]))
            def _():
                own = refs[ends[index] : ends[index + 1]]
                right = jnp.concatenate([ref[...] for ref in own], axis=0)
                total_ref[...] = dot_nn(turned_ref[...], right)

        for place in range(shards // 2):
            kept = pl.multiple_of((2 * place + bit) * shard_rows, 8)
            sent = pl.multiple_of((2 * place + 1 - bit) * shard_rows, 8)
            kept_ref[place] = total_ref[pl.ds(kept, shard_rows), :].astype(bf16)
            sent_ref[place] = total_ref[pl.ds(sent, shard_rows), :].astype(bf16)

    def right_spec(index, count):
        first, last = starts[index], starts[index + 1] - starts[index] - 1
        base = spans[index][0] // tile
        return pl.BlockSpec((count, tile), lambda j, s: (0, base + jnp.clip(j - first, 0, last)))

    out = jax.ShapeDtypeStruct((shards // 2, height, tile), bf16)
    above = offset // shard_rows
    out_spec = pl.BlockSpec((shards // 2, shard_rows, tile), lambda j, s: (0, above + j, 0))
    aliased = 1 + ends[-1]
    return pl.pallas_call(
        kernel,
        grid_spec=pltpu.PrefetchScalarGridSpec(
            num_scalar_prefetch=1,
            grid=(starts[-1],),
            in_specs=[pl.BlockSpec(left.shape, lambda j, s: (0, 0)) for left in lefts]
            + [
                right_spec(index, piece.shape[0])
                for index, pieces in enumerate(rights)
                for piece in pieces
            ]
            + [pl.BlockSpec(memory_space=pl.ANY)] * len(into),
            out_specs=[out_spec, out_spec],
            scratch_shapes=[pltpu.VMEM((depth, rows), bf16), pltpu.VMEM((depth, tile), f32)],
        ),
        out_shape=[out, out],
        input_output_aliases={aliased + k: k for k in range(len(into))},
        compiler_params=pltpu.CompilerParams(vmem_limit_bytes=vmem_bytes),
        cost_estimate=cost_of(5.2e-6 * starts[-1] * tile / 768),
        name=name,
    )(bits, *lefts, *[piece for pieces in rights for piece in pieces], *into)


def add_and_split(bits, level, kept, moved):
    shards, rows, width = kept.shape

    def kernel(bits_ref, kept_stay, moved_stay, kept_go, moved_go, stay_ref, go_ref):
        stay_ref[...] = (kept_stay[...].astype(f32) + moved_stay[...].astype(f32)).astype(bf16)
        go_ref[...] = (kept_go[...].astype(f32) + moved_go[...].astype(f32)).astype(bf16)

    stay = pl.BlockSpec((1, rows, width), lambda j, s: (2 * j + s[level], 0, 0))
    go = pl.BlockSpec((1, rows, width), lambda j, s: (2 * j + 1 - s[level], 0, 0))
    put = pl.BlockSpec((1, rows, width), lambda j, s: (j, 0, 0))
    out = jax.ShapeDtypeStruct((shards // 2, rows, width), bf16)
    return pl.pallas_call(
        kernel,
        grid_spec=pltpu.PrefetchScalarGridSpec(
            num_scalar_prefetch=1,
            grid=(shards // 2,),
            in_specs=[stay, stay, go, go],
            out_specs=[put, put],
        ),
        out_shape=[out, out],
        compiler_params=pltpu.CompilerParams(vmem_limit_bytes=vmem_bytes),
        cost_estimate=cost_of(1e-8),
        name="add_and_split",
    )(bits, kept, moved, kept, moved)


class DpSum:
    def __init__(self, bits, halves):
        self.bits = bits
        self.kept, self.sent = halves
        self.level = 0
        self.levels = len(bits_of("dp"))

    def send(self):
        self.moved = partner(self.sent, "dp", self.level)

    def add(self, *earlier):
        moved = after(self.moved, *earlier) if earlier else self.moved
        self.level += 1
        if self.level < self.levels:
            self.kept, self.sent = add_and_split(self.bits, self.level, self.kept, moved)
            self.send()
        else:
            self.total = self.kept[0].astype(f32) + moved[0].astype(f32)
            self.sent = self.total

    def finish(self, *earlier):
        while self.level < self.levels:
            self.add(*earlier)

    def finish_before(self, value):
        while self.level < self.levels - 1:
            self.add()
        value, moved = lax.optimization_barrier((value, self.moved))
        self.moved = moved
        self.level += 1
        self.total = self.kept[0].astype(f32) + moved[0].astype(f32)
        return value

    def columns(self, offset, shard_rows, width):
        tile = self.total.shape[1]
        parts = [
            self.total[offset + k * shard_rows : offset + (k + 1) * shard_rows]
            for k in range(width // tile)
        ]
        return jnp.concatenate(parts, axis=1)


def assembled(early, late, layout, shapes, name):
    tile = early[0].shape[2]

    def kernel(early_kept, early_moved, late_kept, late_moved, *outs):
        refs = ((early_kept, early_moved), (late_kept, late_moved))
        for out, tiles in zip(outs, layout):
            rows, width = out.shape
            for column, (which, row) in enumerate(tiles):
                left = column * tile
                size = min(tile, width - left)
                if size > 0:
                    kept, moved = refs[which]
                    place = slice(row, row + rows)
                    out[:, left : left + size] = (
                        kept[0, place, 0:size].astype(f32) + moved[0, place, 0:size].astype(f32)
                    )

    return pl.pallas_call(
        kernel,
        out_shape=[jax.ShapeDtypeStruct(shape, f32) for shape in shapes],
        compiler_params=pltpu.CompilerParams(vmem_limit_bytes=vmem_bytes),
        cost_estimate=cost_of(1e-6),
        name=name,
    )(*early, *late)


def tensor_moved(array, step):
    count = lax.axis_size("tensor")
    return lax.ppermute(array, "tensor", [((i + step) % count, i) for i in range(count)])


def gather_blocks(block):
    return [block] + [tensor_moved(block, step) for step in range(1, lax.axis_size("tensor"))]


def after(value, *earlier):
    return lax.optimization_barrier((value, earlier))[0]


def bits_of(axis):
    return range(lax.axis_size(axis).bit_length() - 1)


def partner(array, axis, bit):
    return lax.ppermute(array, axis, [(i, i ^ (1 << bit)) for i in range(lax.axis_size(axis))])


def gather_and_sum(between, own, part):
    for bit in reversed(bits_of("dp")):
        moved = partner(jnp.concatenate([own, part], axis=0), "dp", bit)
        step = between.pop(0) if between else None
        if step:
            moved = step(moved)
        own = jnp.concatenate([own, moved[: own.shape[0]]], axis=0)
        part = part + moved[moved.shape[0] - part.shape[0] :]
    return own, part


def sum_over(array, axis):
    for bit in reversed(bits_of(axis)):
        array = array + partner(array, axis, bit)
    return array


def rope_tables(positions):
    lane = jnp.arange(lanes, dtype=jnp.int32)
    place = lane % 32
    freqs = jnp.power(theta, -((place % 16).astype(f32) / 16))
    spot = jnp.where(place[None, :] < 16, positions[0][:, None], positions[1][:, None])
    angles = spot.astype(f32) * freqs[None, :]
    sign = jnp.where(lane % half_lanes < 32, -1.0, 1.0)
    return (jnp.cos(angles), jnp.sin(angles) * sign[None, :])


def feature_lanes(images, valid, count, ones_at):
    lane = (jnp.arange(lanes, dtype=jnp.int32) % half_lanes)[None, :]
    outside = (lane < count) & ((lane != images[:, None]) | ~valid[:, None])
    ones = (lane >= ones_at) & (lane < ones_at + 3)
    return jnp.where(outside, -penalty, jnp.where(ones, 1.0, 0.0)).astype(bf16)


def pad_columns(values, width):
    return jnp.pad(values, ((0, 0), (0, width - values.shape[1])))


def pad_rows(values, height):
    return jnp.pad(values, ((0, height - values.shape[0]), (0, 0)))


def on_device(
    tokens,
    timestep,
    caption,
    caption_mask,
    image_lengths,
    patch_pos,
    ada_weight,
    ada_bias,
    attention_norm,
    attention_post,
    feedforward_norm,
    feedforward_post,
    query_weight,
    key_weight,
    value_weight,
    query_gain,
    key_gain,
    cross_keys,
    cross_values,
    cross_gain,
    cross_gate,
    output_weight,
    gate_weight,
    up_weight,
    down_weight,
    cotangent,
):
    local_rows, model_width = tokens.shape
    tensor_count = lax.axis_size("tensor")
    tensor_place = lax.axis_index("tensor")
    group_tokens = local_rows * tensor_count
    image_count, cap_len, cap_width = caption.shape
    local_heads, head_size = query_gain.shape
    head_columns = local_heads * head_size
    pairs = (local_heads + 1) // 2
    pair_columns = pairs * lanes
    cap_total = image_count * cap_len

    token_blocks = gather_blocks(tokens)

    places = (
        jnp.arange(group_tokens, dtype=jnp.int32) + tensor_place * local_rows
    ) % group_tokens
    image_all = jnp.zeros((group_tokens,), jnp.int32)
    end = jnp.zeros((), jnp.int32)
    for image in range(image_count - 1):
        end = end + image_lengths[image]
        image_all = image_all + (places >= end).astype(jnp.int32)
    image_own = image_all[:local_rows]
    positions = jnp.roll(patch_pos, -tensor_place * local_rows, axis=1)
    cosine, sine = rope_tables(positions)
    lane = (jnp.arange(lanes, dtype=jnp.int32) % half_lanes)[None, :]
    query_features = (lane == image_all[:, None]).astype(bf16)
    everywhere = jnp.ones((group_tokens,), jnp.bool_)
    key_features = feature_lanes(image_all, everywhere, image_count, 3)
    cap_features = feature_lanes(
        jnp.arange(cap_total, dtype=jnp.int32) // cap_len,
        caption_mask.reshape(-1) > 0,
        image_count,
        6,
    )
    block_total = -(-group_tokens // query_block)
    block_place = jnp.arange(group_tokens, dtype=jnp.int32) // query_block
    hit = (block_place[None, None, :] == jnp.arange(block_total)[:, None, None]) & (
        image_all[None, None, :] == jnp.arange(image_count)[None, :, None]
    )
    hit = jnp.max(hit.astype(jnp.int32), axis=2)
    first_image = jnp.argmax(hit, axis=1).astype(jnp.int32)[:, None]
    beyond = jnp.where(jnp.arange(image_count)[None, :] == first_image, 0, hit)
    present = jnp.concatenate([beyond, first_image], axis=1).reshape(-1)
    head_gate = jnp.tanh(cross_gate)
    gain_rows = jnp.stack(
        [
            query_gain.reshape(-1),
            key_gain.reshape(-1),
            cross_gain.reshape(-1),
            jnp.repeat(head_gate, head_size),
        ]
    )
    gains = (
        jnp.pad(gain_rows, ((0, 4), (0, pair_columns - head_columns)))
        .reshape(8, pairs, lanes)
        .transpose(1, 0, 2)
    )
    tables = (cosine, sine, query_features, key_features, cap_features)

    time_float = timestep.astype(f32)
    silu_time = (time_float * sigmoid_of(time_float)).astype(bf16)
    mod_part = dot_nn(silu_time, ada_weight) + ada_bias
    mod_stack = jnp.roll(jnp.stack(gather_blocks(mod_part)), tensor_place, axis=0)
    modulation = mod_stack.transpose(1, 0, 2).reshape(image_count, 4 * model_width)
    scale_attn = 1.0 + modulation[:, :model_width]
    gate_attn = jnp.tanh(modulation[:, model_width : 2 * model_width])
    scale_ffn = 1.0 + modulation[:, 2 * model_width : 3 * model_width]
    gate_ffn = jnp.tanh(modulation[:, 3 * model_width :])
    norm_attn = scale_attn * attention_norm
    post_attn = gate_attn * attention_post
    norm_ffn = scale_ffn * feedforward_norm
    post_ffn = gate_ffn * feedforward_post

    cap_flat = caption.reshape(cap_total, cap_width)
    ck_raw = pad_columns(dot_nn(cap_flat, cross_keys), pair_columns)
    cap_values = pad_columns(dot_nn(cap_flat, cross_values).astype(bf16), pair_columns)

    normed, q_raw, k_raw, values = [], [], [], []
    for index, block in enumerate(token_blocks):
        images = image_all[index * local_rows : (index + 1) * local_rows]
        (rows,) = row_stage(normed_body, [[block]], [norm_attn], images, [bf16], 0, "normed_in")
        normed.append(rows)
        q_raw.append(pad_columns(dot_nn(rows, query_weight), pair_columns))
        k_raw.append(pad_columns(dot_nn(rows, key_weight), pair_columns))
        values.append(pad_columns(dot_nn(rows, value_weight).astype(bf16), pair_columns))

    mixed, *kept = attention_forward(
        present, q_raw, k_raw, values, ck_raw, cap_values, gains, tables, image_count
    )
    chunks = 2 if local_rows % 32 == 0 else 1
    chunk_rows = local_rows // chunks
    steps = range(1, tensor_count)
    cuts = range(chunks)
    bits = jnp.stack([(lax.axis_index("dp") >> bit) & 1 for bit in bits_of("dp")]).astype(jnp.int32)
    shards = lax.axis_size("dp")
    hidden_columns = gate_weight.shape[1]
    wide_tile = 256 if hidden_columns % 256 == 0 else lanes

    def piece_of(array, step, cut):
        start = step * local_rows + cut * chunk_rows
        return array[start : start + chunk_rows]

    def returned(parts):
        return [tensor_moved(part, -step) for step, part in enumerate(parts, 1)]

    def moved_in(array):
        return [tensor_moved(array, step) for step in steps]

    output_rows = pad_rows(output_weight, pair_columns)
    output_rows = [output_rows] + [tensor_moved(output_rows, -step) for step in steps]
    tokens_cut = [piece_of(tokens, 0, cut) for cut in cuts]
    cotangent_cut = [piece_of(cotangent, 0, cut) for cut in cuts]
    images_cut = [piece_of(image_own, 0, cut) for cut in cuts]

    mixed_own = [
        [piece_of(mixed, 0, cut)] + returned([piece_of(mixed, step, cut) for step in steps])
        for cut in cuts
    ]
    attn, hidden, ffn_in = [], [], []
    for cut in cuts:
        attn_rows, hidden_rows, rows = row_stage(
            hidden_body,
            [
                [sum(dot_nn(part, rows) for part, rows in zip(mixed_own[cut], output_rows))],
                [tokens_cut[cut]],
            ],
            [post_attn, norm_ffn],
            images_cut[cut],
            [f32, f32, bf16],
            0,
            "hidden",
        )
        attn.append(attn_rows)
        hidden.append(hidden_rows)
        ffn_in.append([rows] + moved_in(rows))

    def feed_forward(rows):
        gate = dot_nn(rows, gate_weight)
        up = dot_nn(rows, up_weight)
        inner = (gate * sigmoid_of(gate) * up).astype(bf16)
        return gate.astype(bf16), up.astype(bf16), inner, dot_nn(inner, down_weight)

    latest = ()
    forward, ffn_moved = [], []
    for cut in cuts:
        pieces = []
        for step in range(tensor_count):
            ffn_in[cut][step] = after(ffn_in[cut][step], *latest)
            gate, up, inner, part = feed_forward(ffn_in[cut][step])
            part = part if step == 0 else part.astype(bf16)
            pieces.append((gate, up, inner, part))
            latest = (part,)
        forward.append(pieces)
        ffn_moved.append(returned([piece[3] for piece in pieces[1:]]))

    layer_out, sums_ffn_post, grad_ffn = [], [], []
    for cut in cuts:
        out_rows, rows, sums = row_stage(
            output_body,
            [[forward[cut][0][3]] + ffn_moved[cut], [hidden[cut]], [cotangent_cut[cut]]],
            [post_ffn],
            images_cut[cut],
            [bf16, bf16],
            1,
            "layer_out",
        )
        layer_out.append(out_rows)
        sums_ffn_post.append(sums)
        grad_ffn.append([rows] + moved_in(rows))

    def feed_back(rows, kept):
        gate, up = kept[0].astype(f32), kept[1].astype(f32)
        grad_inner = dot_nt(rows, down_weight)
        sig = sigmoid_of(gate)
        grad_up = (grad_inner * (gate * sig)).astype(bf16)
        grad_gate = (grad_inner * up * sig * (1.0 + gate * (1.0 - sig))).astype(bf16)
        return grad_gate, grad_up, dot_nt(grad_gate, gate_weight) + dot_nt(grad_up, up_weight)

    latest = ()
    backward, grad_in_moved = [], []
    for cut in cuts:
        pieces = []
        for step in range(tensor_count):
            grad_ffn[cut][step] = after(grad_ffn[cut][step], *latest)
            grad_gate, grad_up, part = feed_back(grad_ffn[cut][step], forward[cut][step])
            part = part if step == 0 else part.astype(bf16)
            pieces.append((grad_gate, grad_up, part))
            latest = (part,)
        backward.append(pieces)
        grad_in_moved.append(returned([piece[2] for piece in pieces[1:]]))

    def whole_right(pieces):
        return pieces, 0, pieces[0].shape[1]

    def group_pieces(of):
        return [of(cut, step) for step in range(tensor_count) for cut in cuts]

    grad_hidden, sums_ffn_norm, sums_attn_post, grad_attn = [], [], [], []
    grad_mixed_own, grad_mixed_moved = [], []
    for cut in cuts:
        if cut == chunks - 1:
            lefts = group_pieces(lambda cut, step: grad_ffn[cut][step])
            lefts[0] = after(
                lefts[0], latest, grad_mixed_own, [piece[2] for piece in backward[cut]]
            )
            down_sum = DpSum(
                bits,
                weight_grad(
                    bits,
                    shards,
                    lefts,
                    [whole_right(group_pieces(lambda cut, step: forward[cut][step][2]))],
                    "down_grad",
                    wide_tile,
                ),
            )
            down_sum.send()
            grad_in_moved[cut] = [after(moved, down_sum.sent) for moved in grad_in_moved[cut]]
        hidden_grad, rows, norm_sums, post_sums = row_stage(
            middle_body,
            [
                [backward[cut][0][2]] + grad_in_moved[cut],
                [hidden[cut]],
                [attn[cut]],
                [cotangent_cut[cut]],
            ],
            [norm_ffn, post_attn],
            images_cut[cut],
            [f32, bf16],
            2,
            "hidden_grad",
        )
        grad_hidden.append(hidden_grad)
        sums_ffn_norm.append(norm_sums)
        sums_attn_post.append(post_sums)
        grad_attn.append(rows)
        grad_mixed_own.append([dot_nt(rows, weight).astype(bf16) for weight in output_rows])
        grad_mixed_moved.append(
            [tensor_moved(part, step) for step, part in enumerate(grad_mixed_own[cut][1:], 1)]
        )
        latest = (rows, grad_mixed_own[cut])
    lefts = group_pieces(lambda cut, step: ffn_in[cut][step])

    def hidden_sum(index, *earlier):
        rights = [whole_right(group_pieces(lambda cut, step: backward[cut][step][index]))]
        own = [after(lefts[0], *earlier)] + lefts[1:]
        return DpSum(bits, weight_grad(bits, shards, own, rights, "gate_up_grad", wide_tile))

    gate_sum = hidden_sum(0, latest)
    gate_sum.send()
    up_sum = hidden_sum(1, gate_sum.sent, grad_mixed_moved)
    up_sum.send()
    down_sum.add(up_sum.sent)
    grad_mixed = jnp.concatenate(
        [grad_mixed_own[cut][0] for cut in cuts]
        + [grad_mixed_moved[cut][step - 1] for step in steps for cut in cuts],
        axis=0,
    )
    grad_mixed = after(grad_mixed, down_sum.sent)
    grad_attn = [
        [rows] + moved_in(after(rows, *[m for moved in grad_mixed_moved for m in moved]))
        for rows in grad_attn
    ]
    grad_attn = group_pieces(lambda cut, step: grad_attn[cut][step])

    width_rows, cap_rows = model_width // shards, cap_width // shards

    def side_by_side(parts, start, width, with_output, earlier, between=None):
        tile = 256 if start % 256 == 0 and width % 256 == 0 else lanes
        tiles = width // tile
        ahead = 2 * tiles * cap_rows
        projection_at = -(-ahead // width_rows) * width_rows
        output_at = projection_at + 3 * tiles * width_rows
        height = output_at + (pair_columns // tile * width_rows if with_output else 0)
        lefts = [after(normed[0], *earlier)] + list(normed[1:])
        halves = weight_grad(
            bits,
            shards,
            lefts,
            [([part], start, width) for part in parts[:3]],
            "projection_grad",
            tile,
            height,
            projection_at,
        )
        halves = weight_grad(
            bits,
            shards,
            [cap_flat],
            [([part], start, width) for part in parts[3:5]],
            "caption_grad",
            tile,
            height,
            0,
            halves,
        )
        if with_output:
            own = [after(grad_attn[0], between(halves))] + grad_attn[1:]
            halves = weight_grad(
                bits,
                shards,
                own,
                [whole_right([mixed])],
                "output_grad",
                tile,
                height,
                output_at,
                halves,
            )
        places = [projection_at + k * tiles * width_rows for k in range(3)]
        places += [k * tiles * cap_rows for k in range(2)] + [output_at]
        return DpSum(bits, halves), places

    parts = None
    first = 0
    call_sizes = [2] * (pairs // 2) if pairs % 2 == 0 and pairs > 2 else [1] * pairs
    for call, size in enumerate(call_sizes):
        parts = attention_backward(
            present,
            first,
            size,
            parts,
            q_raw,
            k_raw,
            values,
            ck_raw,
            cap_values,
            gains,
            tables,
            kept,
            grad_mixed,
            image_count,
            15e-6 if call == len(call_sizes) - 1 else 3e-6,
        )
        first += size
        if call == 0:
            gate_sum.add(parts[0])
            down_sum.add(gate_sum.sent)
            up_sum.add(down_sum.sent)
            grad_mixed = after(grad_mixed, up_sum.sent)
        if call == len(call_sizes) - 2:
            early = first * lanes
            gate_sum.add(parts[0])
            down_sum.add(gate_sum.sent)
            early_sum, early_places = side_by_side(
                parts,
                0,
                early,
                True,
                (down_sum.sent,),
                lambda halves: gate_sum.add(halves) or up_sum.add(gate_sum.sent) or up_sum.sent,
            )
            early_sum.send()
            early_sum.add()
            parts = [parts[0]] + list(after(tuple(parts[1:]), early_sum.sent))
            grad_mixed = after(grad_mixed, early_sum.sent)
    parts = gate_sum.finish_before(down_sum.finish_before(tuple(parts)))
    up_sum.add(parts[0])
    parts = after(parts, up_sum.sent)
    grad_q, grad_k, grad_v, grad_ck, grad_cv, stats = parts
    stats = stats.transpose(1, 0, 2).reshape(8, pair_columns)[:, :head_columns]
    stats = stats.reshape(8, local_heads, head_size)
    grad_head_gate = jnp.sum(stats[3], axis=1) * (1.0 - head_gate * head_gate)

    weights_in = [
        pad_columns(weight, pair_columns) for weight in (query_weight, key_weight, value_weight)
    ]

    def input_part(step, cut):
        return sum(
            dot_nt(piece_of(part, step, cut), weight)
            for part, weight in zip((grad_q, grad_k, grad_v), weights_in)
        )

    sent = [[input_part(step, cut).astype(bf16) for step in steps] for cut in cuts]
    grad_normed_moved = [returned(part) for part in sent]
    late = pair_columns - early
    late_sum, late_places = side_by_side(
        [grad_q, grad_k, grad_v, grad_ck, grad_cv], early, late, False, (sent,)
    )
    late_sum.send()
    up_sum.finish(late_sum.sent)
    early_sum.add(late_sum.sent, up_sum.sent)
    grad_q = after(grad_q, early_sum.sent)
    grad_normed_kept = [input_part(0, cut) for cut in cuts]
    late_sum.add(grad_normed_kept)
    grad_normed_moved = [
        [after(moved, late_sum.sent) for moved in part] for part in grad_normed_moved
    ]
    sums_attn_norm, tokens_grad = [], []
    for cut in cuts:
        if cut == chunks - 1 and cut > 0:
            early_sum.add(tokens_grad)
            grad_normed_moved[cut] = [
                after(moved, early_sum.sent) for moved in grad_normed_moved[cut]
            ]
        rows, sums = row_stage(
            input_body,
            [[grad_normed_kept[cut]] + grad_normed_moved[cut], [tokens_cut[cut]], [grad_hidden[cut]]],
            [norm_attn],
            images_cut[cut],
            [f32],
            1,
            "tokens_grad",
            12e-6,
        )
        tokens_grad.append(rows)
        sums_attn_norm.append(sums)
    def totals():
        tile = early_sum.kept.shape[2]
        layout = [
            [(0, early_places[k] + c * rows) for c in range(early // tile)]
            + [(1, late_places[k] + c * rows) for c in range(late // tile)]
            for k, rows in enumerate([width_rows] * 3 + [cap_rows] * 2)
        ]
        return assembled(
            (early_sum.kept, early_sum.moved),
            (late_sum.kept, late_sum.moved),
            layout,
            [(width_rows, head_columns)] * 3 + [(cap_rows, head_columns)] * 2,
            "assembled",
        )

    sums = jnp.concatenate(
        [sum(part) for part in (sums_attn_norm, sums_attn_post, sums_ffn_norm, sums_ffn_post)],
        axis=1,
    )
    late_sum.add(tokens_grad)
    sums = early_sum.finish_before(sum_over(after(sums, late_sum.sent), "tensor"))
    between = [
        None,
        lambda moved: late_sum.add(moved) or after(moved, late_sum.sent),
    ]
    widths = [sums[:, k * model_width : (k + 1) * model_width] for k in range(4)]
    norm_parts = jnp.concatenate(
        [
            jnp.sum(part * factor, axis=0)
            for part, factor in zip(widths, (scale_attn, gate_attn, scale_ffn, gate_ffn))
        ]
    )
    grad_mod = jnp.concatenate(
        [
            widths[0] * attention_norm,
            widths[1] * attention_post * (1.0 - gate_attn * gate_attn),
            widths[2] * feedforward_norm,
            widths[3] * feedforward_post * (1.0 - gate_ffn * gate_ffn),
        ],
        axis=1,
    )
    mod_columns = ada_weight.shape[1]
    grad_mod_own = lax.dynamic_slice_in_dim(
        grad_mod, tensor_place * mod_columns, mod_columns, axis=1
    )
    dp_count = lax.axis_size("dp")
    ada_width = silu_time.shape[1]
    ada_rows = ada_width // dp_count
    small = jnp.concatenate(
        [
            norm_parts,
            jnp.sum(grad_mod_own, axis=0),
            stats[:3].reshape(-1),
            jnp.pad(grad_head_gate, (0, -local_heads % lanes)),
        ]
    )
    length = small.shape[0]
    gathered, small = gather_and_sum(
        between,
        jnp.concatenate([grad_mod_own, silu_time.astype(f32)], axis=1).reshape(-1, lanes),
        jnp.pad(small, (0, -length % 1024)).reshape(-1, lanes),
    )
    gathered = gathered.astype(bf16).reshape(dp_count * image_count, mod_columns + ada_width)
    small = small.reshape(-1)
    time_own = lax.dynamic_slice_in_dim(
        gathered, mod_columns + lax.axis_index("dp") * ada_rows, ada_rows, axis=1
    )
    ada_grad = dot_tn(time_own, gathered[:, :mod_columns])
    for running in (down_sum, gate_sum, up_sum, early_sum):
        running.finish(small)
    while late_sum.level < late_sum.levels - 1:
        late_sum.add()
    projections = totals()
    norm_sums = small[: 4 * model_width].reshape(4, model_width)
    bias_own = small[4 * model_width : 4 * model_width + mod_columns]
    start = 4 * model_width + mod_columns
    gain_sums = small[start : start + 3 * head_columns].reshape(3, local_heads, head_size)
    start = start + 3 * head_columns
    gate_own = small[start : start + local_heads]
    return (
        jnp.concatenate(layer_out, axis=0),
        jnp.concatenate(tokens_grad, axis=0),
        ada_grad,
        bias_own,
        norm_sums[0],
        norm_sums[1],
        norm_sums[2],
        norm_sums[3],
        *projections[:3],
        gain_sums[0],
        gain_sums[1],
        *projections[3:],
        gain_sums[2],
        gate_own,
        early_sum.columns(early_places[5], width_rows, pair_columns).T[:head_columns],
        gate_sum.columns(0, width_rows, hidden_columns),
        up_sum.columns(0, width_rows, hidden_columns),
        down_sum.columns(0, width_rows, hidden_columns).T,
    )


def solution(mesh):
    placed = (
        P(("dp", "tensor"), None),
        P("dp", None),
        P("dp", None, None),
        P("dp", None),
        P("dp"),
        P(None, "dp"),
        P(None, "tensor"),
        P("tensor"),
        P(),
        P(),
        P(),
        P(),
        P(None, "tensor"),
        P(None, "tensor"),
        P(None, "tensor"),
        P("tensor", None),
        P("tensor", None),
        P(None, "tensor"),
        P(None, "tensor"),
        P("tensor", None),
        P("tensor"),
        P("tensor", None),
        P(None, "tensor"),
        P(None, "tensor"),
        P("tensor", None),
        P(("dp", "tensor"), None),
    )
    return jax.shard_map(
        on_device,
        mesh=mesh,
        in_specs=placed,
        out_specs=(
            P(("dp", "tensor"), None),
            P(("dp", "tensor"), None),
            P("dp", "tensor"),
            P("tensor"),
            P(),
            P(),
            P(),
            P(),
            P("dp", "tensor"),
            P("dp", "tensor"),
            P("dp", "tensor"),
            P("tensor", None),
            P("tensor", None),
            P("dp", "tensor"),
            P("dp", "tensor"),
            P("tensor", None),
            P("tensor"),
            P("tensor", "dp"),
            P("dp", "tensor"),
            P("dp", "tensor"),
            P("tensor", "dp"),
        ),
        check_vma=False,
    )
```
